128 devices in a mesh: dp: 8 (over x, core), tensor: 16 (over z, y).
Axes of the slice: x: 4, y: 4, z: 4, core: 2. Of those that a mesh axis runs over, the one named last changes fastest.
Arguments:
- tokens: bfloat16 [16384, 8192], P(('dp', 'tensor')), parts along dimension 0, may hold values from -6 to 6
- route_order: int32 [128, 128], P(('dp', 'tensor')), parts along dimension 0, may hold values from 0 to 127, each once within a row
- route_counts: int32 [128], P(('dp', 'tensor')), parts along dimension 0, may hold values from 1 to 64, 256 in all
- w_router: bfloat16 [8192], replicated, may hold values from -0.125 to 0.125
- gain_in: float32 [8192], replicated, may hold values from 0.1 to 1.9
- w_gate_up: bfloat16 [8192, 4096], P(None, 'tensor'), may hold values from -0.0625 to 0.0625
- w_down: bfloat16 [2048, 8192], P('tensor'), may hold values from -0.125 to 0.125
- gain_next: float32 [8192], replicated, may hold values from 0.1 to 1.9
- w_query: bfloat16 [8192, 2048], P(None, 'tensor'), may hold values from -0.0625 to 0.0625
Outputs:
- mixed: bfloat16 [16384, 8192], P(('dp', 'tensor')), parts along dimension 0
- query: bfloat16 [16384, 2048], P('dp', 'tensor'), parts along dimension 0
The draws below stay inside these ranges and needn't reach their ends.
There are 8 independent parts, one for each index of `dp`. The reference program is written for one: setup_inputs(seed, part) draws one part's arguments, and reference() takes and returns one part's arrays. A program takes and returns all parts, laid end to end along the dimension named above; an argument that names none is the same for every part. Nothing has to cross between parts.
Inputs may be any that keep to these rules, and one draw needn't show every extreme that they name: Each row of route_order is a permutation of the owner's local rows 0 to 127. `route_counts`: the counts of one sequence sum to 256; the largest is exactly 64.
All inputs are finite; a program needn't handle non-finite values. No bound on the sum of `route_counts` on one device may be relied on, other than what follows from the above.
Results may differ from the reference program's by a relative error of at most 0.0065.
Values may be sent and summed in bfloat16 or wider, within the bound.
A program may use at most 192 MiB of HBM per device.

```python
import math
import jax
import jax.numpy as jnp
import numpy as np
from jax import lax

D = 8192
HEAD_DIM = 128
FF_DEV = 128
ROWS_DEV = 128
SLOTS = 64
SEQ = 2048
ROUTED = 256
FFW = 2048
N_TENSOR = 16


def block_scale(key, extent, pieces, least, high):
    level, own = 1.0, jax.random.fold_in(key, 6)
    for axis_at, shards_of in pieces:
        heights = jnp.exp(jax.random.uniform(jax.random.fold_in(own, axis_at), (shards_of,), jnp.float32, least / len(pieces), high / len(pieces)))
        level = level * jnp.repeat(heights, extent[axis_at] // shards_of).reshape([-1 if axis == axis_at else 1 for axis in range(len(extent))])
    return level


def length_profile(number_of, total, bound, skew):
    loads = [(1 << 20) // math.isqrt(rank ** skew) + 1 for rank in range(2, number_of + 1)]
    spare, given = total - bound - (number_of - 1), [1] * (number_of - 1)
    while spare > 0:
        free = [i for i in range(number_of - 1) if given[i] < bound]
        whole, remaining = sum([loads[i] for i in free]), spare
        for i in free:
            more = min(bound - given[i], max(1, remaining * loads[i] // whole), spare)
            given[i] = given[i] + more
            spare = spare - more
    return np.array([bound] + given)


def ragged_sizes(stream_key, number_of, total, reach, skew):
    if number_of == 2:
        one = jax.random.randint(stream_key, (), max(1, total - reach), min(reach, total - 1) + 1)
        return jnp.stack([one, total - one])
    sizes = jnp.asarray(length_profile(number_of, total, reach, skew), jnp.int32)
    pairs = (number_of - 1) // 2
    donor, taker = sizes[1:1 + 2 * pairs:2], sizes[2:2 + 2 * pairs:2]
    room = jnp.minimum(donor - 1, reach - taker)
    passed = jax.random.randint(jax.random.fold_in(stream_key, 1), (pairs,), 0, 1 << 20) % (room + 1)
    sizes = sizes.at[1:1 + 2 * pairs:2].set(donor - passed).at[2:2 + 2 * pairs:2].set(taker + passed)
    return sizes[jax.random.permutation(jax.random.fold_in(stream_key, 2), number_of)]


def bell_draw(own_key, extent, deviation, reach, shards=(), held_as=jnp.bfloat16):
    entries = jax.random.normal(own_key, extent, jnp.float32) * deviation
    if len(shards) > 0:
        entries = block_scale(own_key, extent, shards, -0.22, 0.18) * entries
    return jnp.clip(entries, min=-reach, max=reach).astype(held_as)


def setup_inputs(seed: int = 0, part: int = 0) -> dict:
    streams_of = jax.random.split(jax.random.key(seed), 10)
    own_keys = jax.random.split(jax.random.fold_in(streams_of[9], part), 10)
    tokens = bell_draw(own_keys[0], (SEQ, D), 1.0, 6.0, ((0, 16),))
    route_order = jax.vmap(lambda own: jax.random.permutation(own, ROWS_DEV))(jax.random.split(own_keys[1], N_TENSOR)).reshape((N_TENSOR, ROWS_DEV)).astype(jnp.int32)
    route_counts = ragged_sizes(own_keys[2], N_TENSOR, ROUTED, SLOTS, 2).astype(jnp.int32)
    w_router = bell_draw(streams_of[3], (D,), (D // 4) ** -0.5, 0.125)
    gain_in = jnp.clip(1.0 + 0.18 * jax.random.normal(streams_of[4], (D,), jnp.float32), 0.1, 1.9)
    w_gate_up = bell_draw(streams_of[5], (D, 2 * FFW), D ** -0.5, 0.0625, ((1, 16),))
    w_down = bell_draw(streams_of[6], (FFW, D), FFW ** -0.5, 0.125, ((0, 16),))
    gain_next = jnp.clip(1.0 + 0.18 * jax.random.normal(streams_of[7], (D,), jnp.float32), 0.1, 1.9)
    w_query = bell_draw(streams_of[8], (D, N_TENSOR * HEAD_DIM), D ** -0.5, 0.0625, ((1, 16),))
    return dict(tokens=tokens, route_order=route_order, route_counts=route_counts, w_router=w_router, gain_in=gain_in, w_gate_up=w_gate_up, w_down=w_down, gain_next=gain_next, w_query=w_query)


def rms_scale(values, gain):
    return values * lax.rsqrt(lax.optimization_barrier(jnp.mean(values * values, axis=-1, keepdims=True)) + 1e-05) * gain

def reference(tokens, route_order, route_counts, w_router, gain_in, w_gate_up, w_down, gain_next, w_query):
    owners = jnp.arange(N_TENSOR, dtype=jnp.int32)
    row_ids = (owners[:, None] * ROWS_DEV + route_order[:, :SLOTS]).reshape(-1).astype(jnp.int32)
    is_live = (jnp.arange(SLOTS, dtype=jnp.int32)[None, :] < route_counts[:, None]).reshape(-1)
    chosen = tokens[row_ids]
    chosen_wide = chosen.astype(jnp.float32)
    router_logit = jnp.dot(chosen, w_router, preferred_element_type=jnp.float32)
    normed = jnp.where(is_live[:, None], rms_scale(chosen_wide, gain_in), 0.0).astype(jnp.bfloat16)
    gate_up = jnp.dot(normed, w_gate_up, preferred_element_type=jnp.float32)
    gate_up = gate_up.reshape(-1, N_TENSOR, 2, FF_DEV)
    hidden = (jax.nn.silu(gate_up[:, :, 0]) * gate_up[:, :, 1]).astype(jnp.bfloat16)
    down_blocks = w_down.reshape(N_TENSOR, FF_DEV, D)
    branch = jnp.zeros((N_TENSOR * SLOTS, D), jnp.float32)
    for shard in range(N_TENSOR):
        partial_value = jnp.dot(hidden[:, shard], down_blocks[shard], preferred_element_type=jnp.float32)
        partial_value = lax.optimization_barrier(partial_value.astype(jnp.bfloat16))
        branch = branch + partial_value.astype(jnp.float32)
    update = (chosen_wide + jax.nn.sigmoid(router_logit)[:, None] * branch).astype(jnp.bfloat16)
    update = jnp.where(is_live[:, None], update, chosen)
    mixed = tokens.at[row_ids].set(update)
    normed_next = rms_scale(mixed.astype(jnp.float32), gain_next).astype(jnp.bfloat16)
    query = jnp.dot(normed_next, w_query, preferred_element_type=jnp.float32).astype(jnp.bfloat16)
    return (mixed, query)
```

```python
import jax
import jax.numpy as jnp
from jax import lax
from jax.experimental import pallas as pl
from jax.experimental.pallas import tpu as pltpu
from jax.sharding import PartitionSpec as P

T = 16
DP = 8
D = 8192
ROWS = 128
HEAD = 128
UNITS = 128
QN = 4
CW = D // QN
KE = D // DP
ROUTED = 256
BAL = ROUTED // T
EPS = 1e-05
MESH = pl.DeviceIdType.MESH
BF = jnp.bfloat16
F32 = jnp.float32
I32 = jnp.int32


def spread(axis, size, me, source, target, send_sem, recv_sem):
    def body(k, carry):
        peer = lax.rem(me + k, size)
        pltpu.make_async_remote_copy(
            src_ref=source(peer),
            dst_ref=target,
            send_sem=send_sem,
            recv_sem=recv_sem,
            device_id={axis: peer},
            device_id_type=MESH,
        ).start()
        return carry

    lax.fori_loop(1, size, body, 0)


def drain(view, sem):
    pltpu.make_async_copy(view, view, sem).wait()


def iota(shape, dim):
    return lax.broadcasted_iota(I32, shape, dim)


def dot(a, b):
    return jnp.dot(a, b, preferred_element_type=F32)


def one_hot(mask):
    return jnp.where(mask, 1.0, 0.0).astype(BF)


def column_of(row):
    eye = iota((ROWS, ROWS), 0) == iota((ROWS, ROWS), 1)
    return jnp.sum(jnp.where(eye, row.astype(F32), 0.0), axis=1, keepdims=True).astype(I32)


def kernel(
    order_ref, count_ref, wr_ref, gin_ref, gnx_ref, tok_hbm, wgu_hbm, wd_hbm, wq_hbm,
    mixed_hbm, query_hbm,
    tok, wgu, wd, tabs, offs, n0, xr, wqg, pq, qr, a2s, a2r, ag, part, rs, xb,
    rts, rtr, nn, nr, rp, rpr, rqs, rq, q0s, q0r, mix, qo,
    local_sem, send_sem, recv_sem,
):
    t = lax.axis_index("tensor")
    d = lax.axis_index("dp")

    load_tok = pltpu.make_async_copy(tok_hbm, tok, local_sem.at[0])
    load_tok.start()
    load_wgu = pltpu.make_async_copy(wgu_hbm, wgu, local_sem.at[1])
    load_wgu.start()
    load_wd = pltpu.make_async_copy(wd_hbm, wd, local_sem.at[2])
    load_wd.start()

    def wq_rows(peer_d):
        return wq_hbm.at[pl.ds(pl.multiple_of(peer_d * KE, KE), KE), :]

    def wq_cols(at):
        return wqg.at[:, pl.ds(pl.multiple_of(at * HEAD, HEAD), HEAD)]

    own_wq = pltpu.make_async_copy(wq_rows(d), wq_cols(t), local_sem.at[3])
    own_wq.start()

    barrier = pltpu.get_barrier_semaphore()

    def greet_t(k, carry):
        pl.semaphore_signal(barrier, inc=1, device_id={"tensor": lax.rem(t + k, T)}, device_id_type=MESH)
        return carry

    def greet_d(k, carry):
        pl.semaphore_signal(barrier, inc=1, device_id={"dp": lax.rem(d + k, DP)}, device_id_type=MESH)
        return carry

    lax.fori_loop(1, T, greet_t, 0)
    lax.fori_loop(1, DP, greet_d, 0)
    pl.semaphore_wait(barrier, T - 1 + DP - 1)

    count = count_ref[0]
    slot = iota((8, ROWS), 1)
    values = jnp.where(slot < count, slot + 1, 0).astype(F32).astype(BF)
    pairs = one_hot(iota((ROWS, ROWS), 0) == order_ref[...])
    own = lax.dot_general(values, pairs, (((1,), (1,)), ((), ())), preferred_element_type=F32)
    tabs[pl.ds(t, 1)] = (own.astype(I32) - 1)[None]
    spread("tensor", T, t, lambda peer: tabs.at[t], tabs.at[t], send_sem.at[0], recv_sem.at[0])

    load_tok.wait()
    square = jnp.zeros((ROWS, 1), F32)
    for e in range(DP):
        wide = tok[:, e * KE:(e + 1) * KE].astype(F32)
        square += jnp.sum(wide * wide, axis=1, keepdims=True)
    scale = lax.rsqrt(square / D + EPS)
    for e in range(DP):
        cols = slice(e * KE, (e + 1) * KE)
        n0[e] = (tok[:, cols].astype(F32) * scale * gnx_ref[:, cols]).astype(BF)
    spread("dp", DP, d, lambda peer: n0.at[peer], xr.at[d], send_sem.at[1], recv_sem.at[1])
    own_n0 = pltpu.make_async_copy(n0.at[d], xr.at[d], local_sem.at[4])
    own_n0.start()

    drain(tabs.at[pl.ds(0, T - 1)], recv_sem.at[0])
    marks = one_hot(tabs[...].reshape(T * 8, ROWS) >= 0)
    counts = dot(marks, jnp.ones((ROWS, ROWS), BF))
    sub, lane = iota((ROWS, ROWS), 0), iota((ROWS, ROWS), 1)
    before = one_hot(((lane // 8) < (sub // 8)) & (lane % 8 == 0))
    firsts = dot(before, counts.astype(BF))
    firsts_i, counts_i = firsts.astype(I32), counts.astype(I32)
    offs[...] = firsts_i
    first_l, last_l = [], []
    for half in range(2):
        group = iota((8, ROWS), 1) // 16
        lo, hi = jnp.zeros((8, ROWS), I32), jnp.zeros((8, ROWS), I32)
        for i in range(8):
            o = half * 8 + i
            f = firsts_i[o * 8:(o + 1) * 8]
            c = counts_i[o * 8:(o + 1) * 8]
            lo = jnp.where(group == i, f, lo)
            hi = jnp.where(group == i, f + c, hi)
        first_l.append(lo)
        last_l.append(hi)
    first_l = jnp.concatenate(first_l, axis=1)[:1]
    last_l = jnp.concatenate(last_l, axis=1)[:1]

    my_first = offs[pl.ds(pl.multiple_of(t * 8, 8), 8), :][:1]
    my_slots = tabs[pl.ds(t, 1)][0, :1]
    g_row = jnp.where(my_slots >= 0, my_slots + my_first, -1)
    j = iota((ROUTED, ROWS), 0)
    hit = ((j // 16) == (g_row % 16)) & ((j % 4) == ((g_row // 16) % 4)) & (g_row >= 0)
    pick = jnp.concatenate([one_hot(hit & (((j // 4) % 4) == q)) for q in range(QN)], axis=1)
    tile = 512
    for i in range(CW // tile):
        stacked = jnp.concatenate([tok[:, q * CW + i * tile:q * CW + (i + 1) * tile] for q in range(QN)], axis=0)
        a2s[:, i * tile:(i + 1) * tile] = dot(pick, stacked).astype(BF)

    def block16(ref, at):
        return ref.at[pl.ds(pl.multiple_of(at * 16, 16), 16), :]

    spread("tensor", T, t, lambda peer: block16(a2s, peer), block16(a2r, t), send_sem.at[2], recv_sem.at[2])
    own_a2 = pltpu.make_async_copy(block16(a2s, t), block16(a2r, t), local_sem.at[5])
    own_a2.start()

    spread("tensor", T, t, lambda peer: wq_rows(d), wq_cols(t), send_sem.at[3], recv_sem.at[3])

    bi, bj = iota((QN * BAL, ROUTED), 0), iota((QN * BAL, ROUTED), 1)
    g_bal = (bi % BAL) * T + t
    compact = one_hot(
        ((bi // BAL) == ((bj // 4) % 4)) & ((bj % 4) == (bi % 4)) & (first_l <= g_bal) & (g_bal < last_l)
    )
    own_a2.wait()
    drain(a2r.at[pl.ds(0, (T - 1) * 16), :], recv_sem.at[2])
    square, logit = jnp.zeros((BAL, 1), F32), jnp.zeros((BAL, 1), F32)
    xb[...] = dot(compact, a2r[...])
    for q in range(QN):
        rows = xb[q * BAL:(q + 1) * BAL]
        square += jnp.sum(rows * rows, axis=1, keepdims=True)
        logit += jnp.sum(rows * wr_ref[:, q * CW:(q + 1) * CW].astype(F32), axis=1, keepdims=True)
    scale = lax.rsqrt(square / D + EPS)
    for q in range(QN):
        rows = xb[q * BAL:(q + 1) * BAL] * scale * gin_ref[:, q * CW:(q + 1) * CW]
        ag[q, pl.ds(pl.multiple_of(t * BAL, BAL), BAL), :] = rows.astype(BF)

    def ag_block(ref, at):
        return ref.at[:, pl.ds(pl.multiple_of(at * BAL, BAL), BAL), :]

    spread("tensor", T, t, lambda peer: ag_block(ag, t), ag_block(ag, t), send_sem.at[4], recv_sem.at[4])

    own_n0.wait()
    own_wq.wait()
    drain(xr.at[pl.ds(0, DP - 1)], recv_sem.at[1])
    drain(wqg.at[:, pl.ds(0, (T - 1) * HEAD)], recv_sem.at[3])

    def query_tile(i, carry):
        cols = pl.ds(pl.multiple_of(i * 256, 256), 256)
        weights = wqg[:, cols]
        for e in range(DP):
            pq[e, :, cols] = dot(xr[e], weights).astype(BF)
        return carry

    lax.fori_loop(0, T * HEAD // 256, query_tile, 0)
    spread("dp", DP, d, lambda peer: pq.at[peer], qr.at[d], send_sem.at[5], recv_sem.at[5])
    own_pq = pltpu.make_async_copy(pq.at[d], qr.at[d], local_sem.at[6])
    own_pq.start()

    load_wgu.wait()
    load_wd.wait()
    drain(ag.at[:, pl.ds(0, (T - 1) * BAL), :], recv_sem.at[4])
    gate_up = dot(ag[0], wgu[:CW])
    for q in range(1, QN):
        gate_up += dot(ag[q], wgu[q * CW:(q + 1) * CW])
    gate, up = gate_up[:, :UNITS], gate_up[:, UNITS:]
    hidden = (gate / (1.0 + jnp.exp(-gate)) * up).astype(BF)
    for q in range(QN):
        for i in range(CW // tile):
            at = q * CW + i * tile
            part[q, :, i * tile:(i + 1) * tile] = dot(hidden, wd[:, at:at + tile]).astype(BF)
    spread("tensor", T, t, lambda peer: ag_block(part, peer), rs.at[t], send_sem.at[6], recv_sem.at[6])
    own_part = pltpu.make_async_copy(ag_block(part, t), rs.at[t], local_sem.at[7])
    own_part.start()

    own_pq.wait()
    drain(qr.at[pl.ds(0, DP - 1)], recv_sem.at[5])

    def head_tile(i, carry):
        cols = pl.ds(pl.multiple_of(i * HEAD, HEAD), HEAD)
        total = qr[0, :, cols].astype(F32)
        for e in range(1, DP):
            total += qr[e, :, cols].astype(F32)
        q0s[pl.ds(i, 1)] = total.astype(BF)[None]
        return carry

    lax.fori_loop(0, T, head_tile, 0)
    spread("tensor", T, t, lambda peer: q0s.at[peer], q0r.at[t], send_sem.at[7], recv_sem.at[7])
    own_q0 = pltpu.make_async_copy(q0s.at[t], q0r.at[t], local_sem.at[8])
    own_q0.start()

    own_part.wait()
    drain(rs.at[pl.ds(0, T - 1)], recv_sem.at[6])
    weight = 1.0 / (1.0 + jnp.exp(-logit))
    square = jnp.zeros((BAL, 1), F32)
    mixed_b = []
    for q in range(QN):
        branch = rs[0, q].astype(F32)
        for s in range(1, T):
            branch += rs[s, q].astype(F32)
        rows = (xb[q * BAL:(q + 1) * BAL] + weight * branch).astype(BF)
        mixed_b.append(rows)
        wide = rows.astype(F32)
        square += jnp.sum(wide * wide, axis=1, keepdims=True)
    scale = lax.rsqrt(square / D + EPS)
    for q in range(QN):
        wide = mixed_b[q].astype(F32) * scale * gnx_ref[:, q * CW:(q + 1) * CW]
        for h in range(CW // KE):
            nn[q * (CW // KE) + h] = wide[:, h * KE:(h + 1) * KE].astype(BF)
    spread("dp", DP, d, lambda peer: nn.at[peer], nr.at[d], send_sem.at[8], recv_sem.at[8])
    own_nn = pltpu.make_async_copy(nn.at[d], nr.at[d], local_sem.at[9])
    own_nn.start()

    stacked = jnp.concatenate(mixed_b, axis=0)
    ri, rj = iota((16, QN * BAL), 0), iota((16, QN * BAL), 1)
    g_bal = (rj % BAL) * T + t
    fits = ((rj // BAL) == (ri // 4)) & ((rj % 4) == (ri % 4))
    back = []
    for o in range(T):
        lo = jnp.concatenate([firsts_i[o * 8:(o + 1) * 8, :QN * BAL]] * 2, axis=0)
        n = jnp.concatenate([counts_i[o * 8:(o + 1) * 8, :QN * BAL]] * 2, axis=0)
        back.append(one_hot(fits & (lo <= g_bal) & (g_bal < lo + n)))
    back = jnp.concatenate(back, axis=0)
    for i in range(CW // tile):
        rts[:, i * tile:(i + 1) * tile] = dot(back, stacked[:, i * tile:(i + 1) * tile]).astype(BF)
    spread("tensor", T, t, lambda peer: block16(rts, peer), block16(rtr, t), send_sem.at[9], recv_sem.at[9])
    own_rt = pltpu.make_async_copy(block16(rts, t), block16(rtr, t), local_sem.at[10])
    own_rt.start()

    own_nn.wait()
    drain(nr.at[pl.ds(0, DP - 1)], recv_sem.at[8])
    rows = nr[...].reshape(DP * BAL, KE)
    for i in range(T * HEAD // tile):
        cols = slice(i * tile, (i + 1) * tile)
        rp[:, :, cols] = dot(rows, wqg[:, cols]).astype(BF).reshape(DP, BAL, tile)
    spread("dp", DP, d, lambda peer: rp.at[peer], rpr.at[d], send_sem.at[10], recv_sem.at[10])
    own_rp = pltpu.make_async_copy(rp.at[d], rpr.at[d], local_sem.at[11])
    own_rp.start()

    own_rp.wait()
    drain(rpr.at[pl.ds(0, DP - 1)], recv_sem.at[10])
    total = rpr[0].astype(F32)
    for e in range(1, DP):
        total += rpr[e].astype(F32)
    total = total.astype(BF)
    for h in range(T):
        rqs[h] = total[:, h * HEAD:(h + 1) * HEAD]
    spread("tensor", T, t, lambda peer: rqs.at[peer], rq.at[t], send_sem.at[11], recv_sem.at[11])
    own_rq = pltpu.make_async_copy(rqs.at[t], rq.at[t], local_sem.at[12])
    own_rq.start()

    own_rt.wait()
    drain(rtr.at[pl.ds(0, (T - 1) * 16), :], recv_sem.at[9])
    g_col = column_of(g_row)
    jl = iota((ROWS, ROUTED), 1)
    hit = ((jl // 16) == (g_col % 16)) & ((jl % 4) == ((g_col // 16) % 4)) & (g_col >= 0)
    for q in range(QN):
        place = one_hot(hit & (((jl // 4) % 4) == q))
        for i in range(CW // tile):
            at = q * CW + i * tile
            moved = dot(place, rtr[:, i * tile:(i + 1) * tile]).astype(BF)
            mix[:, at:at + tile] = jnp.where(g_col >= 0, moved, tok[:, at:at + tile])
    out_mixed = pltpu.make_async_copy(mix, mixed_hbm, local_sem.at[13])
    out_mixed.start()

    own_q0.wait()
    drain(q0r.at[pl.ds(0, T - 1)], recv_sem.at[7])
    own_rq.wait()
    drain(rq.at[pl.ds(0, T - 1)], recv_sem.at[11])
    routed = rq[...].reshape(ROUTED, HEAD)
    g_lane = (jl % 16) * T + jl // 16

    def place_owner(o, carry):
        slots = tabs[pl.ds(o, 1)][0, :1]
        lo = offs[pl.ds(pl.multiple_of(o * 8, 8), 8), :][:1]
        col = column_of(jnp.where(slots >= 0, slots + lo, -1))
        moved = dot(one_hot(col == g_lane), routed).astype(BF)
        plain = q0r[pl.ds(o, 1)][0]
        qo[pl.ds(pl.multiple_of(o * ROWS, ROWS), ROWS), :] = jnp.where(col >= 0, moved, plain)
        return carry

    lax.fori_loop(0, T, place_owner, 0)
    out_query = pltpu.make_async_copy(qo, query_hbm, local_sem.at[14])
    out_query.start()

    drain(tabs.at[pl.ds(0, T - 1)], send_sem.at[0])
    drain(n0.at[pl.ds(0, DP - 1)], send_sem.at[1])
    drain(a2s.at[pl.ds(0, (T - 1) * 16), :], send_sem.at[2])
    drain(wqg.at[:, pl.ds(0, (T - 1) * HEAD)], send_sem.at[3])
    drain(ag.at[:, pl.ds(0, (T - 1) * BAL), :], send_sem.at[4])
    drain(pq.at[pl.ds(0, DP - 1)], send_sem.at[5])
    drain(part.at[:, pl.ds(0, (T - 1) * BAL), :], send_sem.at[6])
    drain(q0s.at[pl.ds(0, T - 1)], send_sem.at[7])
    drain(nn.at[pl.ds(0, DP - 1)], send_sem.at[8])
    drain(rts.at[pl.ds(0, (T - 1) * 16), :], send_sem.at[9])
    drain(rp.at[pl.ds(0, DP - 1)], send_sem.at[10])
    drain(rqs.at[pl.ds(0, T - 1)], send_sem.at[11])
    out_mixed.wait()
    out_query.wait()


def on_device(tokens, route_order, route_counts, w_router, gain_in, w_gate_up, w_down, gain_next, w_query):
    vmem = pl.BlockSpec(memory_space=pltpu.VMEM)
    anywhere = pl.BlockSpec(memory_space=pl.ANY)
    return pl.pallas_call(
        kernel,
        out_shape=(
            jax.ShapeDtypeStruct((ROWS, D), BF),
            jax.ShapeDtypeStruct((T * ROWS, HEAD), BF),
        ),
        in_specs=[vmem, pl.BlockSpec(memory_space=pltpu.SMEM), vmem, vmem, vmem] + [anywhere] * 4,
        out_specs=(anywhere, anywhere),
        scratch_shapes=[
            pltpu.VMEM((ROWS, D), BF),
            pltpu.VMEM((D, 2 * UNITS), BF),
            pltpu.VMEM((UNITS, D), BF),
            pltpu.VMEM((T, 8, ROWS), I32),
            pltpu.VMEM((ROWS, ROWS), I32),
            pltpu.VMEM((DP, ROWS, KE), BF),
            pltpu.VMEM((DP, ROWS, KE), BF),
            pltpu.VMEM((KE, T * HEAD), BF),
            pltpu.VMEM((DP, ROWS, T * HEAD), BF),
            pltpu.VMEM((DP, ROWS, T * HEAD), BF),
            pltpu.VMEM((ROUTED, CW), BF),
            pltpu.VMEM((ROUTED, CW), BF),
            pltpu.VMEM((QN, ROUTED, CW), BF),
            pltpu.VMEM((QN, ROUTED, CW), BF),
            pltpu.VMEM((T, QN, BAL, CW), BF),
            pltpu.VMEM((QN * BAL, CW), F32),
            pltpu.VMEM((ROUTED, CW), BF),
            pltpu.VMEM((ROUTED, CW), BF),
            pltpu.VMEM((DP, BAL, KE), BF),
            pltpu.VMEM((DP, BAL, KE), BF),
            pltpu.VMEM((DP, BAL, T * HEAD), BF),
            pltpu.VMEM((DP, BAL, T * HEAD), BF),
            pltpu.VMEM((T, BAL, HEAD), BF),
            pltpu.VMEM((T, BAL, HEAD), BF),
            pltpu.VMEM((T, ROWS, HEAD), BF),
            pltpu.VMEM((T, ROWS, HEAD), BF),
            pltpu.VMEM((ROWS, D), BF),
            pltpu.VMEM((T * ROWS, HEAD), BF),
            pltpu.SemaphoreType.DMA((15,)),
            pltpu.SemaphoreType.DMA((12,)),
            pltpu.SemaphoreType.DMA((12,)),
        ],
        compiler_params=pltpu.CompilerParams(
            collective_id=0, has_side_effects=True, vmem_limit_bytes=60 * 1024 * 1024
        ),
    )(
        route_order, route_counts, w_router.reshape(1, D), gain_in.reshape(1, D), gain_next.reshape(1, D),
        tokens, w_gate_up, w_down, w_query,
    )


def solution(mesh):
    in_specs = (
        P(("dp", "tensor"), None),
        P(("dp", "tensor"), None),
        P(("dp", "tensor")),
        P(),
        P(),
        P(None, "tensor"),
        P("tensor", None),
        P(),
        P(None, "tensor"),
    )
    out_specs = (P(("dp", "tensor"), None), P("dp", "tensor"))
    return jax.shard_map(
        on_device, mesh=mesh, in_specs=in_specs, out_specs=out_specs, check_vma=False
    )
```

```python
import jax
import jax.numpy as jnp
from jax import lax
from jax.experimental import pallas as pl
from jax.experimental.pallas import tpu as pltpu
from jax.sharding import PartitionSpec as P

T = 16
DP = 8
D = 8192
ROWS = 128
HEAD = 128
UNITS = 128
QN = 4
CW = D // QN
KE = D // DP
ROUTED = 256
BAL = ROUTED // T
NZ = 4
NY = 4
NX = 4
NC = 2
LINE = DP * BAL
HALF = KE // 2
EPS = 1e-05
MESH = pl.DeviceIdType.MESH
BF = jnp.bfloat16
F32 = jnp.float32
I32 = jnp.int32


def start(source, target, axis, peer, send_sem, recv_sem):
    pltpu.make_async_remote_copy(
        src_ref=source,
        dst_ref=target,
        send_sem=send_sem,
        recv_sem=recv_sem,
        device_id={axis: peer},
        device_id_type=MESH,
    ).start()


def spread(axis, size, me, source, target, send_sem, recv_sem):
    def body(k, carry):
        peer = lax.rem(me + k, size)
        start(source(peer), target, axis, peer, send_sem, recv_sem)
        return carry

    lax.fori_loop(1, size, body, 0)


def drain(view, sem):
    pltpu.make_async_copy(view, view, sem).wait()


def iota(shape, dim):
    return lax.broadcasted_iota(I32, shape, dim)


def dot(a, b):
    return jnp.dot(a, b, preferred_element_type=F32)


def one_hot(mask):
    return jnp.where(mask, 1.0, 0.0).astype(BF)


def aligned(at, size):
    return pl.ds(pl.multiple_of(at * size, size), size)


def column_of(row):
    eye = iota((ROWS, ROWS), 0) == iota((ROWS, ROWS), 1)
    return jnp.sum(jnp.where(eye, row.astype(F32), 0.0), axis=1, keepdims=True).astype(I32)


def kernel(
    order_ref, count_ref, wr_ref, gin_ref, gnx_ref, tok_hbm, wgu_hbm, wd_hbm, wq_hbm,
    mixed_hbm, query_hbm,
    tok, tabs, offs, n0, xr, wga, wda, wqa, wqb, a2s, a2r, xb, ns, gx, rws, rwr,
    gp, gc, gs, gr, hid, dn, dr, pq, pc, ps, qr, q0s, q0r, ms, mb, rp, rpr, rqs, rq,
    rts, rtr, mix, qo,
    local_sem, send_sem, recv_sem,
):
    t = lax.axis_index("tensor")
    d = lax.axis_index("dp")
    z, y = lax.div(t, NY), lax.rem(t, NY)
    x, c = lax.div(d, NC), lax.rem(d, NC)
    near = (1, 3, 2)

    def at_y(k):
        return lax.rem(y + k, NY)

    def at_z(k):
        return lax.rem(z + k, NZ)

    def at_x(k):
        return lax.rem(x + k, NX)

    my_k = aligned(d, KE)
    load_tok = pltpu.make_async_copy(tok_hbm, tok, local_sem.at[0])
    load_tok.start()
    own_wg = pltpu.make_async_copy(wgu_hbm.at[my_k, :], wga.at[y], local_sem.at[1])
    own_wg.start()
    own_wd = pltpu.make_async_copy(wd_hbm.at[:, my_k], wda.at[y], local_sem.at[2])
    own_wd.start()

    def wq_half(i):
        return wq_hbm.at[pl.ds(pl.multiple_of(d * KE + i * HALF, HALF), HALF), :]

    own_wqa = pltpu.make_async_copy(wq_half(0), wqa.at[:, aligned(z * NY + y, HEAD)], local_sem.at[3])
    own_wqa.start()
    own_wqb = pltpu.make_async_copy(wq_half(1), wqb.at[:, aligned(y * NZ + z, HEAD)], local_sem.at[4])
    own_wqb.start()

    barrier = pltpu.get_barrier_semaphore()

    def greet_t(k, carry):
        pl.semaphore_signal(barrier, inc=1, device_id={"tensor": lax.rem(t + k, T)}, device_id_type=MESH)
        return carry

    def greet_d(k, carry):
        pl.semaphore_signal(barrier, inc=1, device_id={"dp": lax.rem(d + k, DP)}, device_id_type=MESH)
        return carry

    lax.fori_loop(1, T, greet_t, 0)
    lax.fori_loop(1, DP, greet_d, 0)
    pl.semaphore_wait(barrier, T - 1 + DP - 1)

    count = count_ref[0]
    slot = iota((8, ROWS), 1)
    values = jnp.where(slot < count, slot + 1, 0).astype(F32).astype(BF)
    pairs = one_hot(iota((ROWS, ROWS), 0) == order_ref[...])
    own = lax.dot_general(values, pairs, (((1,), (1,)), ((), ())), preferred_element_type=F32)
    tabs[pl.ds(t, 1)] = (own.astype(I32) - 1)[None]
    spread("tensor", T, t, lambda peer: tabs.at[t], tabs.at[t], send_sem.at[0], recv_sem.at[0])

    load_tok.wait()
    square = jnp.zeros((ROWS, 1), F32)
    for e in range(DP):
        wide = tok[:, e * KE:(e + 1) * KE].astype(F32)
        square += jnp.sum(wide * wide, axis=1, keepdims=True)
    scale = lax.rsqrt(square / D + EPS)
    for e in range(DP):
        cols = slice(e * KE, (e + 1) * KE)
        n0[e] = (tok[:, cols].astype(F32) * scale * gnx_ref[:, cols]).astype(BF)
    spread("dp", DP, d, lambda peer: n0.at[peer], xr.at[d], send_sem.at[1], recv_sem.at[1])
    own_n0 = pltpu.make_async_copy(n0.at[d], xr.at[d], local_sem.at[5])
    own_n0.start()

    drain(tabs.at[pl.ds(0, T - 1)], recv_sem.at[0])
    marks = one_hot(tabs[...].reshape(T * 8, ROWS) >= 0)
    counts = dot(marks, jnp.ones((ROWS, ROWS), BF))
    sub, lane = iota((ROWS, ROWS), 0), iota((ROWS, ROWS), 1)
    before = one_hot(((lane // 8) < (sub // 8)) & (lane % 8 == 0))
    firsts = dot(before, counts.astype(BF))
    firsts_i, counts_i = firsts.astype(I32), counts.astype(I32)
    offs[...] = firsts_i
    first_l, last_l = [], []
    for half in range(2):
        group = iota((8, ROWS), 1) // 16
        lo, hi = jnp.zeros((8, ROWS), I32), jnp.zeros((8, ROWS), I32)
        for i in range(8):
            o = half * 8 + i
            f = firsts_i[o * 8:(o + 1) * 8]
            n = counts_i[o * 8:(o + 1) * 8]
            lo = jnp.where(group == i, f, lo)
            hi = jnp.where(group == i, f + n, hi)
        first_l.append(lo)
        last_l.append(hi)
    first_l = jnp.concatenate(first_l, axis=1)[:1]
    last_l = jnp.concatenate(last_l, axis=1)[:1]

    my_first = offs[aligned(t, 8), :][:1]
    my_slots = tabs[pl.ds(t, 1)][0, :1]
    g_row = jnp.where(my_slots >= 0, my_slots + my_first, -1)
    j = iota((ROUTED, ROWS), 0)
    hit = ((j // 16) == (g_row % 16)) & ((j % 4) == ((g_row // 16) % 4)) & (g_row >= 0)
    pick = jnp.concatenate([one_hot(hit & (((j // 4) % 4) == q)) for q in range(QN)], axis=1)
    tile = 512
    for i in range(CW // tile):
        stacked = jnp.concatenate([tok[:, q * CW + i * tile:q * CW + (i + 1) * tile] for q in range(QN)], axis=0)
        a2s[:, i * tile:(i + 1) * tile] = dot(pick, stacked).astype(BF)
    spread("tensor", T, t, lambda peer: a2s.at[aligned(peer, 16), :], a2r.at[aligned(t, 16), :], send_sem.at[2], recv_sem.at[2])
    own_a2 = pltpu.make_async_copy(a2s.at[aligned(t, 16), :], a2r.at[aligned(t, 16), :], local_sem.at[6])
    own_a2.start()

    own_wg.wait()
    own_wd.wait()
    own_wqa.wait()
    own_wqb.wait()
    for k in near:
        start(wga.at[y], wga.at[y], "tensor", z * NY + at_y(k), send_sem.at[3], recv_sem.at[3])
    for k in near:
        start(wqb.at[:, aligned(y * NZ + z, HEAD)], wqb.at[:, aligned(y * NZ + z, HEAD)], "tensor", at_z(k) * NY + y, send_sem.at[4], recv_sem.at[4])
    for k in near:
        start(wqa.at[:, aligned(z * NY + y, HEAD)], wqa.at[:, aligned(z * NY + y, HEAD)], "tensor", z * NY + at_y(k), send_sem.at[5], recv_sem.at[5])
    for k in near:
        start(wda.at[y], wda.at[y], "tensor", z * NY + at_y(k), send_sem.at[6], recv_sem.at[6])

    bi, bj = iota((QN * BAL, ROUTED), 0), iota((QN * BAL, ROUTED), 1)
    g_bal = (bi % BAL) * T + t
    compact = one_hot(
        ((bi // BAL) == ((bj // 4) % 4)) & ((bj % 4) == (bi % 4)) & (first_l <= g_bal) & (g_bal < last_l)
    )
    own_a2.wait()
    drain(a2r.at[pl.ds(0, (T - 1) * 16), :], recv_sem.at[2])
    square, logit = jnp.zeros((BAL, 1), F32), jnp.zeros((BAL, 1), F32)
    xb[...] = dot(compact, a2r[...])
    for q in range(QN):
        rows = xb[q * BAL:(q + 1) * BAL]
        square += jnp.sum(rows * rows, axis=1, keepdims=True)
    scale = lax.rsqrt(square / D + EPS)
    per = CW // KE
    for q in range(QN):
        rows = xb[q * BAL:(q + 1) * BAL] * scale * gin_ref[:, q * CW:(q + 1) * CW]
        for h in range(per):
            ns[q * per + h] = rows[:, h * KE:(h + 1) * KE].astype(BF)
    my_rows = gx.at[z, d]
    spread("dp", DP, d, lambda peer: ns.at[peer], my_rows, send_sem.at[7], recv_sem.at[7])
    own_ns = pltpu.make_async_copy(ns.at[d], my_rows, local_sem.at[7])
    own_ns.start()
    for q in range(QN):
        rows = xb[q * BAL:(q + 1) * BAL]
        logit += jnp.sum(rows * wr_ref[:, q * CW:(q + 1) * CW].astype(F32), axis=1, keepdims=True)
        for h in range(per):
            rws[q * per + h, :, :KE] = rows[:, h * KE:(h + 1) * KE].astype(BF)
    weight = 1.0 / (1.0 + jnp.exp(-logit))
    upper = weight.astype(BF)
    lower = (weight - upper.astype(F32)).astype(BF)
    pair = jnp.where(iota((BAL, 128), 1) == 0, upper.astype(F32), lower.astype(F32)).astype(BF)
    for e in range(DP):
        rws[e, :, KE:] = pair
    spread("dp", DP, d, lambda peer: rws.at[peer], rwr.at[d], send_sem.at[8], recv_sem.at[8])
    own_rw = pltpu.make_async_copy(rws.at[d], rwr.at[d], local_sem.at[8])
    own_rw.start()

    own_ns.wait()
    drain(gx.at[0, pl.ds(0, DP - 1)], recv_sem.at[7])
    for k in near:
        start(gx.at[z], gx.at[z], "tensor", at_z(k) * NY + y, send_sem.at[9], recv_sem.at[9])

    drain(wqa.at[:, pl.ds(0, 3 * HEAD)], recv_sem.at[5])
    drain(wqb.at[:, pl.ds(0, 3 * HEAD)], recv_sem.at[4])
    for k in near:
        start(wqa.at[:, aligned(z, NY * HEAD)], wqa.at[:, aligned(z, NY * HEAD)], "tensor", at_z(k) * NY + y, send_sem.at[10], recv_sem.at[10])
        start(wqb.at[:, aligned(y, NZ * HEAD)], wqb.at[:, aligned(y, NZ * HEAD)], "tensor", z * NY + at_y(k), send_sem.at[11], recv_sem.at[11])

    drain(wga.at[pl.ds(0, NY - 1)], recv_sem.at[3])
    drain(gx.at[pl.ds(0, NZ - 1)], recv_sem.at[9])
    rows = gx[...].reshape(NZ * LINE, KE)
    for i in range(NY):
        gp[:, :, :, i * 2 * UNITS:(i + 1) * 2 * UNITS] = dot(rows, wga[i]).reshape(NC, NX, NZ * LINE // DP, 2 * UNITS)
    sibling = x * NC + 1 - c
    start(gp.at[1 - c], gc, "dp", sibling, send_sem.at[12], recv_sem.at[12])
    drain(gc, recv_sem.at[12])
    for i in range(NX):
        gs[i] = (gp[c, i] + gc[i]).astype(BF)
    for k in near:
        start(gs.at[at_x(k)], gr.at[x], "dp", at_x(k) * NC + c, send_sem.at[13], recv_sem.at[13])
    own_gs = pltpu.make_async_copy(gs.at[x], gr.at[x], local_sem.at[9])
    own_gs.start()

    own_gs.wait()
    drain(gr.at[pl.ds(0, NX - 1)], recv_sem.at[13])
    total = gr[0].astype(F32)
    for i in range(1, NX):
        total += gr[i].astype(F32)
    for i in range(NY):
        gate = total[:, i * 2 * UNITS:i * 2 * UNITS + UNITS]
        up = total[:, i * 2 * UNITS + UNITS:(i + 1) * 2 * UNITS]
        hid[c, pl.ds(x, 1), :, i * UNITS:(i + 1) * UNITS] = (gate / (1.0 + jnp.exp(-gate)) * up).astype(BF)[None]
    for k in near:
        start(hid.at[c, x], hid.at[c, x], "dp", at_x(k) * NC + c, send_sem.at[14], recv_sem.at[14])
    drain(hid.at[0, pl.ds(0, NX - 1)], recv_sem.at[14])
    start(hid.at[c], hid.at[c], "dp", sibling, send_sem.at[15], recv_sem.at[15])

    drain(wda.at[pl.ds(0, NY - 1)], recv_sem.at[6])
    drain(hid.at[0], recv_sem.at[15])
    hidden = hid[...].reshape(NZ * LINE, NY * UNITS)
    down = wda[...].reshape(NY * UNITS, KE)
    for i in range(KE // 256):
        cols = slice(i * 256, (i + 1) * 256)
        dn[:, :, cols] = dot(hidden, down[:, cols]).astype(BF).reshape(NZ, LINE, 256)
    for k in near:
        start(dn.at[at_z(k)], dr.at[z], "tensor", at_z(k) * NY + y, send_sem.at[16], recv_sem.at[16])
    own_dn = pltpu.make_async_copy(dn.at[z], dr.at[z], local_sem.at[10])
    own_dn.start()

    own_n0.wait()
    drain(xr.at[pl.ds(0, DP - 1)], recv_sem.at[1])
    drain(wqa.at[:, pl.ds(0, 3 * NY * HEAD)], recv_sem.at[10])
    drain(wqb.at[:, pl.ds(0, 3 * NZ * HEAD)], recv_sem.at[11])

    def head_pair(i):
        hz, hy = lax.div(i, NY // 2), lax.rem(i, NY // 2) * 2
        upper = wqa[:, aligned(i, 2 * HEAD)]
        lower = jnp.concatenate([wqb[:, aligned(hy * NZ + hz, HEAD)], wqb[:, aligned((hy + 1) * NZ + hz, HEAD)]], axis=1)
        return jnp.concatenate([upper, lower], axis=0)

    def query_tile(i, carry):
        weights = head_pair(i)
        for e in range(DP):
            pq[e % NC, e // NC, :, aligned(i, 2 * HEAD)] = dot(xr[e], weights).astype(BF)
        return carry

    lax.fori_loop(0, T // 2, query_tile, 0)
    start(pq.at[1 - c], pc, "dp", sibling, send_sem.at[17], recv_sem.at[17])
    drain(pc, recv_sem.at[17])

    def pair_sum(i, carry):
        cols = aligned(i, 2 * HEAD)
        ps[:, :, cols] = (pq[c, :, :, cols].astype(F32) + pc[:, :, cols].astype(F32)).astype(BF)
        return carry

    lax.fori_loop(0, T // 2, pair_sum, 0)
    for k in near:
        start(ps.at[at_x(k)], qr.at[x], "dp", at_x(k) * NC + c, send_sem.at[18], recv_sem.at[18])
    own_ps = pltpu.make_async_copy(ps.at[x], qr.at[x], local_sem.at[11])
    own_ps.start()

    own_rw.wait()
    drain(rwr.at[pl.ds(0, DP - 1)], recv_sem.at[8])
    own_dn.wait()
    drain(dr.at[pl.ds(0, NZ - 1)], recv_sem.at[16])
    branch = dr[0].astype(F32)
    for i in range(1, NZ):
        branch += dr[i].astype(F32)
    raw = rwr[...].reshape(LINE, KE + 128)
    both = raw[:, KE:].astype(F32)
    weight = both[:, :1] + both[:, 1:2]
    rows = (raw[:, :KE].astype(F32) + weight * branch).astype(BF)
    ms[...] = rows.reshape(DP, BAL, KE)
    spread("dp", DP, d, lambda peer: ms.at[peer], mb.at[d], send_sem.at[19], recv_sem.at[19])
    own_ms = pltpu.make_async_copy(ms.at[d], mb.at[d], local_sem.at[12])
    own_ms.start()
    rows = (rows.astype(F32) * gnx_ref[:, my_k]).astype(BF)
    for i in range(T // 2):
        cols = slice(i * 2 * HEAD, (i + 1) * 2 * HEAD)
        hz, hy = i // (NY // 2), i % (NY // 2) * 2
        first, second = (hy * NZ + hz) * HEAD, ((hy + 1) * NZ + hz) * HEAD
        lower = jnp.concatenate([wqb[:, first:first + HEAD], wqb[:, second:second + HEAD]], axis=1)
        weights = jnp.concatenate([wqa[:, cols], lower], axis=0)
        rp[:, :, cols] = dot(rows, weights).astype(BF).reshape(DP, BAL, 2 * HEAD)
    spread("dp", DP, d, lambda peer: rp.at[peer], rpr.at[d], send_sem.at[20], recv_sem.at[20])
    own_rp = pltpu.make_async_copy(rp.at[d], rpr.at[d], local_sem.at[13])
    own_rp.start()

    own_ms.wait()
    drain(mb.at[pl.ds(0, DP - 1)], recv_sem.at[19])
    square = jnp.zeros((BAL, 1), F32)
    for e in range(DP):
        wide = mb[e].astype(F32)
        square += jnp.sum(wide * wide, axis=1, keepdims=True)
    scale = lax.rsqrt(square / D + EPS)
    ri, rj = iota((16, QN * BAL), 0), iota((16, QN * BAL), 1)
    g_bal = (rj % BAL) * T + t
    fits = ((rj // BAL) == (ri // 4)) & ((rj % 4) == (ri % 4))
    back = []
    for o in range(T):
        lo = jnp.concatenate([firsts_i[o * 8:(o + 1) * 8, :QN * BAL]] * 2, axis=0)
        n = jnp.concatenate([counts_i[o * 8:(o + 1) * 8, :QN * BAL]] * 2, axis=0)
        back.append(one_hot(fits & (lo <= g_bal) & (g_bal < lo + n)))
    back = jnp.concatenate(back, axis=0)
    for h in range(per):
        stacked = jnp.concatenate([mb[q * per + h] for q in range(QN)], axis=0)
        for i in range(KE // tile):
            at = h * KE + i * tile
            rts[:, at:at + tile] = dot(back, stacked[:, i * tile:(i + 1) * tile]).astype(BF)
    spread("tensor", T, t, lambda peer: rts.at[aligned(peer, 16), :], rtr.at[aligned(t, 16), :], send_sem.at[21], recv_sem.at[21])
    own_rt = pltpu.make_async_copy(rts.at[aligned(t, 16), :], rtr.at[aligned(t, 16), :], local_sem.at[14])
    own_rt.start()

    own_rp.wait()
    drain(rpr.at[pl.ds(0, DP - 1)], recv_sem.at[20])
    total = rpr[0].astype(F32)
    for e in range(1, DP):
        total += rpr[e].astype(F32)
    total = (total * scale).astype(BF)
    for h in range(T):
        rqs[h] = total[:, h * HEAD:(h + 1) * HEAD]
    spread("tensor", T, t, lambda peer: rqs.at[peer], rq.at[t], send_sem.at[22], recv_sem.at[22])
    own_rq = pltpu.make_async_copy(rqs.at[t], rq.at[t], local_sem.at[15])
    own_rq.start()

    own_ps.wait()
    drain(qr.at[pl.ds(0, NX - 1)], recv_sem.at[18])

    def head_tile(i, carry):
        cols = aligned(i, HEAD)
        total = qr[0, :, cols].astype(F32)
        for e in range(1, NX):
            total += qr[e, :, cols].astype(F32)
        q0s[pl.ds(i, 1)] = total.astype(BF)[None]
        return carry

    lax.fori_loop(0, T, head_tile, 0)
    spread("tensor", T, t, lambda peer: q0s.at[peer], q0r.at[t], send_sem.at[23], recv_sem.at[23])
    own_q0 = pltpu.make_async_copy(q0s.at[t], q0r.at[t], local_sem.at[16])
    own_q0.start()

    own_rt.wait()
    drain(rtr.at[pl.ds(0, (T - 1) * 16), :], recv_sem.at[21])
    g_col = column_of(g_row)
    jl = iota((ROWS, ROUTED), 1)
    hit = ((jl // 16) == (g_col % 16)) & ((jl % 4) == ((g_col // 16) % 4)) & (g_col >= 0)
    for q in range(QN):
        place = one_hot(hit & (((jl // 4) % 4) == q))
        for i in range(CW // tile):
            at = q * CW + i * tile
            moved = dot(place, rtr[:, i * tile:(i + 1) * tile]).astype(BF)
            mix[:, at:at + tile] = jnp.where(g_col >= 0, moved, tok[:, at:at + tile])
    out_mixed = pltpu.make_async_copy(mix, mixed_hbm, local_sem.at[17])
    out_mixed.start()

    own_q0.wait()
    drain(q0r.at[pl.ds(0, T - 1)], recv_sem.at[23])
    own_rq.wait()
    drain(rq.at[pl.ds(0, T - 1)], recv_sem.at[22])
    routed = rq[...].reshape(ROUTED, HEAD)
    g_lane = (jl % 16) * T + jl // 16

    def place_owner(o, carry):
        slots = tabs[pl.ds(o, 1)][0, :1]
        lo = offs[aligned(o, 8), :][:1]
        col = column_of(jnp.where(slots >= 0, slots + lo, -1))
        moved = dot(one_hot(col == g_lane), routed).astype(BF)
        plain = q0r[pl.ds(o, 1)][0]
        qo[aligned(o, ROWS), :] = jnp.where(col >= 0, moved, plain)
        return carry

    lax.fori_loop(0, T, place_owner, 0)
    out_query = pltpu.make_async_copy(qo, query_hbm, local_sem.at[18])
    out_query.start()

    drain(tabs.at[pl.ds(0, T - 1)], send_sem.at[0])
    drain(n0.at[pl.ds(0, DP - 1)], send_sem.at[1])
    drain(a2s.at[pl.ds(0, (T - 1) * 16), :], send_sem.at[2])
    drain(wga.at[pl.ds(0, NY - 1)], send_sem.at[3])
    drain(wqb.at[:, pl.ds(0, 3 * HEAD)], send_sem.at[4])
    drain(wqa.at[:, pl.ds(0, 3 * HEAD)], send_sem.at[5])
    drain(wda.at[pl.ds(0, NY - 1)], send_sem.at[6])
    drain(ns.at[pl.ds(0, DP - 1)], send_sem.at[7])
    drain(rws.at[pl.ds(0, DP - 1)], send_sem.at[8])
    drain(gx.at[pl.ds(0, NZ - 1)], send_sem.at[9])
    drain(wqa.at[:, pl.ds(0, 3 * NY * HEAD)], send_sem.at[10])
    drain(wqb.at[:, pl.ds(0, 3 * NZ * HEAD)], send_sem.at[11])
    drain(gc, send_sem.at[12])
    drain(gs.at[pl.ds(0, NX - 1)], send_sem.at[13])
    drain(hid.at[0, pl.ds(0, NX - 1)], send_sem.at[14])
    drain(hid.at[0], send_sem.at[15])
    drain(dn.at[pl.ds(0, NZ - 1)], send_sem.at[16])
    drain(pc, send_sem.at[17])
    drain(ps.at[pl.ds(0, NX - 1)], send_sem.at[18])
    drain(ms.at[pl.ds(0, DP - 1)], send_sem.at[19])
    drain(rp.at[pl.ds(0, DP - 1)], send_sem.at[20])
    drain(rts.at[pl.ds(0, (T - 1) * 16), :], send_sem.at[21])
    drain(rqs.at[pl.ds(0, T - 1)], send_sem.at[22])
    drain(q0s.at[pl.ds(0, T - 1)], send_sem.at[23])
    out_mixed.wait()
    out_query.wait()


def on_device(tokens, route_order, route_counts, w_router, gain_in, w_gate_up, w_down, gain_next, w_query):
    vmem = pl.BlockSpec(memory_space=pltpu.VMEM)
    anywhere = pl.BlockSpec(memory_space=pl.ANY)
    return pl.pallas_call(
        kernel,
        out_shape=(
            jax.ShapeDtypeStruct((ROWS, D), BF),
            jax.ShapeDtypeStruct((T * ROWS, HEAD), BF),
        ),
        in_specs=[vmem, pl.BlockSpec(memory_space=pltpu.SMEM), vmem, vmem, vmem] + [anywhere] * 4,
        out_specs=(anywhere, anywhere),
        scratch_shapes=[
            pltpu.VMEM((ROWS, D), BF),
            pltpu.VMEM((T, 8, ROWS), I32),
            pltpu.VMEM((ROWS, ROWS), I32),
            pltpu.VMEM((DP, ROWS, KE), BF),
            pltpu.VMEM((DP, ROWS, KE), BF),
            pltpu.VMEM((NY, KE, 2 * UNITS), BF),
            pltpu.VMEM((NY, UNITS, KE), BF),
            pltpu.VMEM((HALF, T * HEAD), BF),
            pltpu.VMEM((HALF, T * HEAD), BF),
            pltpu.VMEM((ROUTED, CW), BF),
            pltpu.VMEM((ROUTED, CW), BF),
            pltpu.VMEM((QN * BAL, CW), F32),
            pltpu.VMEM((DP, BAL, KE), BF),
            pltpu.VMEM((NZ, DP, BAL, KE), BF),
            pltpu.VMEM((DP, BAL, KE + 128), BF),
            pltpu.VMEM((DP, BAL, KE + 128), BF),
            pltpu.VMEM((NC, NX, NZ * LINE // DP, NY * 2 * UNITS), F32),
            pltpu.VMEM((NX, NZ * LINE // DP, NY * 2 * UNITS), F32),
            pltpu.VMEM((NX, NZ * LINE // DP, NY * 2 * UNITS), BF),
            pltpu.VMEM((NX, NZ * LINE // DP, NY * 2 * UNITS), BF),
            pltpu.VMEM((NC, NX, NZ * LINE // DP, NY * UNITS), BF),
            pltpu.VMEM((NZ, LINE, KE), BF),
            pltpu.VMEM((NZ, LINE, KE), BF),
            pltpu.VMEM((NC, NX, ROWS, T * HEAD), BF),
            pltpu.VMEM((NX, ROWS, T * HEAD), BF),
            pltpu.VMEM((NX, ROWS, T * HEAD), BF),
            pltpu.VMEM((NX, ROWS, T * HEAD), BF),
            pltpu.VMEM((T, ROWS, HEAD), BF),
            pltpu.VMEM((T, ROWS, HEAD), BF),
            pltpu.VMEM((DP, BAL, KE), BF),
            pltpu.VMEM((DP, BAL, KE), BF),
            pltpu.VMEM((DP, BAL, T * HEAD), BF),
            pltpu.VMEM((DP, BAL, T * HEAD), BF),
            pltpu.VMEM((T, BAL, HEAD), BF),
            pltpu.VMEM((T, BAL, HEAD), BF),
            pltpu.VMEM((ROUTED, CW), BF),
            pltpu.VMEM((ROUTED, CW), BF),
            pltpu.VMEM((ROWS, D), BF),
            pltpu.VMEM((T * ROWS, HEAD), BF),
            pltpu.SemaphoreType.DMA((19,)),
            pltpu.SemaphoreType.DMA((24,)),
            pltpu.SemaphoreType.DMA((24,)),
        ],
        compiler_params=pltpu.CompilerParams(
            collective_id=0, has_side_effects=True, vmem_limit_bytes=60 * 1024 * 1024
        ),
    )(
        route_order, route_counts, w_router.reshape(1, D), gain_in.reshape(1, D), gain_next.reshape(1, D),
        tokens, w_gate_up, w_down, w_query,
    )


def solution(mesh):
    in_specs = (
        P(("dp", "tensor"), None),
        P(("dp", "tensor"), None),
        P(("dp", "tensor")),
        P(),
        P(),
        P(None, "tensor"),
        P("tensor", None),
        P(),
        P(None, "tensor"),
    )
    out_specs = (P(("dp", "tensor"), None), P("dp", "tensor"))
    return jax.shard_map(
        on_device, mesh=mesh, in_specs=in_specs, out_specs=out_specs, check_vma=False
    )
```

```python
import jax
import jax.numpy as jnp
from jax import lax
from jax.experimental import pallas as pl
from jax.experimental.pallas import tpu as pltpu
from jax.sharding import PartitionSpec as P

T = 16
DP = 8
D = 8192
ROWS = 128
HEAD = 128
UNITS = 128
QN = 4
CW = D // QN
KE = D // DP
ROUTED = 256
BAL = ROUTED // T
NZ = 4
NY = 4
NX = 4
NC = 2
LINE = DP * BAL
ZC = NY * HEAD
BLK = NZ * LINE // DP
EPS = 1e-05
MESH = pl.DeviceIdType.MESH
BF = jnp.bfloat16
F32 = jnp.float32
I32 = jnp.int32


def start(source, target, axis, peer, send_sem, recv_sem):
    pltpu.make_async_remote_copy(
        src_ref=source,
        dst_ref=target,
        send_sem=send_sem,
        recv_sem=recv_sem,
        device_id={axis: peer},
        device_id_type=MESH,
    ).start()


def spread(axis, size, me, source, target, send_sem, recv_sem):
    def body(k, carry):
        peer = lax.rem(me + k, size)
        start(source(peer), target, axis, peer, send_sem, recv_sem)
        return carry

    lax.fori_loop(1, size, body, 0)


def drain(view, sem):
    pltpu.make_async_copy(view, view, sem).wait()


def iota(shape, dim):
    return lax.broadcasted_iota(I32, shape, dim)


def dot(a, b):
    return jnp.dot(a, b, preferred_element_type=F32)


def one_hot(mask):
    return jnp.where(mask, 1.0, 0.0).astype(BF)


def aligned(at, size):
    return pl.ds(pl.multiple_of(at * size, size), size)


def column_of(row):
    eye = iota((ROWS, ROWS), 0) == iota((ROWS, ROWS), 1)
    return jnp.sum(jnp.where(eye, row.astype(F32), 0.0), axis=1, keepdims=True).astype(I32)


def kernel(
    order_ref, count_ref, wr_ref, gin_ref, gnx_ref, tok_hbm, wgu_hbm, wd_hbm, wq_hbm,
    mixed_hbm, query_hbm,
    tok, tabs, offs, n0, xr, wga, wda, wqg, a2s, a2r, xb, ns, gx, rws, rwr,
    gp, gc, gs, gr, hid, dn, dr, pq, pc, ps, qr, q0s, q0r, ms, mb, rp, rpr, rqs, rq,
    rts, rtr, mix, qo, spots, spot_m, back,
    local_sem, send_sem, recv_sem, pc_send, pc_recv, qr_send, qr_recv, out_sem,
):
    t = lax.axis_index("tensor")
    d = lax.axis_index("dp")
    z, y = lax.div(t, NY), lax.rem(t, NY)
    x, c = lax.div(d, NC), lax.rem(d, NC)
    sibling = x * NC + 1 - c
    near = (1, 3, 2)
    tile = 512
    per = CW // KE

    def at_y(k):
        return lax.rem(y + k, NY)

    def at_z(k):
        return lax.rem(z + k, NZ)

    def at_x(k):
        return lax.rem(x + k, NX)

    my_k = aligned(d, KE)
    wq_own = wq_hbm.at[my_k, :]
    load_tok = pltpu.make_async_copy(tok_hbm, tok, local_sem.at[0])
    load_tok.start()
    own_wg = pltpu.make_async_copy(wgu_hbm.at[my_k, :], wga.at[y], local_sem.at[1])
    own_wg.start()
    own_wd = pltpu.make_async_copy(wd_hbm.at[:, my_k], wda.at[y], local_sem.at[2])
    own_wd.start()
    own_wq = pltpu.make_async_copy(wq_own, wqg.at[:, aligned(t, HEAD)], local_sem.at[3])
    own_wq.start()

    barrier = pltpu.get_barrier_semaphore()

    def greet_t(k, carry):
        pl.semaphore_signal(barrier, inc=1, device_id={"tensor": lax.rem(t + k, T)}, device_id_type=MESH)
        return carry

    def greet_d(k, carry):
        pl.semaphore_signal(barrier, inc=1, device_id={"dp": lax.rem(d + k, DP)}, device_id_type=MESH)
        return carry

    lax.fori_loop(1, T, greet_t, 0)
    lax.fori_loop(1, DP, greet_d, 0)

    count = count_ref[0]
    slot = iota((8, ROWS), 1)
    values = jnp.where(slot < count, slot + 1, 0).astype(F32).astype(BF)
    pairs = one_hot(iota((ROWS, ROWS), 0) == order_ref[...])
    own = lax.dot_general(values, pairs, (((1,), (1,)), ((), ())), preferred_element_type=F32)
    tabs[pl.ds(t, 1)] = (own.astype(I32) - 1)[None]
    pl.semaphore_wait(barrier, T - 1 + DP - 1)
    spread("tensor", T, t, lambda peer: tabs.at[t], tabs.at[t], send_sem.at[0], recv_sem.at[0])

    start(wq_own, wqg.at[:, aligned(t, HEAD)], "tensor", at_z(2) * NY + y, send_sem.at[1], recv_sem.at[1])
    for k in near:
        start(wq_own, wqg.at[:, aligned(t, HEAD)], "tensor", z * NY + at_y(k), send_sem.at[2], recv_sem.at[2])

    load_tok.wait()
    square = jnp.zeros((ROWS, 1), F32)
    for e in range(DP):
        wide = tok[:, e * KE:(e + 1) * KE].astype(F32)
        square += jnp.sum(wide * wide, axis=1, keepdims=True)
    scale = lax.rsqrt(square / D + EPS)
    for e in range(DP):
        cols = slice(e * KE, (e + 1) * KE)
        n0[e] = (tok[:, cols].astype(F32) * scale * gnx_ref[:, cols]).astype(BF)
    my_n0 = xr.at[c, x]
    for k in (1, 3):
        for i in range(NC):
            peer = at_x(k) * NC + i
            start(n0.at[peer], my_n0, "dp", peer, send_sem.at[3], recv_sem.at[3])
    start(n0.at[sibling], my_n0, "dp", sibling, send_sem.at[3], recv_sem.at[3])
    own_n0 = pltpu.make_async_copy(n0.at[d], my_n0, local_sem.at[4])
    own_n0.start()
    for i in range(NC):
        peer = at_x(2) * NC + i
        start(n0.at[peer], my_n0, "dp", peer, send_sem.at[3], recv_sem.at[3])
    drain(tabs.at[pl.ds(0, T - 1)], recv_sem.at[0])
    marks = one_hot(tabs[...].reshape(T * 8, ROWS) >= 0)
    counts = dot(marks, jnp.ones((ROWS, ROWS), BF))
    sub, lane = iota((ROWS, ROWS), 0), iota((ROWS, ROWS), 1)
    before = one_hot(((lane // 8) < (sub // 8)) & (lane % 8 == 0))
    firsts = dot(before, counts.astype(BF))
    firsts_i, counts_i = firsts.astype(I32), counts.astype(I32)
    offs[...] = firsts_i

    my_first = offs[aligned(t, 8), :][:1]
    my_slots = tabs[pl.ds(t, 1)][0, :1]
    g_row = jnp.where(my_slots >= 0, my_slots + my_first, -1)
    j = iota((ROUTED, ROWS), 0)
    hit = ((j // 16) == (g_row % 16)) & ((j % 4) == ((g_row // 16) % 4)) & (g_row >= 0)
    pick = jnp.concatenate([one_hot(hit & (((j // 4) % 4) == q)) for q in range(QN)], axis=1)
    for i in range(CW // tile):
        stacked = jnp.concatenate([tok[:, q * CW + i * tile:q * CW + (i + 1) * tile] for q in range(QN)], axis=0)
        a2s[:, i * tile:(i + 1) * tile] = dot(pick, stacked).astype(BF)
    spread("tensor", T, t, lambda peer: a2s.at[aligned(peer, 16), :], a2r.at[aligned(t, 16), :], send_sem.at[4], recv_sem.at[4])
    a2r[aligned(t, 16), :] = a2s[aligned(t, 16), :]

    own_wg.wait()
    for k in near:
        start(wga.at[y], wga.at[y], "tensor", z * NY + at_y(k), send_sem.at[5], recv_sem.at[5])

    first_l, last_l = [], []
    for half in range(2):
        group = iota((8, ROWS), 1) // 16
        lo, hi = jnp.zeros((8, ROWS), I32), jnp.zeros((8, ROWS), I32)
        for i in range(8):
            o = half * 8 + i
            f = firsts_i[o * 8:(o + 1) * 8]
            n = counts_i[o * 8:(o + 1) * 8]
            lo = jnp.where(group == i, f, lo)
            hi = jnp.where(group == i, f + n, hi)
        first_l.append(lo)
        last_l.append(hi)
    first_l = jnp.concatenate(first_l, axis=1)[:1]
    last_l = jnp.concatenate(last_l, axis=1)[:1]
    bi, bj = iota((QN * BAL, ROUTED), 0), iota((QN * BAL, ROUTED), 1)
    g_bal = (bi % BAL) * T + t
    compact = one_hot(
        ((bi // BAL) == ((bj // 4) % 4)) & ((bj % 4) == (bi % 4)) & (first_l <= g_bal) & (g_bal < last_l)
    )
    ri, rj = iota((16, QN * BAL), 0), iota((16, QN * BAL), 1)
    g_bal = (rj % BAL) * T + t
    fits = ((rj // BAL) == (ri // 4)) & ((rj % 4) == (ri % 4))
    for o in range(T):
        lo = jnp.concatenate([firsts_i[o * 8:(o + 1) * 8, :QN * BAL]] * 2, axis=0)
        n = jnp.concatenate([counts_i[o * 8:(o + 1) * 8, :QN * BAL]] * 2, axis=0)
        back[o * 16:(o + 1) * 16, :] = one_hot(fits & (lo <= g_bal) & (g_bal < lo + n))
    g_col = column_of(g_row)
    jl = iota((ROWS, ROUTED), 1)
    hit = ((jl // 16) == (g_col % 16)) & ((jl % 4) == ((g_col // 16) % 4)) & (g_col >= 0)
    for q in range(QN):
        spot_m[q] = one_hot(hit & (((jl // 4) % 4) == q))
    g_lane = (jl % 16) * T + jl // 16

    def find_owner(o, carry):
        slots = tabs[pl.ds(o, 1)][0, :1]
        lo = offs[aligned(o, 8), :][:1]
        col = column_of(jnp.where(slots >= 0, slots + lo, -1))
        spots[pl.ds(o, 1)] = one_hot(col == g_lane)[None]
        return carry

    lax.fori_loop(0, T, find_owner, 0)

    drain(a2r.at[pl.ds(0, (T - 1) * 16), :], recv_sem.at[4])
    square, logit = jnp.zeros((BAL, 1), F32), jnp.zeros((BAL, 1), F32)
    xb[...] = dot(compact, a2r[...])
    for q in range(QN):
        rows = xb[q * BAL:(q + 1) * BAL]
        square += jnp.sum(rows * rows, axis=1, keepdims=True)
    scale = lax.rsqrt(square / D + EPS)
    for q in range(QN):
        rows = xb[q * BAL:(q + 1) * BAL] * scale * gin_ref[:, q * CW:(q + 1) * CW]
        for h in range(per):
            ns[q * per + h] = rows[:, h * KE:(h + 1) * KE].astype(BF)
    my_rows = gx.at[z, d]
    spread("dp", DP, d, lambda peer: ns.at[peer], my_rows, send_sem.at[6], recv_sem.at[6])
    gx[pl.ds(z, 1), pl.ds(d, 1)] = ns[pl.ds(d, 1)][None]

    own_wq.wait()
    drain(wqg.at[:, pl.ds(0, 3 * HEAD)], recv_sem.at[2])

    def send_piece(i):
        piece = wqg.at[i * (KE // 4):(i + 1) * (KE // 4), aligned(z, ZC)]
        for k in (1, 3):
            start(piece, piece, "tensor", at_z(k) * NY + y, send_sem.at[7], recv_sem.at[7 if k == 3 else 8])

    send_piece(0)
    for q in range(QN):
        rows = xb[q * BAL:(q + 1) * BAL]
        logit += jnp.sum(rows * wr_ref[:, q * CW:(q + 1) * CW].astype(F32), axis=1, keepdims=True)
        for h in range(per):
            rws[q * per + h, :, :KE] = rows[:, h * KE:(h + 1) * KE].astype(BF)
    weight = 1.0 / (1.0 + jnp.exp(-logit))
    upper = weight.astype(BF)
    lower = (weight - upper.astype(F32)).astype(BF)
    pair = jnp.where(iota((BAL, 128), 1) == 0, upper.astype(F32), lower.astype(F32)).astype(BF)
    for e in range(DP):
        rws[e, :, KE:] = pair
    rwr[pl.ds(d, 1)] = rws[pl.ds(d, 1)]

    drain(gx.at[0, pl.ds(0, DP - 1)], recv_sem.at[6])
    for k in near:
        start(gx.at[z], gx.at[z], "tensor", at_z(k) * NY + y, send_sem.at[9], recv_sem.at[9])
    for i in range(1, 4):
        send_piece(i)
    own_wd.wait()
    for k in near:
        start(wda.at[y], wda.at[y], "tensor", z * NY + at_y(k), send_sem.at[10], recv_sem.at[10])
    drain(wqg.at[:, pl.ds(0, HEAD)], recv_sem.at[1])
    far_head = wqg.at[:, aligned(at_z(2) * NY + y, HEAD)]
    for k in near:
        start(far_head, far_head, "tensor", z * NY + at_y(k), send_sem.at[11], recv_sem.at[11])
    spread("dp", DP, d, lambda peer: rws.at[peer], rwr.at[d], send_sem.at[12], recv_sem.at[12])

    def chunk_product(k):
        rows = xr[...].reshape(DP * ROWS, KE)
        for i in range(2):
            cols = pl.ds(pl.multiple_of(at_z(k) * ZC + i * (ZC // 2), ZC // 2), ZC // 2)
            product = dot(rows, wqg[:, cols]).astype(BF)
            pq[k, :, :, :, i * (ZC // 2):(i + 1) * (ZC // 2)] = product.reshape(NC, NX, ROWS, ZC // 2)
        start(pq.at[k, 1 - c], pc.at[k], "dp", sibling, pc_send.at[k], pc_recv.at[k])

    def chunk_pair(k):
        drain(pc.at[k], pc_recv.at[k])
        for i in range(NX):
            ps[k, i] = (pq[k, c, i].astype(F32) + pc[k, i].astype(F32)).astype(BF)
        for i in near:
            start(ps.at[k, at_x(i)], qr.at[k, i - 1], "dp", at_x(i) * NC + c, qr_send.at[k], qr_recv.at[k])

    def chunk_sum(k):
        drain(qr.at[k], qr_recv.at[k])
        total = ps[k, pl.ds(x, 1)][0].astype(F32)
        for i in range(NX - 1):
            total += qr[k, i].astype(F32)
        total = jnp.where(g_col >= 0, 0.0, total).astype(BF)
        for i in range(NY):
            q0s[k, i] = total[:, i * HEAD:(i + 1) * HEAD]
        for i in range(NY):
            if k > 0 or i > 0:
                start(q0s.at[k, at_y(i)], q0r.at[t], "tensor", at_z(k) * NY + at_y(i), send_sem.at[13], recv_sem.at[13])
        if k == 0:
            q0r[pl.ds(t, 1)] = q0s[0, pl.ds(y, 1)]

    own_n0.wait()
    drain(n0.at[pl.ds(0, DP - 1)], recv_sem.at[3])
    chunk_product(0)
    chunk_pair(0)

    drain(wga.at[pl.ds(0, NY - 1)], recv_sem.at[5])
    drain(gx.at[pl.ds(0, NZ - 1)], recv_sem.at[9])
    rows = gx[...].reshape(NZ * LINE, KE)
    for i in range(NY):
        gp[:, :, :, i * 2 * UNITS:(i + 1) * 2 * UNITS] = dot(rows, wga[i]).reshape(NC, NX, BLK, 2 * UNITS)
    start(gp.at[1 - c], gc, "dp", sibling, send_sem.at[14], recv_sem.at[14])
    drain(gc, recv_sem.at[14])
    for i in range(NX):
        gs[i] = (gp[c, i] + gc[i]).astype(BF)
    for k in near:
        start(gs.at[at_x(k)], gr.at[k - 1], "dp", at_x(k) * NC + c, send_sem.at[15], recv_sem.at[15])
    drain(gr, recv_sem.at[15])
    total = gp[pl.ds(c, 1), pl.ds(x, 1)][0, 0] + gc[pl.ds(x, 1)][0]
    for i in range(NX - 1):
        total += gr[i].astype(F32)
    for i in range(NY):
        gate = total[:, i * 2 * UNITS:i * 2 * UNITS + UNITS]
        up = total[:, i * 2 * UNITS + UNITS:(i + 1) * 2 * UNITS]
        hid[c, pl.ds(x, 1), :, i * UNITS:(i + 1) * UNITS] = (gate / (1.0 + jnp.exp(-gate)) * up).astype(BF)[None]
    for k in near:
        start(hid.at[c, x], hid.at[c, x], "dp", at_x(k) * NC + c, send_sem.at[16], recv_sem.at[16])
    drain(hid.at[0, pl.ds(0, NX - 1)], recv_sem.at[16])
    start(hid.at[c], hid.at[c], "dp", sibling, send_sem.at[17], recv_sem.at[17])

    drain(wda.at[pl.ds(0, NY - 1)], recv_sem.at[10])
    drain(hid.at[0], recv_sem.at[17])
    hidden = hid[...].reshape(NZ * LINE, NY * UNITS)
    down = wda[...].reshape(NY * UNITS, KE)
    for i in range(KE // 256):
        cols = slice(i * 256, (i + 1) * 256)
        dn[:, :, cols] = dot(hidden, down[:, cols]).astype(BF).reshape(NZ, LINE, 256)
    for k in near:
        start(dn.at[at_z(k)], dr.at[k - 1], "tensor", at_z(k) * NY + y, send_sem.at[18], recv_sem.at[18])
    drain(wqg.at[:, pl.ds(0, ZC)], recv_sem.at[7])
    chunk_product(1)
    drain(wqg.at[:, pl.ds(0, ZC)], recv_sem.at[8])
    chunk_product(3)
    chunk_pair(1)
    chunk_sum(0)
    chunk_pair(3)
    drain(rwr.at[pl.ds(0, DP - 1)], recv_sem.at[12])
    drain(dr, recv_sem.at[18])
    branch = dn[pl.ds(z, 1)][0].astype(F32)
    for i in range(NZ - 1):
        branch += dr[i].astype(F32)
    raw = rwr[...].reshape(LINE, KE + 128)
    both = raw[:, KE:].astype(F32)
    weight = both[:, :1] + both[:, 1:2]
    rows = (raw[:, :KE].astype(F32) + weight * branch).astype(BF)
    ms[...] = rows.reshape(DP, BAL, KE)
    spread("dp", DP, d, lambda peer: ms.at[peer], mb.at[d], send_sem.at[19], recv_sem.at[19])
    mb[pl.ds(d, 1)] = ms[pl.ds(d, 1)]
    rows = (rows.astype(F32) * gnx_ref[:, my_k]).astype(BF)
    drain(wqg.at[:, pl.ds(0, 3 * HEAD)], recv_sem.at[11])
    for i in range(T // 2):
        cols = slice(i * 2 * HEAD, (i + 1) * 2 * HEAD)
        rp[:, :, cols] = dot(rows, wqg[:, cols]).astype(BF).reshape(DP, BAL, 2 * HEAD)
    spread("dp", DP, d, lambda peer: rp.at[peer], rpr.at[d], send_sem.at[20], recv_sem.at[20])
    rpr[pl.ds(d, 1)] = rp[pl.ds(d, 1)]
    chunk_product(2)
    chunk_pair(2)
    chunk_sum(1)
    drain(mb.at[pl.ds(0, DP - 1)], recv_sem.at[19])
    square = jnp.zeros((BAL, 1), F32)
    for e in range(DP):
        wide = mb[e].astype(F32)
        square += jnp.sum(wide * wide, axis=1, keepdims=True)
    scale = lax.rsqrt(square / D + EPS)
    for h in range(per):
        stacked = jnp.concatenate([mb[q * per + h] for q in range(QN)], axis=0)
        for i in range(KE // tile):
            at = h * KE + i * tile
            rts[:, at:at + tile] = dot(back[...], stacked[:, i * tile:(i + 1) * tile]).astype(BF)
    spread("tensor", T, t, lambda peer: rts.at[aligned(peer, 16), :], rtr.at[aligned(t, 16), :], send_sem.at[21], recv_sem.at[21])
    rtr[aligned(t, 16), :] = rts[aligned(t, 16), :]

    drain(rpr.at[pl.ds(0, DP - 1)], recv_sem.at[20])
    total = rpr[0].astype(F32)
    for e in range(1, DP):
        total += rpr[e].astype(F32)
    total = (total * scale).astype(BF)
    for h in range(T):
        rqs[h] = total[:, h * HEAD:(h + 1) * HEAD]
    spread("tensor", T, t, lambda peer: rqs.at[peer], rq.at[t], send_sem.at[22], recv_sem.at[23])
    rq[pl.ds(t, 1)] = rqs[pl.ds(t, 1)]
    chunk_sum(3)
    chunk_sum(2)
    drain(rtr.at[pl.ds(0, (T - 1) * 16), :], recv_sem.at[21])
    outs = []
    for q in range(QN):
        for i in range(CW // tile):
            at = q * CW + i * tile
            moved = dot(spot_m[q], rtr[:, i * tile:(i + 1) * tile]).astype(BF)
            mix[:, at:at + tile] = jnp.where(g_col >= 0, moved, tok[:, at:at + tile])
        cols = pl.ds(q * CW, CW)
        copy = pltpu.make_async_copy(mix.at[:, cols], mixed_hbm.at[:, cols], out_sem.at[q])
        copy.start()
        outs.append(copy)

    drain(q0r.at[pl.ds(0, T - 1)], recv_sem.at[13])
    drain(rq.at[pl.ds(0, T - 1)], recv_sem.at[23])
    routed = rq[...].reshape(ROUTED, HEAD)

    def place_owner(o, carry):
        moved = dot(spots[pl.ds(o, 1)][0], routed)
        plain = q0r[pl.ds(o, 1)][0].astype(F32)
        qo[aligned(o, ROWS), :] = (moved + plain).astype(BF)
        return carry

    lax.fori_loop(0, T, place_owner, 0, unroll=4)
    out_query = pltpu.make_async_copy(qo, query_hbm, out_sem.at[QN])
    out_query.start()

    drain(tabs.at[pl.ds(0, T - 1)], send_sem.at[0])
    drain(wqg.at[:, pl.ds(0, HEAD)], send_sem.at[1])
    drain(wqg.at[:, pl.ds(0, 3 * HEAD)], send_sem.at[2])
    drain(n0.at[pl.ds(0, DP - 1)], send_sem.at[3])
    drain(a2s.at[pl.ds(0, (T - 1) * 16), :], send_sem.at[4])
    drain(wga.at[pl.ds(0, NY - 1)], send_sem.at[5])
    drain(ns.at[pl.ds(0, DP - 1)], send_sem.at[6])
    drain(wqg.at[:, pl.ds(0, 2 * ZC)], send_sem.at[7])
    drain(rqs.at[pl.ds(0, T - 1)], send_sem.at[22])
    drain(gx.at[pl.ds(0, NZ - 1)], send_sem.at[9])
    drain(wda.at[pl.ds(0, NY - 1)], send_sem.at[10])
    drain(wqg.at[:, pl.ds(0, 3 * HEAD)], send_sem.at[11])
    drain(rws.at[pl.ds(0, DP - 1)], send_sem.at[12])
    drain(q0r.at[pl.ds(0, T - 1)], send_sem.at[13])
    drain(gc, send_sem.at[14])
    drain(gr, send_sem.at[15])
    drain(hid.at[0, pl.ds(0, NX - 1)], send_sem.at[16])
    drain(hid.at[0], send_sem.at[17])
    drain(dr, send_sem.at[18])
    drain(ms.at[pl.ds(0, DP - 1)], send_sem.at[19])
    drain(rp.at[pl.ds(0, DP - 1)], send_sem.at[20])
    drain(rts.at[pl.ds(0, (T - 1) * 16), :], send_sem.at[21])
    for k in range(NZ):
        drain(pc.at[k], pc_send.at[k])
        drain(qr.at[k], qr_send.at[k])
    for copy in outs:
        copy.wait()
    out_query.wait()


def on_device(tokens, route_order, route_counts, w_router, gain_in, w_gate_up, w_down, gain_next, w_query):
    vmem = pl.BlockSpec(memory_space=pltpu.VMEM)
    anywhere = pl.BlockSpec(memory_space=pl.ANY)
    return pl.pallas_call(
        kernel,
        out_shape=(
            jax.ShapeDtypeStruct((ROWS, D), BF),
            jax.ShapeDtypeStruct((T * ROWS, HEAD), BF),
        ),
        in_specs=[vmem, pl.BlockSpec(memory_space=pltpu.SMEM), vmem, vmem, vmem] + [anywhere] * 4,
        out_specs=(anywhere, anywhere),
        scratch_shapes=[
            pltpu.VMEM((ROWS, D), BF),
            pltpu.VMEM((T, 8, ROWS), I32),
            pltpu.VMEM((ROWS, ROWS), I32),
            pltpu.VMEM((DP, ROWS, KE), BF),
            pltpu.VMEM((NC, NX, ROWS, KE), BF),
            pltpu.VMEM((NY, KE, 2 * UNITS), BF),
            pltpu.VMEM((NY, UNITS, KE), BF),
            pltpu.VMEM((KE, T * HEAD), BF),
            pltpu.VMEM((ROUTED, CW), BF),
            pltpu.VMEM((ROUTED, CW), BF),
            pltpu.VMEM((QN * BAL, CW), F32),
            pltpu.VMEM((DP, BAL, KE), BF),
            pltpu.VMEM((NZ, DP, BAL, KE), BF),
            pltpu.VMEM((DP, BAL, KE + 128), BF),
            pltpu.VMEM((DP, BAL, KE + 128), BF),
            pltpu.VMEM((NC, NX, BLK, NY * 2 * UNITS), F32),
            pltpu.VMEM((NX, BLK, NY * 2 * UNITS), F32),
            pltpu.VMEM((NX, BLK, NY * 2 * UNITS), BF),
            pltpu.VMEM((NX - 1, BLK, NY * 2 * UNITS), BF),
            pltpu.VMEM((NC, NX, BLK, NY * UNITS), BF),
            pltpu.VMEM((NZ, LINE, KE), BF),
            pltpu.VMEM((NZ - 1, LINE, KE), BF),
            pltpu.VMEM((NZ, NC, NX, ROWS, ZC), BF),
            pltpu.VMEM((NZ, NX, ROWS, ZC), BF),
            pltpu.VMEM((NZ, NX, ROWS, ZC), BF),
            pltpu.VMEM((NZ, NX - 1, ROWS, ZC), BF),
            pltpu.VMEM((NZ, NY, ROWS, HEAD), BF),
            pltpu.VMEM((T, ROWS, HEAD), BF),
            pltpu.VMEM((DP, BAL, KE), BF),
            pltpu.VMEM((DP, BAL, KE), BF),
            pltpu.VMEM((DP, BAL, T * HEAD), BF),
            pltpu.VMEM((DP, BAL, T * HEAD), BF),
            pltpu.VMEM((T, BAL, HEAD), BF),
            pltpu.VMEM((T, BAL, HEAD), BF),
            pltpu.VMEM((ROUTED, CW), BF),
            pltpu.VMEM((ROUTED, CW), BF),
            pltpu.VMEM((ROWS, D), BF),
            pltpu.VMEM((T * ROWS, HEAD), BF),
            pltpu.VMEM((T, ROWS, ROUTED), BF),
            pltpu.VMEM((QN, ROWS, ROUTED), BF),
            pltpu.VMEM((ROUTED, QN * BAL), BF),
            pltpu.SemaphoreType.DMA((5,)),
            pltpu.SemaphoreType.DMA((24,)),
            pltpu.SemaphoreType.DMA((24,)),
            pltpu.SemaphoreType.DMA((NZ,)),
            pltpu.SemaphoreType.DMA((NZ,)),
            pltpu.SemaphoreType.DMA((NZ,)),
            pltpu.SemaphoreType.DMA((NZ,)),
            pltpu.SemaphoreType.DMA((QN + 1,)),
        ],
        compiler_params=pltpu.CompilerParams(
            collective_id=0, has_side_effects=True, vmem_limit_bytes=60 * 1024 * 1024
        ),
    )(
        route_order, route_counts, w_router.reshape(1, D), gain_in.reshape(1, D), gain_next.reshape(1, D),
        tokens, w_gate_up, w_down, w_query,
    )


def solution(mesh):
    in_specs = (
        P(("dp", "tensor"), None),
        P(("dp", "tensor"), None),
        P(("dp", "tensor")),
        P(),
        P(),
        P(None, "tensor"),
        P("tensor", None),
        P(),
        P(None, "tensor"),
    )
    out_specs = (P(("dp", "tensor"), None), P("dp", "tensor"))
    return jax.shard_map(
        on_device, mesh=mesh, in_specs=in_specs, out_specs=out_specs, check_vma=False
    )
```

```python
import jax
import jax.numpy as jnp
from jax import lax
from jax.experimental import pallas as pl
from jax.experimental.pallas import tpu as pltpu
from jax.sharding import PartitionSpec as P

T = 16
DP = 8
D = 8192
ROWS = 128
HEAD = 128
UNITS = 128
QN = 4
CW = D // QN
KE = D // DP
ROUTED = 256
BAL = ROUTED // T
NZ = 4
NY = 4
NX = 4
NC = 2
LINE = DP * BAL
ZC = NY * HEAD
BLK = NZ * LINE // DP
LIMIT = 60
EPS = 1e-05
MESH = pl.DeviceIdType.MESH
BF = jnp.bfloat16
F32 = jnp.float32
I32 = jnp.int32


def start(source, target, axis, peer, send_sem, recv_sem):
    pltpu.make_async_remote_copy(
        src_ref=source,
        dst_ref=target,
        send_sem=send_sem,
        recv_sem=recv_sem,
        device_id={axis: peer},
        device_id_type=MESH,
    ).start()


def spread(axis, size, me, source, target, send_sem, recv_sem):
    def body(k, carry):
        peer = lax.rem(me + k, size)
        start(source(peer), target, axis, peer, send_sem, recv_sem)
        return carry

    lax.fori_loop(1, size, body, 0)


def drain(view, sem):
    pltpu.make_async_copy(view, view, sem).wait()


def iota(shape, dim):
    return lax.broadcasted_iota(I32, shape, dim)


def dot(a, b):
    return jnp.dot(a, b, preferred_element_type=F32)


def one_hot(mask):
    return jnp.where(mask, 1.0, 0.0).astype(BF)


def aligned(at, size):
    return pl.ds(pl.multiple_of(at * size, size), size)


def column_of(row):
    eye = iota((ROWS, ROWS), 0) == iota((ROWS, ROWS), 1)
    return jnp.sum(jnp.where(eye, row.astype(F32), 0.0), axis=1, keepdims=True).astype(I32)


def kernel(
    order_hbm, count_ref, wr_hbm, gin_hbm, gnx_hbm, tok_hbm, wgu_hbm, wd_hbm, wq_hbm,
    mixed_hbm, query_hbm,
    order_ref, wr_ref, gin_ref, gnx_ref, tok, tabs, offs, n0, xr, wga, wda, wqg, a2s, a2r, xb, gx, rws, rwr,
    gp, gc, gs, gr, hid, dn, dr, pq, pc, ps, fr, qr, q0s, q0r, ms, mb, rp, rpc, rps, rpr, rqs, rq,
    rts, rtr, mix, qo, spots, spot_m, back,
    local_sem, send_sem, recv_sem, pc_send, pc_recv, fr_send, fr_recv, qr_send, qr_recv, out_sem,
    dn_send, dn_recv, ms_send, ms_recv, rt_send, rt_recv,
):
    t = lax.axis_index("tensor")
    d = lax.axis_index("dp")
    z, y = lax.div(t, NY), lax.rem(t, NY)
    x, c = lax.div(d, NC), lax.rem(d, NC)
    sibling = x * NC + 1 - c
    near = (1, 3, 2)
    tile = 512
    per = CW // KE

    def at_y(k):
        return lax.rem(y + k, NY)

    def at_z(k):
        return lax.rem(z + k, NZ)

    def at_x(k):
        return lax.rem(x + k, NX)

    def pass_on(part, sem):
        for half, k in ((0, 1), (1, 3)):
            piece = part(at_y(4 - k), half)
            start(piece, piece, "tensor", z * NY + at_y(k), send_sem.at[sem], recv_sem.at[sem])

    my_k = aligned(d, KE)
    wq_own = wq_hbm.at[my_k, :]
    load_order = pltpu.make_async_copy(order_hbm, order_ref, local_sem.at[5])
    load_order.start()
    load_tok = pltpu.make_async_copy(tok_hbm, tok, local_sem.at[0])
    load_tok.start()
    load_gnx = pltpu.make_async_copy(gnx_hbm, gnx_ref, local_sem.at[6])
    load_gnx.start()
    load_gin = pltpu.make_async_copy(gin_hbm, gin_ref, local_sem.at[7])
    load_gin.start()
    load_wr = pltpu.make_async_copy(wr_hbm, wr_ref, local_sem.at[8])
    load_wr.start()
    own_wg = pltpu.make_async_copy(wgu_hbm.at[my_k, :], wga.at[y], local_sem.at[1])
    own_wg.start()
    own_wd = pltpu.make_async_copy(wd_hbm.at[:, my_k], wda.at[y], local_sem.at[2])
    own_wd.start()
    own_wq = pltpu.make_async_copy(wq_own, wqg.at[:, aligned(t, HEAD)], local_sem.at[3])
    own_wq.start()

    barrier = pltpu.get_barrier_semaphore()

    def greet_t(k, carry):
        pl.semaphore_signal(barrier, inc=1, device_id={"tensor": lax.rem(t + k, T)}, device_id_type=MESH)
        return carry

    def greet_d(k, carry):
        pl.semaphore_signal(barrier, inc=1, device_id={"dp": lax.rem(d + k, DP)}, device_id_type=MESH)
        return carry

    lax.fori_loop(1, T, greet_t, 0)
    lax.fori_loop(1, DP, greet_d, 0)

    count = count_ref[0]
    slot = iota((8, ROWS), 1)
    values = jnp.where(slot < count, slot + 1, 0).astype(F32).astype(BF)
    load_order.wait()
    pairs = one_hot(iota((ROWS, ROWS), 0) == order_ref[...])
    own = lax.dot_general(values, pairs, (((1,), (1,)), ((), ())), preferred_element_type=F32)
    tabs[pl.ds(t, 1)] = (own.astype(I32) - 1)[None]

    load_tok.wait()
    load_gnx.wait()
    square = jnp.zeros((ROWS, 1), F32)
    for e in range(DP):
        wide = tok[:, e * KE:(e + 1) * KE].astype(F32)
        square += jnp.sum(wide * wide, axis=1, keepdims=True)
    scale = lax.rsqrt(square / D + EPS)
    for e in range(DP):
        cols = slice(e * KE, (e + 1) * KE)
        n0[e] = (tok[:, cols].astype(F32) * scale * gnx_ref[:, cols]).astype(BF)
    pl.semaphore_wait(barrier, T - 1 + DP - 1)
    spread("tensor", T, t, lambda peer: tabs.at[t], tabs.at[t], send_sem.at[0], recv_sem.at[0])

    start(wq_own, wqg.at[:, aligned(t, HEAD)], "tensor", at_z(2) * NY + y, send_sem.at[1], recv_sem.at[1])
    for k in (1, 3):
        start(wq_own, wqg.at[:, aligned(t, HEAD)], "tensor", z * NY + at_y(k), send_sem.at[2], recv_sem.at[2])

    my_n0 = xr.at[c, x]
    for k in (1, 3):
        for i in range(NC):
            peer = at_x(k) * NC + i
            start(n0.at[peer], my_n0, "dp", peer, send_sem.at[3], recv_sem.at[3])
    start(n0.at[sibling], my_n0, "dp", sibling, send_sem.at[3], recv_sem.at[3])

    def far_n0(i):
        peer = at_x(2) * NC + i
        start(n0.at[peer], my_n0, "dp", peer, send_sem.at[3], recv_sem.at[3])

    own_n0 = pltpu.make_async_copy(n0.at[d], my_n0, local_sem.at[4])
    own_n0.start()
    far_n0(c)
    drain(tabs.at[pl.ds(0, T - 1)], recv_sem.at[0])
    marks = one_hot(tabs[...].reshape(T * 8, ROWS) >= 0)
    counts = dot(marks, jnp.ones((ROWS, ROWS), BF))
    sub, lane = iota((ROWS, ROWS), 0), iota((ROWS, ROWS), 1)
    before = one_hot(((lane // 8) < (sub // 8)) & (lane % 8 == 0))
    firsts = dot(before, counts.astype(BF))
    firsts_i, counts_i = firsts.astype(I32), counts.astype(I32)
    offs[...] = firsts_i

    my_first = offs[aligned(t, 8), :][:1]
    my_slots = tabs[pl.ds(t, 1)][0, :1]
    g_row = jnp.where(my_slots >= 0, my_slots + my_first, -1)
    j = iota((ROUTED, ROWS), 0)
    hit = ((j // 16) == (g_row % 16)) & ((j % 4) == ((g_row // 16) % 4)) & (g_row >= 0)
    pick = jnp.concatenate([one_hot(hit & (((j // 4) % 4) == q)) for q in range(QN)], axis=1)
    for i in range(CW // tile):
        stacked = jnp.concatenate([tok[:, q * CW + i * tile:q * CW + (i + 1) * tile] for q in range(QN)], axis=0)
        a2s[:, i * tile:(i + 1) * tile] = dot(pick, stacked).astype(BF)
    spread("tensor", T, t, lambda peer: a2s.at[aligned(peer, 16), :], a2r.at[aligned(t, 16), :], send_sem.at[4], recv_sem.at[4])
    a2r[aligned(t, 16), :] = a2s[aligned(t, 16), :]

    drain(wqg.at[:, pl.ds(0, 2 * HEAD)], recv_sem.at[2])
    pass_on(lambda at, half: wqg.at[half * (KE // 2):(half + 1) * (KE // 2), aligned(z * NY + at, HEAD)], 7)

    own_wg.wait()
    for k in (1, 3):
        start(wga.at[y], wga.at[y], "tensor", z * NY + at_y(k), send_sem.at[5], recv_sem.at[5])

    first_l, last_l = [], []
    for half in range(2):
        group = iota((8, ROWS), 1) // 16
        lo, hi = jnp.zeros((8, ROWS), I32), jnp.zeros((8, ROWS), I32)
        for i in range(8):
            o = half * 8 + i
            f = firsts_i[o * 8:(o + 1) * 8]
            n = counts_i[o * 8:(o + 1) * 8]
            lo = jnp.where(group == i, f, lo)
            hi = jnp.where(group == i, f + n, hi)
        first_l.append(lo)
        last_l.append(hi)
    first_l = jnp.concatenate(first_l, axis=1)[:1]
    last_l = jnp.concatenate(last_l, axis=1)[:1]
    bi, bj = iota((QN * BAL, ROUTED), 0), iota((QN * BAL, ROUTED), 1)
    g_bal = (bi % BAL) * T + t
    compact = one_hot(
        ((bi // BAL) == ((bj // 4) % 4)) & ((bj % 4) == (bi % 4)) & (first_l <= g_bal) & (g_bal < last_l)
    )
    ri, rj = iota((16, QN * BAL), 0), iota((16, QN * BAL), 1)
    g_bal = (rj % BAL) * T + t
    fits = ((rj // BAL) == (ri // 4)) & ((rj % 4) == (ri % 4))
    for o in range(T):
        lo = jnp.concatenate([firsts_i[o * 8:(o + 1) * 8, :QN * BAL]] * 2, axis=0)
        n = jnp.concatenate([counts_i[o * 8:(o + 1) * 8, :QN * BAL]] * 2, axis=0)
        back[o * 16:(o + 1) * 16, :] = one_hot(fits & (lo <= g_bal) & (g_bal < lo + n))
    g_col = column_of(g_row)
    jl = iota((ROWS, ROUTED), 1)
    hit = ((jl // 16) == (g_col % 16)) & ((jl % 4) == ((g_col // 16) % 4)) & (g_col >= 0)
    for q in range(QN):
        spot_m[q] = one_hot(hit & (((jl // 4) % 4) == q))
    g_lane = (jl % 16) * T + jl // 16

    def find_owner(o, carry):
        slots = tabs[pl.ds(o, 1)][0, :1]
        lo = offs[aligned(o, 8), :][:1]
        col = column_of(jnp.where(slots >= 0, slots + lo, -1))
        spots[pl.ds(o, 1)] = one_hot(col == g_lane)[None]
        return carry

    lax.fori_loop(0, T, find_owner, 0)

    load_gin.wait()
    load_wr.wait()
    drain(a2r.at[pl.ds(0, (T - 1) * 16), :], recv_sem.at[4])
    xb[...] = dot(compact, a2r[...])
    square, logit = jnp.zeros((BAL, 128), F32), jnp.zeros((BAL, 128), F32)
    for q in range(QN):
        rows = xb[q * BAL:(q + 1) * BAL]
        for h in range(per):
            rws[q * per + h, :, :KE] = rows[:, h * KE:(h + 1) * KE].astype(BF)
        for i in range(CW // 128):
            part = rows[:, i * 128:(i + 1) * 128]
            at = q * (CW // 128) + i
            square += part * part
            logit += part * wr_ref[at:at + 1, :].astype(F32)
    scale = lax.rsqrt(jnp.sum(square, axis=1, keepdims=True) / D + EPS)
    weight = 1.0 / (1.0 + jnp.exp(-jnp.sum(logit, axis=1, keepdims=True)))
    terms = []
    for value in (scale, weight):
        for i in range(3):
            terms.append(value.astype(BF).astype(F32))
            value = value - terms[-1]
    at = iota((BAL, 128), 1)
    tail = jnp.zeros((BAL, 128), F32)
    for i in range(6):
        tail = jnp.where(at == i, terms[i], tail)
    for e in range(DP):
        rws[e, :, KE:] = tail.astype(BF)
    spread("dp", DP, d, lambda peer: rws.at[peer], rwr.at[d], send_sem.at[12], recv_sem.at[12])
    rwr[pl.ds(d, 1)] = rws[pl.ds(d, 1)]

    own_wq.wait()
    drain(wqg.at[:, pl.ds(0, HEAD)], recv_sem.at[7])

    def send_piece(i):
        piece = wqg.at[i * (KE // 8):(i + 1) * (KE // 8), aligned(z, ZC)]
        for k in (1, 3):
            start(piece, piece, "tensor", at_z(k) * NY + y, send_sem.at[8], recv_sem.at[8 if k == 3 else 6])

    send_piece(0)

    drain(rwr.at[pl.ds(0, DP - 1)], recv_sem.at[12])
    far_n0(1 - c)
    raw = rwr[...].reshape(LINE, KE + 128)
    both = raw[:, KE:].astype(F32)
    scale = both[:, :1] + both[:, 1:2] + both[:, 2:3]
    line_weight = both[:, 3:4] + both[:, 4:5] + both[:, 5:6]
    normed = (raw[:, :KE].astype(F32) * scale * gin_ref[:, my_k]).astype(BF)
    gx[pl.ds(z, 1)] = normed.reshape(1, DP, BAL, KE)
    for k in near:
        start(gx.at[z], gx.at[z], "tensor", at_z(k) * NY + y, send_sem.at[9], recv_sem.at[9])
    send_piece(1)
    send_piece(2)
    send_piece(3)
    send_piece(4)
    send_piece(5)
    send_piece(6)
    send_piece(7)

    def chunk_product(k):
        rows = xr[...].reshape(DP * ROWS, KE)
        for i in range(2):
            cols = pl.ds(pl.multiple_of(at_z(k) * ZC + i * (ZC // 2), ZC // 2), ZC // 2)
            product = dot(rows, wqg[:, cols]).astype(BF)
            pq[k, :, :, :, i * (ZC // 2):(i + 1) * (ZC // 2)] = product.reshape(NC, NX, ROWS, ZC // 2)
        start(pq.at[k, 1 - c], pc.at[k], "dp", sibling, pc_send.at[k], pc_recv.at[k])

    def chunk_pair(k):
        drain(pc.at[k], pc_recv.at[k])
        for i in range(NX):
            ps[k, i] = (pq[k, c, i].astype(F32) + pc[k, i].astype(F32)).astype(BF)
        for half, i in ((0, 1), (1, 3)):
            part = ps.at[k, at_x(2), half * (ROWS // 2):(half + 1) * (ROWS // 2)]
            start(part, fr.at[k, half], "dp", at_x(i) * NC + c, fr_send.at[k], fr_recv.at[k])

    def chunk_pass(k):
        drain(fr.at[k], fr_recv.at[k])
        for half, i in ((0, 1), (1, 3)):
            rows = slice(half * (ROWS // 2), (half + 1) * (ROWS // 2))
            total = ps[k, pl.ds(at_x(i), 1), rows].astype(F32) + fr[k, half].astype(F32)[None]
            ps[k, pl.ds(at_x(i), 1), rows] = total.astype(BF)
        for half, i in ((0, 1), (1, 3)):
            start(ps.at[k, at_x(i)], qr.at[k, half], "dp", at_x(i) * NC + c, qr_send.at[k], qr_recv.at[k])

    def chunk_sum(k):
        drain(qr.at[k], qr_recv.at[k])
        total = ps[k, pl.ds(x, 1)][0].astype(F32)
        for i in range(2):
            total += qr[k, i].astype(F32)
        total = jnp.where(g_col >= 0, 0.0, total).astype(BF)
        for i in range(NY):
            q0s[k, i] = total[:, i * HEAD:(i + 1) * HEAD]
        for i in range(NY):
            if k > 0 or i > 0:
                start(q0s.at[k, at_y(i)], q0r.at[t], "tensor", at_z(k) * NY + at_y(i), send_sem.at[13], recv_sem.at[13])
        if k == 0:
            q0r[pl.ds(t, 1)] = q0s[0, pl.ds(y, 1)]

    drain(wga.at[pl.ds(0, 2)], recv_sem.at[5])
    pass_on(lambda at, half: wga.at[at, half * (KE // 2):(half + 1) * (KE // 2)], 23)
    own_wd.wait()
    for k in (1, 3):
        start(wda.at[y], wda.at[y], "tensor", z * NY + at_y(k), send_sem.at[10], recv_sem.at[10])
    drain(wqg.at[:, pl.ds(0, HEAD)], recv_sem.at[1])

    def send_far():
        far_head = wqg.at[:, aligned(at_z(2) * NY + y, HEAD)]
        for k in near:
            start(far_head, far_head, "tensor", z * NY + at_y(k), send_sem.at[11], recv_sem.at[11])

    def pass_wda():
        drain(wda.at[pl.ds(0, 2)], recv_sem.at[10])
        pass_on(lambda at, half: wda.at[at, half * (UNITS // 2):(half + 1) * (UNITS // 2)], 25)


    own_n0.wait()
    drain(n0.at[pl.ds(0, DP - 1)], recv_sem.at[3])
    chunk_product(0)
    chunk_pair(0)

    drain(wga.at[0], recv_sem.at[23])
    chunk_pass(0)
    drain(gx.at[pl.ds(0, NZ - 1)], recv_sem.at[9])
    rows = gx[...].reshape(NZ * LINE, KE)
    for i in range(NY):
        gp[i // 2, :, :, :, i % 2 * 2 * UNITS:(i % 2 + 1) * 2 * UNITS] = dot(rows, wga[i]).reshape(NC, NX, BLK, 2 * UNITS)
        if i % 2 == 1:
            start(gp.at[i // 2, 1 - c], gc.at[i // 2], "dp", sibling, send_sem.at[14], recv_sem.at[14])
    drain(gc, recv_sem.at[14])
    for i in range(NX):
        for h in range(2):
            gs[i, :, h * 4 * UNITS:(h + 1) * 4 * UNITS] = (gp[h, c, i] + gc[h, i]).astype(BF)
    for k in near:
        start(gs.at[at_x(k)], gr.at[k - 1], "dp", at_x(k) * NC + c, send_sem.at[15], recv_sem.at[15])
    pass_wda()
    send_far()
    drain(gr, recv_sem.at[15])
    total = jnp.concatenate([gp[h, pl.ds(c, 1), pl.ds(x, 1)][0, 0] + gc[h, pl.ds(x, 1)][0] for h in range(2)], axis=1)
    for i in range(NX - 1):
        total += gr[i].astype(F32)
    for i in range(NY):
        gate = total[:, i * 2 * UNITS:i * 2 * UNITS + UNITS]
        up = total[:, i * 2 * UNITS + UNITS:(i + 1) * 2 * UNITS]
        hid[c, pl.ds(x, 1), :, i * UNITS:(i + 1) * UNITS] = (gate / (1.0 + jnp.exp(-gate)) * up).astype(BF)[None]
    for k in near:
        start(hid.at[c, x], hid.at[c, x], "dp", at_x(k) * NC + c, send_sem.at[16], recv_sem.at[16])
    drain(hid.at[0, pl.ds(0, NX - 1)], recv_sem.at[16])
    start(hid.at[c], hid.at[c], "dp", sibling, send_sem.at[17], recv_sem.at[17])

    drain(wda.at[0], recv_sem.at[25])
    drain(hid.at[0], recv_sem.at[17])
    hidden = hid[...].reshape(NZ * LINE, NY * UNITS)
    down = wda[...].reshape(NY * UNITS, KE)
    for h in range(2):
        for i in range(tile // 256):
            at = h * tile + i * 256
            dn[h, :, :, i * 256:(i + 1) * 256] = dot(hidden, down[:, at:at + 256]).astype(BF).reshape(NZ, LINE, 256)
        for k in near:
            start(dn.at[h, at_z(k)], dr.at[h, k - 1], "tensor", at_z(k) * NY + y, dn_send.at[h], dn_recv.at[h])
    chunk_sum(0)
    drain(wqg.at[:, pl.ds(0, ZC)], recv_sem.at[8])
    chunk_product(1)
    chunk_pair(1)
    drain(wqg.at[:, pl.ds(0, ZC)], recv_sem.at[6])
    chunk_product(3)
    def mix_half(h):
        drain(dr.at[h], dn_recv.at[h])
        branch = dn[h, pl.ds(z, 1)][0].astype(F32)
        for i in range(NZ - 1):
            branch += dr[h, i].astype(F32)
        cols = slice(h * tile, (h + 1) * tile)
        mixed = (raw[:, cols].astype(F32) + line_weight * branch).astype(BF)
        ms[h] = mixed.reshape(DP, BAL, tile)
        spread("dp", DP, d, lambda peer: ms.at[h, peer], mb.at[h, d], ms_send.at[h], ms_recv.at[h])
        mb[h, pl.ds(d, 1)] = ms[h, pl.ds(d, 1)]
        gain = gnx_ref[:, pl.ds(pl.multiple_of(d * KE + h * tile, tile), tile)]
        return (mixed.astype(F32) * gain).astype(BF)

    def return_half(h):
        drain(mb.at[h, pl.ds(0, DP - 1)], ms_recv.at[h])
        for i in range(per):
            stacked = jnp.concatenate([mb[h, q * per + i] for q in range(QN)], axis=0)
            rts[h, :, i * tile:(i + 1) * tile] = dot(back[...], stacked).astype(BF)
        spread("tensor", T, t, lambda peer: rts.at[h, aligned(peer, 16), :], rtr.at[h, aligned(t, 16), :], rt_send.at[h], rt_recv.at[h])
        rtr[h, aligned(t, 16), :] = rts[h, aligned(t, 16), :]

    upper_rows = mix_half(0)
    chunk_pair(3)
    chunk_pass(1)
    drain(wqg.at[:, pl.ds(0, 3 * HEAD)], recv_sem.at[11])
    chunk_product(2)
    return_half(0)
    chunk_pass(3)
    rows = jnp.concatenate([upper_rows, mix_half(1)], axis=1)
    for i in range(T // 2):
        cols = slice(i * 2 * HEAD, (i + 1) * 2 * HEAD)
        product = dot(rows, wqg[:, cols]).astype(BF)
        for e in range(DP):
            rp[e % NC, e // NC, :, cols] = product[e * BAL:(e + 1) * BAL]
    start(rp.at[1 - c], rpc, "dp", sibling, send_sem.at[20], recv_sem.at[20])
    chunk_pair(2)
    drain(rpc, recv_sem.at[20])
    for i in range(NX):
        rps[i] = (rp[c, i].astype(F32) + rpc[i].astype(F32)).astype(BF)
    for k in near:
        start(rps.at[at_x(k)], rpr.at[k - 1], "dp", at_x(k) * NC + c, send_sem.at[6], recv_sem.at[24])
    chunk_sum(1)
    chunk_sum(3)
    return_half(1)
    square = jnp.zeros((BAL, 1), F32)
    for h in range(2):
        for e in range(DP):
            wide = mb[h, e].astype(F32)
            square += jnp.sum(wide * wide, axis=1, keepdims=True)
    scale = lax.rsqrt(square / D + EPS)
    chunk_pass(2)
    drain(rpr, recv_sem.at[24])
    total = rps[pl.ds(x, 1)][0].astype(F32)
    for i in range(NX - 1):
        total += rpr[i].astype(F32)
    total = (total * scale).astype(BF)
    for h in range(T):
        rqs[h] = total[:, h * HEAD:(h + 1) * HEAD]
    spread("tensor", T, t, lambda peer: rqs.at[peer], rq.at[t], send_sem.at[22], recv_sem.at[22])
    rq[pl.ds(t, 1)] = rqs[pl.ds(t, 1)]
    chunk_sum(2)
    for h in range(2):
        drain(rtr.at[h, pl.ds(0, (T - 1) * 16), :], rt_recv.at[h])
    outs = []
    for q in range(QN):
        for i in range(per):
            for h in range(2):
                at = q * CW + i * KE + h * tile
                moved = dot(spot_m[q], rtr[h, :, i * tile:(i + 1) * tile]).astype(BF)
                mix[:, at:at + tile] = jnp.where(g_col >= 0, moved, tok[:, at:at + tile])
        cols = pl.ds(q * CW, CW)
        copy = pltpu.make_async_copy(mix.at[:, cols], mixed_hbm.at[:, cols], out_sem.at[q])
        copy.start()
        outs.append(copy)

    drain(q0r.at[pl.ds(0, T - 1)], recv_sem.at[13])
    drain(rq.at[pl.ds(0, T - 1)], recv_sem.at[22])
    routed = rq[...].reshape(ROUTED, HEAD)

    def place_owner(o, carry):
        moved = dot(spots[pl.ds(o, 1)][0], routed)
        plain = q0r[pl.ds(o, 1)][0].astype(F32)
        qo[aligned(o, ROWS), :] = (moved + plain).astype(BF)
        return carry

    for i in range(NZ):
        for o in range(i * NY, (i + 1) * NY):
            place_owner(o, 0)
        rows = pl.ds(i * NY * ROWS, NY * ROWS)
        copy = pltpu.make_async_copy(qo.at[rows, :], query_hbm.at[rows, :], out_sem.at[QN + i])
        copy.start()
        outs.append(copy)

    drain(tabs.at[pl.ds(0, T - 1)], send_sem.at[0])
    drain(wqg.at[:, pl.ds(0, HEAD)], send_sem.at[1])
    drain(wqg.at[:, pl.ds(0, 2 * HEAD)], send_sem.at[2])
    drain(n0.at[pl.ds(0, DP - 1)], send_sem.at[3])
    drain(a2s.at[pl.ds(0, (T - 1) * 16), :], send_sem.at[4])
    drain(wga.at[pl.ds(0, 2)], send_sem.at[5])
    drain(wqg.at[:, pl.ds(0, HEAD)], send_sem.at[7])
    drain(wqg.at[:, pl.ds(0, 2 * ZC)], send_sem.at[8])
    drain(rqs.at[pl.ds(0, T - 1)], send_sem.at[22])
    drain(wga.at[0], send_sem.at[23])
    drain(gx.at[pl.ds(0, NZ - 1)], send_sem.at[9])
    drain(wda.at[pl.ds(0, 2)], send_sem.at[10])
    drain(wda.at[0], send_sem.at[25])
    drain(wqg.at[:, pl.ds(0, 3 * HEAD)], send_sem.at[11])
    drain(rws.at[pl.ds(0, DP - 1)], send_sem.at[12])
    drain(q0r.at[pl.ds(0, T - 1)], send_sem.at[13])
    drain(gc, send_sem.at[14])
    drain(gr, send_sem.at[15])
    drain(hid.at[0, pl.ds(0, NX - 1)], send_sem.at[16])
    drain(hid.at[0], send_sem.at[17])
    for h in range(2):
        drain(dr.at[h], dn_send.at[h])
        drain(ms.at[h, pl.ds(0, DP - 1)], ms_send.at[h])
        drain(rts.at[h, pl.ds(0, (T - 1) * 16), :], rt_send.at[h])
    drain(rpc, send_sem.at[20])
    drain(rpr, send_sem.at[6])
    for k in range(NZ):
        drain(pc.at[k], pc_send.at[k])
        drain(fr.at[k], fr_send.at[k])
        drain(qr.at[k], qr_send.at[k])
    for copy in outs:
        copy.wait()


def on_device(tokens, route_order, route_counts, w_router, gain_in, w_gate_up, w_down, gain_next, w_query):
    hbm = pl.BlockSpec(memory_space=pltpu.HBM)
    anywhere = pl.BlockSpec(memory_space=pl.ANY)
    return pl.pallas_call(
        kernel,
        out_shape=(
            jax.ShapeDtypeStruct((ROWS, D), BF),
            jax.ShapeDtypeStruct((T * ROWS, HEAD), BF),
        ),
        in_specs=[hbm, pl.BlockSpec(memory_space=pltpu.SMEM)] + [hbm] * 7,
        out_specs=(anywhere, anywhere),
        scratch_shapes=[
            pltpu.VMEM((1, ROWS), I32),
            pltpu.VMEM((D // 128, 128), BF),
            pltpu.VMEM((1, D), F32),
            pltpu.VMEM((1, D), F32),
            pltpu.VMEM((ROWS, D), BF),
            pltpu.VMEM((T, 8, ROWS), I32),
            pltpu.VMEM((ROWS, ROWS), I32),
            pltpu.VMEM((DP, ROWS, KE), BF),
            pltpu.VMEM((NC, NX, ROWS, KE), BF),
            pltpu.VMEM((NY, KE, 2 * UNITS), BF),
            pltpu.VMEM((NY, UNITS, KE), BF),
            pltpu.VMEM((KE, T * HEAD), BF),
            pltpu.VMEM((ROUTED, CW), BF),
            pltpu.VMEM((ROUTED, CW), BF),
            pltpu.VMEM((QN * BAL, CW), F32),
            pltpu.VMEM((NZ, DP, BAL, KE), BF),
            pltpu.VMEM((DP, BAL, KE + 128), BF),
            pltpu.VMEM((DP, BAL, KE + 128), BF),
            pltpu.VMEM((2, NC, NX, BLK, NY * UNITS), F32),
            pltpu.VMEM((2, NX, BLK, NY * UNITS), F32),
            pltpu.VMEM((NX, BLK, NY * 2 * UNITS), BF),
            pltpu.VMEM((NX - 1, BLK, NY * 2 * UNITS), BF),
            pltpu.VMEM((NC, NX, BLK, NY * UNITS), BF),
            pltpu.VMEM((2, NZ, LINE, KE // 2), BF),
            pltpu.VMEM((2, NZ - 1, LINE, KE // 2), BF),
            pltpu.VMEM((NZ, NC, NX, ROWS, ZC), BF),
            pltpu.VMEM((NZ, NX, ROWS, ZC), BF),
            pltpu.VMEM((NZ, NX, ROWS, ZC), BF),
            pltpu.VMEM((NZ, 2, ROWS // 2, ZC), BF),
            pltpu.VMEM((NZ, 2, ROWS, ZC), BF),
            pltpu.VMEM((NZ, NY, ROWS, HEAD), BF),
            pltpu.VMEM((T, ROWS, HEAD), BF),
            pltpu.VMEM((2, DP, BAL, KE // 2), BF),
            pltpu.VMEM((2, DP, BAL, KE // 2), BF),
            pltpu.VMEM((NC, NX, BAL, T * HEAD), BF),
            pltpu.VMEM((NX, BAL, T * HEAD), BF),
            pltpu.VMEM((NX, BAL, T * HEAD), BF),
            pltpu.VMEM((NX - 1, BAL, T * HEAD), BF),
            pltpu.VMEM((T, BAL, HEAD), BF),
            pltpu.VMEM((T, BAL, HEAD), BF),
            pltpu.VMEM((2, ROUTED, CW // 2), BF),
            pltpu.VMEM((2, ROUTED, CW // 2), BF),
            pltpu.VMEM((ROWS, D), BF),
            pltpu.VMEM((T * ROWS, HEAD), BF),
            pltpu.VMEM((T, ROWS, ROUTED), BF),
            pltpu.VMEM((QN, ROWS, ROUTED), BF),
            pltpu.VMEM((ROUTED, QN * BAL), BF),
            pltpu.SemaphoreType.DMA((9,)),
            pltpu.SemaphoreType.DMA((26,)),
            pltpu.SemaphoreType.DMA((26,)),
            pltpu.SemaphoreType.DMA((NZ,)),
            pltpu.SemaphoreType.DMA((NZ,)),
            pltpu.SemaphoreType.DMA((NZ,)),
            pltpu.SemaphoreType.DMA((NZ,)),
            pltpu.SemaphoreType.DMA((NZ,)),
            pltpu.SemaphoreType.DMA((NZ,)),
            pltpu.SemaphoreType.DMA((QN + NZ,)),
            pltpu.SemaphoreType.DMA((2,)),
            pltpu.SemaphoreType.DMA((2,)),
            pltpu.SemaphoreType.DMA((2,)),
            pltpu.SemaphoreType.DMA((2,)),
            pltpu.SemaphoreType.DMA((2,)),
            pltpu.SemaphoreType.DMA((2,)),
        ],
        compiler_params=pltpu.CompilerParams(
            collective_id=0, has_side_effects=True, vmem_limit_bytes=LIMIT * 1024 * 1024
        ),
    )(
        route_order, route_counts, w_router.reshape(D // 128, 128), gain_in.reshape(1, D), gain_next.reshape(1, D),
        tokens, w_gate_up, w_down, w_query,
    )


def solution(mesh):
    in_specs = (
        P(("dp", "tensor"), None),
        P(("dp", "tensor"), None),
        P(("dp", "tensor")),
        P(),
        P(),
        P(None, "tensor"),
        P("tensor", None),
        P(),
        P(None, "tensor"),
    )
    out_specs = (P(("dp", "tensor"), None), P("dp", "tensor"))
    return jax.shard_map(
        on_device, mesh=mesh, in_specs=in_specs, out_specs=out_specs, check_vma=False
    )
```

```python
import jax
import jax.numpy as jnp
from jax import lax
from jax.experimental import pallas as pl
from jax.experimental.pallas import tpu as pltpu
from jax.sharding import PartitionSpec as P

T = 16
DP = 8
D = 8192
ROWS = 128
HEAD = 128
UNITS = 128
QN = 4
CW = D // QN
KE = D // DP
ROUTED = 256
BAL = ROUTED // T
NZ = 4
NY = 4
NX = 4
NC = 2
LINE = DP * BAL
ZC = NY * HEAD
BLK = NZ * LINE // DP
LIMIT = 60
PARTS = 4
EPS = 1e-05
MESH = pl.DeviceIdType.MESH
BF = jnp.bfloat16
F32 = jnp.float32
I32 = jnp.int32


def start(source, target, axis, peer, send_sem, recv_sem):
    pltpu.make_async_remote_copy(
        src_ref=source,
        dst_ref=target,
        send_sem=send_sem,
        recv_sem=recv_sem,
        device_id={axis: peer},
        device_id_type=MESH,
    ).start()


def spread(axis, size, me, source, target, send_sem, recv_sem):
    def body(k, carry):
        peer = lax.rem(me + k, size)
        start(source(peer), target, axis, peer, send_sem, recv_sem)
        return carry

    lax.fori_loop(1, size, body, 0)


def drain(view, sem):
    pltpu.make_async_copy(view, view, sem).wait()


def iota(shape, dim):
    return lax.broadcasted_iota(I32, shape, dim)


def dot(a, b):
    return jnp.dot(a, b, preferred_element_type=F32)


def one_hot(mask):
    return jnp.where(mask, 1.0, 0.0).astype(BF)


def aligned(at, size):
    return pl.ds(pl.multiple_of(at * size, size), size)


def column_of(row):
    eye = iota((ROWS, ROWS), 0) == iota((ROWS, ROWS), 1)
    return jnp.sum(jnp.where(eye, row.astype(F32), 0.0), axis=1, keepdims=True).astype(I32)


def kernel(
    order_hbm, count_ref, wr_hbm, gin_hbm, gnx_hbm, tok_hbm, wgu_hbm, wd_hbm, wq_hbm,
    mixed_hbm, query_hbm,
    order_ref, wr_ref, gin_ref, gnx_ref, tok, tabs, offs, n0, xr, wga, wda, wqg, a2s, a2r, xb, gx, rws, rwr,
    gp, gc, gs, gr, hid, dn, dr, pq, pc, ps, fr, qr, q0s, q0r, ms, mb, rp, rpc, rps, rpr, rqs, rq,
    rts, rtr, mix, qo, spots, spot_m, back,
    local_sem, send_sem, recv_sem, pc_send, pc_recv, fr_send, fr_recv, qr_send, qr_recv, out_sem,
    gc_send, gc_recv, gs_send, gs_recv, hx_send, hx_recv, hc_send, hc_recv,
    dn_send, dn_recv, ms_send, ms_recv, rt_send, rt_recv,
):
    t = lax.axis_index("tensor")
    d = lax.axis_index("dp")
    z, y = lax.div(t, NY), lax.rem(t, NY)
    x, c = lax.div(d, NC), lax.rem(d, NC)
    sibling = x * NC + 1 - c
    near = (1, 3, 2)
    tile = 512
    per = CW // KE

    def at_y(k):
        return lax.rem(y + k, NY)

    def at_z(k):
        return lax.rem(z + k, NZ)

    def at_x(k):
        return lax.rem(x + k, NX)

    def pass_on(part, sem):
        for half, k in ((0, 1), (1, 3)):
            piece = part(at_y(4 - k), half)
            start(piece, piece, "tensor", z * NY + at_y(k), send_sem.at[sem], recv_sem.at[sem])

    my_k = aligned(d, KE)
    wq_own = wq_hbm.at[my_k, :]
    load_order = pltpu.make_async_copy(order_hbm, order_ref, local_sem.at[5])
    load_order.start()
    load_tok = pltpu.make_async_copy(tok_hbm, tok, local_sem.at[0])
    load_tok.start()
    load_gnx = pltpu.make_async_copy(gnx_hbm, gnx_ref, local_sem.at[6])
    load_gnx.start()
    load_gin = pltpu.make_async_copy(gin_hbm, gin_ref, local_sem.at[7])
    load_gin.start()
    load_wr = pltpu.make_async_copy(wr_hbm, wr_ref, local_sem.at[8])
    load_wr.start()
    own_wg = pltpu.make_async_copy(wgu_hbm.at[my_k, :], wga.at[y], local_sem.at[1])
    own_wg.start()
    own_wd = pltpu.make_async_copy(wd_hbm.at[:, my_k], wda.at[y], local_sem.at[2])
    own_wd.start()
    own_wq = pltpu.make_async_copy(wq_own, wqg.at[:, aligned(t, HEAD)], local_sem.at[3])
    own_wq.start()

    barrier = pltpu.get_barrier_semaphore()

    def greet_t(k, carry):
        pl.semaphore_signal(barrier, inc=1, device_id={"tensor": lax.rem(t + k, T)}, device_id_type=MESH)
        return carry

    def greet_d(k, carry):
        pl.semaphore_signal(barrier, inc=1, device_id={"dp": lax.rem(d + k, DP)}, device_id_type=MESH)
        return carry

    lax.fori_loop(1, T, greet_t, 0)
    lax.fori_loop(1, DP, greet_d, 0)

    count = count_ref[0]
    slot = iota((8, ROWS), 1)
    values = jnp.where(slot < count, slot + 1, 0).astype(F32).astype(BF)
    load_order.wait()
    pairs = one_hot(iota((ROWS, ROWS), 0) == order_ref[...])
    own = lax.dot_general(values, pairs, (((1,), (1,)), ((), ())), preferred_element_type=F32)
    tabs[pl.ds(t, 1)] = (own.astype(I32) - 1)[None]

    load_tok.wait()
    load_gnx.wait()
    square = jnp.zeros((ROWS, 1), F32)
    for e in range(DP):
        wide = tok[:, e * KE:(e + 1) * KE].astype(F32)
        square += jnp.sum(wide * wide, axis=1, keepdims=True)
    scale = lax.rsqrt(square / D + EPS)
    for e in range(DP):
        cols = slice(e * KE, (e + 1) * KE)
        n0[e] = (tok[:, cols].astype(F32) * scale * gnx_ref[:, cols]).astype(BF)
    pl.semaphore_wait(barrier, T - 1 + DP - 1)
    spread("tensor", T, t, lambda peer: tabs.at[t], tabs.at[t], send_sem.at[0], recv_sem.at[0])

    start(wq_own, wqg.at[:, aligned(t, HEAD)], "tensor", at_z(2) * NY + y, send_sem.at[1], recv_sem.at[1])
    for k in (1, 3):
        start(wq_own, wqg.at[:, aligned(t, HEAD)], "tensor", z * NY + at_y(k), send_sem.at[2], recv_sem.at[2])

    my_n0 = xr.at[c, x]
    for k in (1, 3):
        for i in range(NC):
            peer = at_x(k) * NC + i
            start(n0.at[peer], my_n0, "dp", peer, send_sem.at[3], recv_sem.at[3])
    start(n0.at[sibling], my_n0, "dp", sibling, send_sem.at[3], recv_sem.at[3])

    def far_n0(i):
        peer = at_x(2) * NC + i
        start(n0.at[peer], my_n0, "dp", peer, send_sem.at[3], recv_sem.at[3])

    own_n0 = pltpu.make_async_copy(n0.at[d], my_n0, local_sem.at[4])
    own_n0.start()
    far_n0(c)
    drain(tabs.at[pl.ds(0, T - 1)], recv_sem.at[0])
    marks = one_hot(tabs[...].reshape(T * 8, ROWS) >= 0)
    counts = dot(marks, jnp.ones((ROWS, ROWS), BF))
    sub, lane = iota((ROWS, ROWS), 0), iota((ROWS, ROWS), 1)
    before = one_hot(((lane // 8) < (sub // 8)) & (lane % 8 == 0))
    firsts = dot(before, counts.astype(BF))
    firsts_i, counts_i = firsts.astype(I32), counts.astype(I32)
    offs[...] = firsts_i

    my_first = offs[aligned(t, 8), :][:1]
    my_slots = tabs[pl.ds(t, 1)][0, :1]
    g_row = jnp.where(my_slots >= 0, my_slots + my_first, -1)
    j = iota((ROUTED, ROWS), 0)
    hit = ((j // 16) == (g_row % 16)) & ((j % 4) == ((g_row // 16) % 4)) & (g_row >= 0)
    pick = jnp.concatenate([one_hot(hit & (((j // 4) % 4) == q)) for q in range(QN)], axis=1)
    for i in range(CW // tile):
        stacked = jnp.concatenate([tok[:, q * CW + i * tile:q * CW + (i + 1) * tile] for q in range(QN)], axis=0)
        a2s[:, i * tile:(i + 1) * tile] = dot(pick, stacked).astype(BF)
    spread("tensor", T, t, lambda peer: a2s.at[aligned(peer, 16), :], a2r.at[aligned(t, 16), :], send_sem.at[4], recv_sem.at[4])
    a2r[aligned(t, 16), :] = a2s[aligned(t, 16), :]

    drain(wqg.at[:, pl.ds(0, 2 * HEAD)], recv_sem.at[2])
    pass_on(lambda at, half: wqg.at[half * (KE // 2):(half + 1) * (KE // 2), aligned(z * NY + at, HEAD)], 7)

    own_wg.wait()
    for k in (1, 3):
        start(wga.at[y], wga.at[y], "tensor", z * NY + at_y(k), send_sem.at[5], recv_sem.at[5])

    first_l, last_l = [], []
    for half in range(2):
        group = iota((8, ROWS), 1) // 16
        lo, hi = jnp.zeros((8, ROWS), I32), jnp.zeros((8, ROWS), I32)
        for i in range(8):
            o = half * 8 + i
            f = firsts_i[o * 8:(o + 1) * 8]
            n = counts_i[o * 8:(o + 1) * 8]
            lo = jnp.where(group == i, f, lo)
            hi = jnp.where(group == i, f + n, hi)
        first_l.append(lo)
        last_l.append(hi)
    first_l = jnp.concatenate(first_l, axis=1)[:1]
    last_l = jnp.concatenate(last_l, axis=1)[:1]
    bi, bj = iota((QN * BAL, ROUTED), 0), iota((QN * BAL, ROUTED), 1)
    g_bal = (bi % BAL) * T + t
    compact = one_hot(
        ((bi // BAL) == ((bj // 4) % 4)) & ((bj % 4) == (bi % 4)) & (first_l <= g_bal) & (g_bal < last_l)
    )
    ri, rj = iota((16, QN * BAL), 0), iota((16, QN * BAL), 1)
    g_bal = (rj % BAL) * T + t
    fits = ((rj // BAL) == (ri // 4)) & ((rj % 4) == (ri % 4))
    for o in range(T):
        lo = jnp.concatenate([firsts_i[o * 8:(o + 1) * 8, :QN * BAL]] * 2, axis=0)
        n = jnp.concatenate([counts_i[o * 8:(o + 1) * 8, :QN * BAL]] * 2, axis=0)
        back[o * 16:(o + 1) * 16, :] = one_hot(fits & (lo <= g_bal) & (g_bal < lo + n))
    g_col = column_of(g_row)
    jl = iota((ROWS, ROUTED), 1)
    hit = ((jl // 16) == (g_col % 16)) & ((jl % 4) == ((g_col // 16) % 4)) & (g_col >= 0)
    for q in range(QN):
        spot_m[q] = one_hot(hit & (((jl // 4) % 4) == q))
    g_lane = (jl % 16) * T + jl // 16

    def find_owner(o, carry):
        slots = tabs[pl.ds(o, 1)][0, :1]
        lo = offs[aligned(o, 8), :][:1]
        col = column_of(jnp.where(slots >= 0, slots + lo, -1))
        spots[pl.ds(o, 1)] = one_hot(col == g_lane)[None]
        return carry

    lax.fori_loop(0, T, find_owner, 0)

    load_gin.wait()
    load_wr.wait()
    drain(a2r.at[pl.ds(0, (T - 1) * 16), :], recv_sem.at[4])
    xb[...] = dot(compact, a2r[...])
    square, logit = jnp.zeros((BAL, 128), F32), jnp.zeros((BAL, 128), F32)
    for q in range(QN):
        rows = xb[q * BAL:(q + 1) * BAL]
        for h in range(per):
            rws[q * per + h, :, :KE] = rows[:, h * KE:(h + 1) * KE].astype(BF)
        for i in range(CW // 128):
            part = rows[:, i * 128:(i + 1) * 128]
            at = q * (CW // 128) + i
            square += part * part
            logit += part * wr_ref[at:at + 1, :].astype(F32)
    scale = lax.rsqrt(jnp.sum(square, axis=1, keepdims=True) / D + EPS)
    weight = 1.0 / (1.0 + jnp.exp(-jnp.sum(logit, axis=1, keepdims=True)))
    terms = []
    for value in (scale, weight):
        for i in range(3):
            terms.append(value.astype(BF).astype(F32))
            value = value - terms[-1]
    at = iota((BAL, 128), 1)
    tail = jnp.zeros((BAL, 128), F32)
    for i in range(6):
        tail = jnp.where(at == i, terms[i], tail)
    for e in range(DP):
        rws[e, :, KE:] = tail.astype(BF)
    spread("dp", DP, d, lambda peer: rws.at[peer], rwr.at[d], send_sem.at[12], recv_sem.at[12])
    rwr[pl.ds(d, 1)] = rws[pl.ds(d, 1)]

    own_wq.wait()
    drain(wqg.at[:, pl.ds(0, HEAD)], recv_sem.at[7])

    def send_piece(i):
        piece = wqg.at[i * (KE // 8):(i + 1) * (KE // 8), aligned(z, ZC)]
        for k in (1, 3):
            start(piece, piece, "tensor", at_z(k) * NY + y, send_sem.at[8], recv_sem.at[8 if k == 3 else 6])

    send_piece(0)

    drain(rwr.at[pl.ds(0, DP - 1)], recv_sem.at[12])
    far_n0(1 - c)
    raw = rwr[...].reshape(LINE, KE + 128)
    both = raw[:, KE:].astype(F32)
    scale = both[:, :1] + both[:, 1:2] + both[:, 2:3]
    line_weight = both[:, 3:4] + both[:, 4:5] + both[:, 5:6]
    normed = (raw[:, :KE].astype(F32) * scale * gin_ref[:, my_k]).astype(BF)
    gx[pl.ds(z, 1)] = normed.reshape(1, DP, BAL, KE)
    for k in (1, 3):
        start(gx.at[z], gx.at[z], "tensor", at_z(k) * NY + y, send_sem.at[9], recv_sem.at[9])
    send_piece(1)

    def pass_gx():
        drain(gx.at[pl.ds(0, 2)], recv_sem.at[9])
        for half, k in ((0, 1), (1, 3)):
            piece = gx.at[at_z(4 - k), half * (DP // 2):(half + 1) * (DP // 2)]
            start(piece, piece, "tensor", at_z(k) * NY + y, send_sem.at[14], recv_sem.at[14])

    def chunk_product(k):
        rows = xr[...].reshape(DP * ROWS, KE)
        for i in range(2):
            cols = pl.ds(pl.multiple_of(at_z(k) * ZC + i * (ZC // 2), ZC // 2), ZC // 2)
            product = dot(rows, wqg[:, cols]).astype(BF)
            pq[k, :, :, :, i * (ZC // 2):(i + 1) * (ZC // 2)] = product.reshape(NC, NX, ROWS, ZC // 2)
        start(pq.at[k, 1 - c], pc.at[k], "dp", sibling, pc_send.at[k], pc_recv.at[k])

    def chunk_pair(k):
        drain(pc.at[k], pc_recv.at[k])
        for i in range(NX):
            ps[k, i] = (pq[k, c, i].astype(F32) + pc[k, i].astype(F32)).astype(BF)
        for half, i in ((0, 1), (1, 3)):
            part = ps.at[k, at_x(2), half * (ROWS // 2):(half + 1) * (ROWS // 2)]
            start(part, fr.at[k, half], "dp", at_x(i) * NC + c, fr_send.at[k], fr_recv.at[k])

    def chunk_pass(k):
        drain(fr.at[k], fr_recv.at[k])
        for half, i in ((0, 1), (1, 3)):
            rows = slice(half * (ROWS // 2), (half + 1) * (ROWS // 2))
            total = ps[k, pl.ds(at_x(i), 1), rows].astype(F32) + fr[k, half].astype(F32)[None]
            ps[k, pl.ds(at_x(i), 1), rows] = total.astype(BF)
        for half, i in ((0, 1), (1, 3)):
            start(ps.at[k, at_x(i)], qr.at[k, half], "dp", at_x(i) * NC + c, qr_send.at[k], qr_recv.at[k])

    def chunk_sum(k):
        drain(qr.at[k], qr_recv.at[k])
        total = ps[k, pl.ds(x, 1)][0].astype(F32)
        for i in range(2):
            total += qr[k, i].astype(F32)
        total = jnp.where(g_col >= 0, 0.0, total).astype(BF)
        for i in range(NY):
            q0s[k, i] = total[:, i * HEAD:(i + 1) * HEAD]
        for i in range(NY):
            if k > 0 or i > 0:
                start(q0s.at[k, at_y(i)], q0r.at[t], "tensor", at_z(k) * NY + at_y(i), send_sem.at[13], recv_sem.at[13])
        if k == 0:
            q0r[pl.ds(t, 1)] = q0s[0, pl.ds(y, 1)]

    drain(wga.at[pl.ds(0, 2)], recv_sem.at[5])
    pass_on(lambda at, half: wga.at[at, half * (KE // 2):(half + 1) * (KE // 2)], 23)
    pass_gx()
    send_piece(2)
    send_piece(3)
    send_piece(4)
    send_piece(5)
    send_piece(6)
    send_piece(7)
    own_wd.wait()
    for k in (1, 3):
        start(wda.at[y], wda.at[y], "tensor", z * NY + at_y(k), send_sem.at[10], recv_sem.at[10])
    drain(wqg.at[:, pl.ds(0, HEAD)], recv_sem.at[1])

    def send_far():
        far_head = wqg.at[:, aligned(at_z(2) * NY + y, HEAD)]
        for k in near:
            start(far_head, far_head, "tensor", z * NY + at_y(k), send_sem.at[11], recv_sem.at[11])

    def pass_wda():
        drain(wda.at[pl.ds(0, 2)], recv_sem.at[10])
        pass_on(lambda at, half: wda.at[at, half * (UNITS // 2):(half + 1) * (UNITS // 2)], 25)


    own_n0.wait()
    drain(n0.at[pl.ds(0, DP - 1)], recv_sem.at[3])
    chunk_product(0)
    chunk_pair(0)

    drain(wga.at[0], recv_sem.at[23])
    chunk_pass(0)
    drain(gx.at[0], recv_sem.at[14])
    rows = gx[...].reshape(NZ * LINE, KE)
    for i in range(NY):
        gp[i // 2, :, :, :, i % 2 * 2 * UNITS:(i % 2 + 1) * 2 * UNITS] = dot(rows, wga[i]).reshape(NC, NX, BLK, 2 * UNITS)
        if i % 2 == 1:
            start(gp.at[i // 2, 1 - c], gc.at[i // 2], "dp", sibling, gc_send.at[i // 2], gc_recv.at[i // 2])
    for h in range(2):
        drain(gc.at[h], gc_recv.at[h])
        for i in range(NX):
            gs[h, i] = (gp[h, c, i] + gc[h, i]).astype(BF)
        for k in near:
            start(gs.at[h, at_x(k)], gr.at[h, k - 1], "dp", at_x(k) * NC + c, gs_send.at[h], gs_recv.at[h])
    pass_wda()
    send_far()
    for h in range(2):
        drain(gr.at[h], gs_recv.at[h])
        total = gp[h, pl.ds(c, 1), pl.ds(x, 1)][0, 0] + gc[h, pl.ds(x, 1)][0]
        for i in range(NX - 1):
            total += gr[h, i].astype(F32)
        for i in range(NY // 2):
            gate = total[:, i * 2 * UNITS:i * 2 * UNITS + UNITS]
            up = total[:, i * 2 * UNITS + UNITS:(i + 1) * 2 * UNITS]
            units = (gate / (1.0 + jnp.exp(-gate)) * up).astype(BF)
            hid[h, pl.ds(c, 1), pl.ds(x, 1), :, i * UNITS:(i + 1) * UNITS] = units[None, None]
        for k in near:
            start(hid.at[h, c, x], hid.at[h, c, x], "dp", at_x(k) * NC + c, hx_send.at[h], hx_recv.at[h])
    for h in range(2):
        drain(hid.at[h, 0, pl.ds(0, NX - 1)], hx_recv.at[h])
        start(hid.at[h, c], hid.at[h, c], "dp", sibling, hc_send.at[h], hc_recv.at[h])
    drain(wda.at[0], recv_sem.at[25])
    for h in range(2):
        drain(hid.at[h, 0], hc_recv.at[h])
    hidden = [hid[h].reshape(NZ * LINE, NY * UNITS // 2) for h in range(2)]
    down = wda[...].reshape(2, NY * UNITS // 2, KE)
    for h in range(2):
        for i in range(tile // 256):
            at = h * tile + i * 256
            dn[h, :, :, i * 256:(i + 1) * 256] = (dot(hidden[0], down[0, :, at:at + 256]) + dot(hidden[1], down[1, :, at:at + 256])).astype(BF).reshape(NZ, LINE, 256)
        for k in near:
            start(dn.at[h, at_z(k)], dr.at[h, k - 1], "tensor", at_z(k) * NY + y, dn_send.at[h], dn_recv.at[h])
    chunk_sum(0)
    drain(wqg.at[:, pl.ds(0, ZC)], recv_sem.at[8])
    chunk_product(1)
    chunk_pair(1)
    drain(wqg.at[:, pl.ds(0, ZC)], recv_sem.at[6])
    chunk_product(3)
    def mix_half(h):
        drain(dr.at[h], dn_recv.at[h])
        branch = dn[h, pl.ds(z, 1)][0].astype(F32)
        for i in range(NZ - 1):
            branch += dr[h, i].astype(F32)
        cols = slice(h * tile, (h + 1) * tile)
        mixed = (raw[:, cols].astype(F32) + line_weight * branch).astype(BF)
        ms[h] = mixed.reshape(DP, BAL, tile)
        spread("dp", DP, d, lambda peer: ms.at[h, peer], mb.at[h, d], ms_send.at[h], ms_recv.at[h])
        mb[h, pl.ds(d, 1)] = ms[h, pl.ds(d, 1)]
        gain = gnx_ref[:, pl.ds(pl.multiple_of(d * KE + h * tile, tile), tile)]
        return (mixed.astype(F32) * gain).astype(BF)

    def return_half(h):
        drain(mb.at[h, pl.ds(0, DP - 1)], ms_recv.at[h])
        for i in range(per):
            stacked = jnp.concatenate([mb[h, q * per + i] for q in range(QN)], axis=0)
            rts[h, :, i * tile:(i + 1) * tile] = dot(back[...], stacked).astype(BF)
        spread("tensor", T, t, lambda peer: rts.at[h, aligned(peer, 16), :], rtr.at[h, aligned(t, 16), :], rt_send.at[h], rt_recv.at[h])
        rtr[h, aligned(t, 16), :] = rts[h, aligned(t, 16), :]

    upper_rows = mix_half(0)
    chunk_pair(3)
    chunk_pass(1)
    drain(wqg.at[:, pl.ds(0, 3 * HEAD)], recv_sem.at[11])
    chunk_product(2)
    return_half(0)
    chunk_pass(3)
    rows = jnp.concatenate([upper_rows, mix_half(1)], axis=1)
    for i in range(T // 2):
        cols = slice(i * 2 * HEAD, (i + 1) * 2 * HEAD)
        product = dot(rows, wqg[:, cols]).astype(BF)
        for e in range(DP):
            rp[e % NC, e // NC, :, cols] = product[e * BAL:(e + 1) * BAL]
    start(rp.at[1 - c], rpc, "dp", sibling, send_sem.at[20], recv_sem.at[20])
    chunk_pair(2)
    drain(rpc, recv_sem.at[20])
    for i in range(NX):
        rps[i] = (rp[c, i].astype(F32) + rpc[i].astype(F32)).astype(BF)
    for k in near:
        start(rps.at[at_x(k)], rpr.at[k - 1], "dp", at_x(k) * NC + c, send_sem.at[6], recv_sem.at[24])
    chunk_sum(1)
    chunk_sum(3)
    return_half(1)
    square = jnp.zeros((BAL, 1), F32)
    for h in range(2):
        for e in range(DP):
            wide = mb[h, e].astype(F32)
            square += jnp.sum(wide * wide, axis=1, keepdims=True)
    scale = lax.rsqrt(square / D + EPS)
    chunk_pass(2)
    drain(rpr, recv_sem.at[24])
    total = rps[pl.ds(x, 1)][0].astype(F32)
    for i in range(NX - 1):
        total += rpr[i].astype(F32)
    total = (total * scale).astype(BF)
    for h in range(T):
        rqs[h] = total[:, h * HEAD:(h + 1) * HEAD]
    spread("tensor", T, t, lambda peer: rqs.at[peer], rq.at[t], send_sem.at[22], recv_sem.at[22])
    rq[pl.ds(t, 1)] = rqs[pl.ds(t, 1)]
    chunk_sum(2)
    for h in range(2):
        drain(rtr.at[h, pl.ds(0, (T - 1) * 16), :], rt_recv.at[h])
    outs = []
    for q in range(QN):
        for i in range(per):
            for h in range(2):
                at = q * CW + i * KE + h * tile
                moved = dot(spot_m[q], rtr[h, :, i * tile:(i + 1) * tile]).astype(BF)
                mix[:, at:at + tile] = jnp.where(g_col >= 0, moved, tok[:, at:at + tile])
        cols = pl.ds(q * CW, CW)
        copy = pltpu.make_async_copy(mix.at[:, cols], mixed_hbm.at[:, cols], out_sem.at[q])
        copy.start()
        outs.append(copy)

    drain(q0r.at[pl.ds(0, T - 1)], recv_sem.at[13])
    drain(rq.at[pl.ds(0, T - 1)], recv_sem.at[22])
    routed = rq[...].reshape(ROUTED, HEAD)

    def place_owner(o, carry):
        moved = dot(spots[pl.ds(o, 1)][0], routed)
        plain = q0r[pl.ds(o, 1)][0].astype(F32)
        qo[aligned(o, ROWS), :] = (moved + plain).astype(BF)
        return carry

    for i in range(NZ):
        for o in range(i * NY, (i + 1) * NY):
            place_owner(o, 0)
        rows = pl.ds(i * NY * ROWS, NY * ROWS)
        copy = pltpu.make_async_copy(qo.at[rows, :], query_hbm.at[rows, :], out_sem.at[QN + i])
        copy.start()
        outs.append(copy)

    drain(tabs.at[pl.ds(0, T - 1)], send_sem.at[0])
    drain(wqg.at[:, pl.ds(0, HEAD)], send_sem.at[1])
    drain(wqg.at[:, pl.ds(0, 2 * HEAD)], send_sem.at[2])
    drain(n0.at[pl.ds(0, DP - 1)], send_sem.at[3])
    drain(a2s.at[pl.ds(0, (T - 1) * 16), :], send_sem.at[4])
    drain(wga.at[pl.ds(0, 2)], send_sem.at[5])
    drain(wqg.at[:, pl.ds(0, HEAD)], send_sem.at[7])
    drain(wqg.at[:, pl.ds(0, 2 * ZC)], send_sem.at[8])
    drain(rqs.at[pl.ds(0, T - 1)], send_sem.at[22])
    drain(wga.at[0], send_sem.at[23])
    drain(gx.at[pl.ds(0, 2)], send_sem.at[9])
    drain(gx.at[0], send_sem.at[14])
    drain(wda.at[pl.ds(0, 2)], send_sem.at[10])
    drain(wda.at[0], send_sem.at[25])
    drain(wqg.at[:, pl.ds(0, 3 * HEAD)], send_sem.at[11])
    drain(rws.at[pl.ds(0, DP - 1)], send_sem.at[12])
    drain(q0r.at[pl.ds(0, T - 1)], send_sem.at[13])
    for h in range(2):
        drain(gc.at[h], gc_send.at[h])
        drain(gr.at[h], gs_send.at[h])
        drain(hid.at[h, 0, pl.ds(0, NX - 1)], hx_send.at[h])
        drain(hid.at[h, 0], hc_send.at[h])
    for h in range(2):
        drain(dr.at[h], dn_send.at[h])
        drain(ms.at[h, pl.ds(0, DP - 1)], ms_send.at[h])
        drain(rts.at[h, pl.ds(0, (T - 1) * 16), :], rt_send.at[h])
    drain(rpc, send_sem.at[20])
    drain(rpr, send_sem.at[6])
    for k in range(NZ):
        drain(pc.at[k], pc_send.at[k])
        drain(fr.at[k], fr_send.at[k])
        drain(qr.at[k], qr_send.at[k])
    for copy in outs:
        copy.wait()


def hand_over(mixed, query, mixed_out, query_out, held_mixed, held_query, in_sem, out_sem):
    loads, stores = [], []
    for i in range(PARTS):
        for j, (source, held, target) in enumerate(((mixed, held_mixed, mixed_out), (query, held_query, query_out))):
            n = source.shape[0] // PARTS
            rows = pl.ds(i * n, n)
            loads.append(pltpu.make_async_copy(source.at[rows, :], held.at[rows, :], in_sem.at[2 * i + j]))
            stores.append(pltpu.make_async_copy(held.at[rows, :], target.at[rows, :], out_sem.at[2 * i + j]))
            loads[-1].start()
    for load, store in zip(loads, stores):
        load.wait()
        store.start()
    for store in stores:
        store.wait()


def on_device(tokens, route_order, route_counts, w_router, gain_in, w_gate_up, w_down, gain_next, w_query):
    hbm = pl.BlockSpec(memory_space=pltpu.HBM)
    anywhere = pl.BlockSpec(memory_space=pl.ANY)
    mixed, query = pl.pallas_call(
        kernel,
        out_shape=(
            jax.ShapeDtypeStruct((ROWS, D), BF),
            jax.ShapeDtypeStruct((T * ROWS, HEAD), BF),
        ),
        in_specs=[hbm, pl.BlockSpec(memory_space=pltpu.SMEM)] + [hbm] * 7,
        out_specs=(anywhere, anywhere),
        scratch_shapes=[
            pltpu.VMEM((1, ROWS), I32),
            pltpu.VMEM((D // 128, 128), BF),
            pltpu.VMEM((1, D), F32),
            pltpu.VMEM((1, D), F32),
            pltpu.VMEM((ROWS, D), BF),
            pltpu.VMEM((T, 8, ROWS), I32),
            pltpu.VMEM((ROWS, ROWS), I32),
            pltpu.VMEM((DP, ROWS, KE), BF),
            pltpu.VMEM((NC, NX, ROWS, KE), BF),
            pltpu.VMEM((NY, KE, 2 * UNITS), BF),
            pltpu.VMEM((NY, UNITS, KE), BF),
            pltpu.VMEM((KE, T * HEAD), BF),
            pltpu.VMEM((ROUTED, CW), BF),
            pltpu.VMEM((ROUTED, CW), BF),
            pltpu.VMEM((QN * BAL, CW), F32),
            pltpu.VMEM((NZ, DP, BAL, KE), BF),
            pltpu.VMEM((DP, BAL, KE + 128), BF),
            pltpu.VMEM((DP, BAL, KE + 128), BF),
            pltpu.VMEM((2, NC, NX, BLK, NY * UNITS), F32),
            pltpu.VMEM((2, NX, BLK, NY * UNITS), F32),
            pltpu.VMEM((2, NX, BLK, NY * UNITS), BF),
            pltpu.VMEM((2, NX - 1, BLK, NY * UNITS), BF),
            pltpu.VMEM((2, NC, NX, BLK, NY * UNITS // 2), BF),
            pltpu.VMEM((2, NZ, LINE, KE // 2), BF),
            pltpu.VMEM((2, NZ - 1, LINE, KE // 2), BF),
            pltpu.VMEM((NZ, NC, NX, ROWS, ZC), BF),
            pltpu.VMEM((NZ, NX, ROWS, ZC), BF),
            pltpu.VMEM((NZ, NX, ROWS, ZC), BF),
            pltpu.VMEM((NZ, 2, ROWS // 2, ZC), BF),
            pltpu.VMEM((NZ, 2, ROWS, ZC), BF),
            pltpu.VMEM((NZ, NY, ROWS, HEAD), BF),
            pltpu.VMEM((T, ROWS, HEAD), BF),
            pltpu.VMEM((2, DP, BAL, KE // 2), BF),
            pltpu.VMEM((2, DP, BAL, KE // 2), BF),
            pltpu.VMEM((NC, NX, BAL, T * HEAD), BF),
            pltpu.VMEM((NX, BAL, T * HEAD), BF),
            pltpu.VMEM((NX, BAL, T * HEAD), BF),
            pltpu.VMEM((NX - 1, BAL, T * HEAD), BF),
            pltpu.VMEM((T, BAL, HEAD), BF),
            pltpu.VMEM((T, BAL, HEAD), BF),
            pltpu.VMEM((2, ROUTED, CW // 2), BF),
            pltpu.VMEM((2, ROUTED, CW // 2), BF),
            pltpu.VMEM((ROWS, D), BF),
            pltpu.VMEM((T * ROWS, HEAD), BF),
            pltpu.VMEM((T, ROWS, ROUTED), BF),
            pltpu.VMEM((QN, ROWS, ROUTED), BF),
            pltpu.VMEM((ROUTED, QN * BAL), BF),
            pltpu.SemaphoreType.DMA((9,)),
            pltpu.SemaphoreType.DMA((26,)),
            pltpu.SemaphoreType.DMA((26,)),
            pltpu.SemaphoreType.DMA((NZ,)),
            pltpu.SemaphoreType.DMA((NZ,)),
            pltpu.SemaphoreType.DMA((NZ,)),
            pltpu.SemaphoreType.DMA((NZ,)),
            pltpu.SemaphoreType.DMA((NZ,)),
            pltpu.SemaphoreType.DMA((NZ,)),
            pltpu.SemaphoreType.DMA((QN + NZ,)),
            pltpu.SemaphoreType.DMA((2,)),
            pltpu.SemaphoreType.DMA((2,)),
            pltpu.SemaphoreType.DMA((2,)),
            pltpu.SemaphoreType.DMA((2,)),
            pltpu.SemaphoreType.DMA((2,)),
            pltpu.SemaphoreType.DMA((2,)),
            pltpu.SemaphoreType.DMA((2,)),
            pltpu.SemaphoreType.DMA((2,)),
            pltpu.SemaphoreType.DMA((2,)),
            pltpu.SemaphoreType.DMA((2,)),
            pltpu.SemaphoreType.DMA((2,)),
            pltpu.SemaphoreType.DMA((2,)),
            pltpu.SemaphoreType.DMA((2,)),
            pltpu.SemaphoreType.DMA((2,)),
        ],
        compiler_params=pltpu.CompilerParams(
            collective_id=0, has_side_effects=True, vmem_limit_bytes=LIMIT * 1024 * 1024
        ),
    )(
        route_order, route_counts, w_router.reshape(D // 128, 128), gain_in.reshape(1, D), gain_next.reshape(1, D),
        tokens, w_gate_up, w_down, w_query,
    )
    return pl.pallas_call(
        hand_over,
        out_shape=(
            jax.ShapeDtypeStruct((ROWS, D), BF),
            jax.ShapeDtypeStruct((T * ROWS, HEAD), BF),
        ),
        in_specs=[anywhere] * 2,
        out_specs=(anywhere, anywhere),
        scratch_shapes=[
            pltpu.VMEM((ROWS, D), BF),
            pltpu.VMEM((T * ROWS, HEAD), BF),
            pltpu.SemaphoreType.DMA((2 * PARTS,)),
            pltpu.SemaphoreType.DMA((2 * PARTS,)),
        ],
    )(mixed, query)


def solution(mesh):
    in_specs = (
        P(("dp", "tensor"), None),
        P(("dp", "tensor"), None),
        P(("dp", "tensor")),
        P(),
        P(),
        P(None, "tensor"),
        P("tensor", None),
        P(),
        P(None, "tensor"),
    )
    out_specs = (P(("dp", "tensor"), None), P("dp", "tensor"))
    return jax.shard_map(
        on_device, mesh=mesh, in_specs=in_specs, out_specs=out_specs, check_vma=False
    )
```

```python
import jax
import jax.numpy as jnp
from jax import lax
from jax.experimental import pallas as pl
from jax.experimental.pallas import tpu as pltpu
from jax.sharding import PartitionSpec as P

T = 16
DP = 8
D = 8192
ROWS = 128
HEAD = 128
UNITS = 128
QN = 4
CW = D // QN
KE = D // DP
ROUTED = 256
BAL = ROUTED // T
NZ = 4
NY = 4
NX = 4
NC = 2
LINE = DP * BAL
ZC = NY * HEAD
BLK = NZ * LINE // DP
LIMIT = 60
PARTS = 4
EPS = 1e-05
MESH = pl.DeviceIdType.MESH
BF = jnp.bfloat16
F32 = jnp.float32
I32 = jnp.int32


def start(source, target, axis, peer, send_sem, recv_sem):
    pltpu.make_async_remote_copy(
        src_ref=source,
        dst_ref=target,
        send_sem=send_sem,
        recv_sem=recv_sem,
        device_id={axis: peer},
        device_id_type=MESH,
    ).start()


def spread(axis, size, me, source, target, send_sem, recv_sem):
    def body(k, carry):
        peer = lax.rem(me + k, size)
        start(source(peer), target, axis, peer, send_sem, recv_sem)
        return carry

    lax.fori_loop(1, size, body, 0)


def drain(view, sem):
    pltpu.make_async_copy(view, view, sem).wait()


def iota(shape, dim):
    return lax.broadcasted_iota(I32, shape, dim)


def dot(a, b):
    return jnp.dot(a, b, preferred_element_type=F32)


def one_hot(mask):
    return jnp.where(mask, 1.0, 0.0).astype(BF)


def aligned(at, size):
    return pl.ds(pl.multiple_of(at * size, size), size)


def column_of(row):
    eye = iota((ROWS, ROWS), 0) == iota((ROWS, ROWS), 1)
    return jnp.sum(jnp.where(eye, row.astype(F32), 0.0), axis=1, keepdims=True).astype(I32)


def kernel(
    order_hbm, count_ref, wr_hbm, gin_hbm, gnx_hbm, tok_hbm, wgu_hbm, wd_hbm, wq_hbm,
    mixed_hbm, query_hbm,
    order_ref, wr_ref, gin_ref, gnx_ref, tok, tabs, offs, n0, xr, wga, wda, wqg, a2s, a2r, xb, gx, rws, rwr,
    gp, gc, gs, gr, hid, dn, dr, pq, pc, ps, fr, qr, q0s, q0r, ms, mb, rp, rpc, rps, rpr, rqs, rq,
    rts, rtr, mix, qo, spots, spot_m, back,
    local_sem, send_sem, recv_sem, pc_send, pc_recv, fr_send, fr_recv, qr_send, qr_recv, q0_recv, out_sem,
    gc_send, gc_recv, gs_send, gs_recv, hx_send, hx_recv, hc_send, hc_recv,
    dn_send, dn_recv, ms_send, ms_recv, rt_send, rt_recv,
):
    t = lax.axis_index("tensor")
    d = lax.axis_index("dp")
    z, y = lax.div(t, NY), lax.rem(t, NY)
    x, c = lax.div(d, NC), lax.rem(d, NC)
    sibling = x * NC + 1 - c
    near = (2, 1, 3)
    tile = 512
    per = CW // KE

    def at_y(k):
        return lax.rem(y + k, NY)

    def at_z(k):
        return lax.rem(z + k, NZ)

    def at_x(k):
        return lax.rem(x + k, NX)

    def pass_on(part, sem):
        for half, k in ((0, 1), (1, 3)):
            piece = part(at_y(4 - k), half)
            start(piece, piece, "tensor", z * NY + at_y(k), send_sem.at[sem], recv_sem.at[sem])

    my_k = aligned(d, KE)
    wq_own = wq_hbm.at[my_k, :]
    load_order = pltpu.make_async_copy(order_hbm, order_ref, local_sem.at[5])
    load_order.start()
    load_tok = pltpu.make_async_copy(tok_hbm, tok, local_sem.at[0])
    load_tok.start()
    load_gnx = pltpu.make_async_copy(gnx_hbm, gnx_ref, local_sem.at[6])
    load_gnx.start()
    load_gin = pltpu.make_async_copy(gin_hbm, gin_ref, local_sem.at[7])
    load_gin.start()
    load_wr = pltpu.make_async_copy(wr_hbm, wr_ref, local_sem.at[8])
    load_wr.start()
    own_wg = pltpu.make_async_copy(wgu_hbm.at[my_k, :], wga.at[y], local_sem.at[1])
    own_wg.start()
    own_wd = pltpu.make_async_copy(wd_hbm.at[:, my_k], wda.at[y], local_sem.at[2])
    own_wd.start()
    own_wq = pltpu.make_async_copy(wq_own, wqg.at[:, aligned(t, HEAD)], local_sem.at[3])
    own_wq.start()

    barrier = pltpu.get_barrier_semaphore()

    def greet_t(k, carry):
        pl.semaphore_signal(barrier, inc=1, device_id={"tensor": lax.rem(t + k, T)}, device_id_type=MESH)
        return carry

    def greet_d(k, carry):
        pl.semaphore_signal(barrier, inc=1, device_id={"dp": lax.rem(d + k, DP)}, device_id_type=MESH)
        return carry

    lax.fori_loop(1, T, greet_t, 0)
    lax.fori_loop(1, DP, greet_d, 0)

    count = count_ref[0]
    slot = iota((8, ROWS), 1)
    values = jnp.where(slot < count, slot + 1, 0).astype(F32).astype(BF)
    load_order.wait()
    pairs = one_hot(iota((ROWS, ROWS), 0) == order_ref[...])
    own = lax.dot_general(values, pairs, (((1,), (1,)), ((), ())), preferred_element_type=F32)
    tabs[pl.ds(t, 1)] = (own.astype(I32) - 1)[None]

    load_tok.wait()
    load_gnx.wait()
    square = jnp.zeros((ROWS, 1), F32)
    for e in range(DP):
        wide = tok[:, e * KE:(e + 1) * KE].astype(F32)
        square += jnp.sum(wide * wide, axis=1, keepdims=True)
    scale = lax.rsqrt(square / D + EPS)
    for e in range(DP):
        cols = slice(e * KE, (e + 1) * KE)
        n0[e] = (tok[:, cols].astype(F32) * scale * gnx_ref[:, cols]).astype(BF)
    pl.semaphore_wait(barrier, T - 1 + DP - 1)
    spread("tensor", T, t, lambda peer: tabs.at[t], tabs.at[t], send_sem.at[0], recv_sem.at[0])

    start(wq_own, wqg.at[:, aligned(t, HEAD)], "tensor", at_z(2) * NY + y, send_sem.at[1], recv_sem.at[1])
    for k in (1, 3):
        start(wq_own, wqg.at[:, aligned(t, HEAD)], "tensor", z * NY + at_y(k), send_sem.at[2], recv_sem.at[2])

    my_n0 = xr.at[c, x]
    for k in (1, 3):
        for i in range(NC):
            peer = at_x(k) * NC + i
            start(n0.at[peer], my_n0, "dp", peer, send_sem.at[3], recv_sem.at[3])
    start(n0.at[sibling], my_n0, "dp", sibling, send_sem.at[3], recv_sem.at[3])

    def far_n0(i):
        peer = at_x(2) * NC + i
        start(n0.at[peer], my_n0, "dp", peer, send_sem.at[3], recv_sem.at[3])

    own_n0 = pltpu.make_async_copy(n0.at[d], my_n0, local_sem.at[4])
    own_n0.start()
    far_n0(c)
    drain(tabs.at[pl.ds(0, T - 1)], recv_sem.at[0])
    marks = one_hot(tabs[...].reshape(T * 8, ROWS) >= 0)
    counts = dot(marks, jnp.ones((ROWS, ROWS), BF))
    sub, lane = iota((ROWS, ROWS), 0), iota((ROWS, ROWS), 1)
    before = one_hot(((lane // 8) < (sub // 8)) & (lane % 8 == 0))
    firsts = dot(before, counts.astype(BF))
    firsts_i, counts_i = firsts.astype(I32), counts.astype(I32)
    offs[...] = firsts_i

    my_first = offs[aligned(t, 8), :][:1]
    my_slots = tabs[pl.ds(t, 1)][0, :1]
    g_row = jnp.where(my_slots >= 0, my_slots + my_first, -1)
    j = iota((ROUTED, ROWS), 0)
    hit = ((j // 16) == (g_row % 16)) & ((j % 4) == ((g_row // 16) % 4)) & (g_row >= 0)
    pick = jnp.concatenate([one_hot(hit & (((j // 4) % 4) == q)) for q in range(QN)], axis=1)
    for i in range(CW // tile):
        stacked = jnp.concatenate([tok[:, q * CW + i * tile:q * CW + (i + 1) * tile] for q in range(QN)], axis=0)
        a2s[:, i * tile:(i + 1) * tile] = dot(pick, stacked).astype(BF)
    spread("tensor", T, t, lambda peer: a2s.at[aligned(peer, 16), :], a2r.at[aligned(t, 16), :], send_sem.at[4], recv_sem.at[4])
    a2r[aligned(t, 16), :] = a2s[aligned(t, 16), :]

    drain(wqg.at[:, pl.ds(0, 2 * HEAD)], recv_sem.at[2])
    pass_on(lambda at, half: wqg.at[half * (KE // 2):(half + 1) * (KE // 2), aligned(z * NY + at, HEAD)], 7)

    own_wg.wait()
    for k in (1, 3):
        start(wga.at[y], wga.at[y], "tensor", z * NY + at_y(k), send_sem.at[5], recv_sem.at[5])

    first_l, last_l = [], []
    for half in range(2):
        group = iota((8, ROWS), 1) // 16
        lo, hi = jnp.zeros((8, ROWS), I32), jnp.zeros((8, ROWS), I32)
        for i in range(8):
            o = half * 8 + i
            f = firsts_i[o * 8:(o + 1) * 8]
            n = counts_i[o * 8:(o + 1) * 8]
            lo = jnp.where(group == i, f, lo)
            hi = jnp.where(group == i, f + n, hi)
        first_l.append(lo)
        last_l.append(hi)
    first_l = jnp.concatenate(first_l, axis=1)[:1]
    last_l = jnp.concatenate(last_l, axis=1)[:1]
    bi, bj = iota((QN * BAL, ROUTED), 0), iota((QN * BAL, ROUTED), 1)
    g_bal = (bi % BAL) * T + t
    compact = one_hot(
        ((bi // BAL) == ((bj // 4) % 4)) & ((bj % 4) == (bi % 4)) & (first_l <= g_bal) & (g_bal < last_l)
    )
    ri, rj = iota((16, QN * BAL), 0), iota((16, QN * BAL), 1)
    g_bal = (rj % BAL) * T + t
    fits = ((rj // BAL) == (ri // 4)) & ((rj % 4) == (ri % 4))
    for o in range(T):
        lo = jnp.concatenate([firsts_i[o * 8:(o + 1) * 8, :QN * BAL]] * 2, axis=0)
        n = jnp.concatenate([counts_i[o * 8:(o + 1) * 8, :QN * BAL]] * 2, axis=0)
        back[o * 16:(o + 1) * 16, :] = one_hot(fits & (lo <= g_bal) & (g_bal < lo + n))
    g_col = column_of(g_row)
    jl = iota((ROWS, ROUTED), 1)
    hit = ((jl // 16) == (g_col % 16)) & ((jl % 4) == ((g_col // 16) % 4)) & (g_col >= 0)
    for q in range(QN):
        spot_m[q] = one_hot(hit & (((jl // 4) % 4) == q))
    g_lane = (jl % 16) * T + jl // 16

    def find_owner(o, carry):
        slots = tabs[pl.ds(o, 1)][0, :1]
        lo = offs[aligned(o, 8), :][:1]
        col = column_of(jnp.where(slots >= 0, slots + lo, -1))
        spots[pl.ds(o, 1)] = one_hot(col == g_lane)[None]
        return carry

    lax.fori_loop(0, T, find_owner, 0)

    load_gin.wait()
    load_wr.wait()
    drain(a2r.at[pl.ds(0, (T - 1) * 16), :], recv_sem.at[4])
    xb[...] = dot(compact, a2r[...])
    square, logit = jnp.zeros((BAL, 128), F32), jnp.zeros((BAL, 128), F32)
    for q in range(QN):
        rows = xb[q * BAL:(q + 1) * BAL]
        for h in range(per):
            rws[q * per + h, :, :KE] = rows[:, h * KE:(h + 1) * KE].astype(BF)
        for i in range(CW // 128):
            part = rows[:, i * 128:(i + 1) * 128]
            at = q * (CW // 128) + i
            square += part * part
            logit += part * wr_ref[at:at + 1, :].astype(F32)
    scale = lax.rsqrt(jnp.sum(square, axis=1, keepdims=True) / D + EPS)
    weight = 1.0 / (1.0 + jnp.exp(-jnp.sum(logit, axis=1, keepdims=True)))
    terms = []
    for value in (scale, weight):
        for i in range(3):
            terms.append(value.astype(BF).astype(F32))
            value = value - terms[-1]
    at = iota((BAL, 128), 1)
    tail = jnp.zeros((BAL, 128), F32)
    for i in range(6):
        tail = jnp.where(at == i, terms[i], tail)
    for e in range(DP):
        rws[e, :, KE:] = tail.astype(BF)
    spread("dp", DP, d, lambda peer: rws.at[peer], rwr.at[d], send_sem.at[12], recv_sem.at[12])
    rwr[pl.ds(d, 1)] = rws[pl.ds(d, 1)]

    own_wq.wait()
    drain(wqg.at[:, pl.ds(0, HEAD)], recv_sem.at[7])

    def send_piece(i):
        piece = wqg.at[i * (KE // 8):(i + 1) * (KE // 8), aligned(z, ZC)]
        for k in (1, 3):
            start(piece, piece, "tensor", at_z(k) * NY + y, send_sem.at[8], recv_sem.at[8 if k == 3 else 6])

    send_piece(0)

    drain(rwr.at[pl.ds(0, DP - 1)], recv_sem.at[12])
    far_n0(1 - c)
    raw = rwr[...].reshape(LINE, KE + 128)
    both = raw[:, KE:].astype(F32)
    scale = both[:, :1] + both[:, 1:2] + both[:, 2:3]
    line_weight = both[:, 3:4] + both[:, 4:5] + both[:, 5:6]
    normed = (raw[:, :KE].astype(F32) * scale * gin_ref[:, my_k]).astype(BF)
    gx[pl.ds(z, 1)] = normed.reshape(1, DP, BAL, KE)
    for k in (1, 3):
        start(gx.at[z], gx.at[z], "tensor", at_z(k) * NY + y, send_sem.at[9], recv_sem.at[9])
    send_piece(1)

    def pass_gx():
        drain(gx.at[pl.ds(0, 2)], recv_sem.at[9])
        for half, k in ((0, 1), (1, 3)):
            piece = gx.at[at_z(4 - k), half * (DP // 2):(half + 1) * (DP // 2)]
            start(piece, piece, "tensor", at_z(k) * NY + y, send_sem.at[14], recv_sem.at[14])

    def chunk_product(k):
        rows = xr[...].reshape(DP * ROWS, KE)
        for i in range(2):
            cols = pl.ds(pl.multiple_of(at_z(k) * ZC + i * (ZC // 2), ZC // 2), ZC // 2)
            product = dot(rows, wqg[:, cols]).astype(BF)
            pq[k, :, :, :, i * (ZC // 2):(i + 1) * (ZC // 2)] = product.reshape(NC, NX, ROWS, ZC // 2)
        start(pq.at[k, 1 - c], pc.at[k], "dp", sibling, pc_send.at[k], pc_recv.at[k])

    def chunk_pair(k):
        drain(pc.at[k], pc_recv.at[k])
        for i in range(NX):
            ps[k, i] = (pq[k, c, i].astype(F32) + pc[k, i].astype(F32)).astype(BF)
        for half, i in ((0, 1), (1, 3)):
            part = ps.at[k, at_x(2), half * (ROWS // 2):(half + 1) * (ROWS // 2)]
            start(part, fr.at[k, half], "dp", at_x(i) * NC + c, fr_send.at[k], fr_recv.at[k])

    def chunk_pass(k):
        drain(fr.at[k], fr_recv.at[k])
        for half, i in ((0, 1), (1, 3)):
            rows = slice(half * (ROWS // 2), (half + 1) * (ROWS // 2))
            total = ps[k, pl.ds(at_x(i), 1), rows].astype(F32) + fr[k, half].astype(F32)[None]
            ps[k, pl.ds(at_x(i), 1), rows] = total.astype(BF)
        for half, i in ((0, 1), (1, 3)):
            start(ps.at[k, at_x(i)], qr.at[k, half], "dp", at_x(i) * NC + c, qr_send.at[k], qr_recv.at[k])

    def chunk_sum(k):
        drain(qr.at[k], qr_recv.at[k])
        total = ps[k, pl.ds(x, 1)][0].astype(F32)
        for i in range(2):
            total += qr[k, i].astype(F32)
        total = jnp.where(g_col >= 0, 0.0, total).astype(BF)
        for i in range(NY):
            q0s[k, i] = total[:, i * HEAD:(i + 1) * HEAD]
        for i in range(NY):
            if k > 0 or i > 0:
                start(q0s.at[k, at_y(i)], q0r.at[t], "tensor", at_z(k) * NY + at_y(i), send_sem.at[13], q0_recv.at[k])
        if k == 0:
            q0r[pl.ds(t, 1)] = q0s[0, pl.ds(y, 1)]

    drain(wga.at[pl.ds(0, 2)], recv_sem.at[5])
    pass_on(lambda at, half: wga.at[at, half * (KE // 2):(half + 1) * (KE // 2)], 23)
    pass_gx()
    send_piece(2)
    send_piece(3)
    send_piece(4)
    send_piece(5)
    send_piece(6)
    send_piece(7)
    own_wd.wait()
    for k in (1, 3):
        start(wda.at[y], wda.at[y], "tensor", z * NY + at_y(k), send_sem.at[10], recv_sem.at[10])
    drain(wqg.at[:, pl.ds(0, HEAD)], recv_sem.at[1])

    def send_far():
        far_head = wqg.at[:, aligned(at_z(2) * NY + y, HEAD)]
        for k in near:
            start(far_head, far_head, "tensor", z * NY + at_y(k), send_sem.at[11], recv_sem.at[11])

    def pass_wda():
        drain(wda.at[pl.ds(0, 2)], recv_sem.at[10])
        pass_on(lambda at, half: wda.at[at, half * (UNITS // 2):(half + 1) * (UNITS // 2)], 25)


    own_n0.wait()
    drain(n0.at[pl.ds(0, DP - 1)], recv_sem.at[3])
    chunk_product(0)
    chunk_pair(0)

    drain(wga.at[0], recv_sem.at[23])
    chunk_pass(0)
    drain(gx.at[0], recv_sem.at[14])
    rows = gx[...].reshape(NZ * LINE, KE)
    for i in range(NY):
        gp[i // 2, :, :, :, i % 2 * 2 * UNITS:(i % 2 + 1) * 2 * UNITS] = dot(rows, wga[i]).reshape(NC, NX, BLK, 2 * UNITS)
        if i % 2 == 1:
            start(gp.at[i // 2, 1 - c], gc.at[i // 2], "dp", sibling, gc_send.at[i // 2], gc_recv.at[i // 2])
    for h in range(2):
        drain(gc.at[h], gc_recv.at[h])
        for i in range(NX):
            gs[h, i] = (gp[h, c, i] + gc[h, i]).astype(BF)
        for k in near:
            start(gs.at[h, at_x(k)], gr.at[h, k - 1], "dp", at_x(k) * NC + c, gs_send.at[h], gs_recv.at[h])
    pass_wda()
    send_far()
    for h in range(2):
        drain(gr.at[h], gs_recv.at[h])
        total = gp[h, pl.ds(c, 1), pl.ds(x, 1)][0, 0] + gc[h, pl.ds(x, 1)][0]
        for i in range(NX - 1):
            total += gr[h, i].astype(F32)
        for i in range(NY // 2):
            gate = total[:, i * 2 * UNITS:i * 2 * UNITS + UNITS]
            up = total[:, i * 2 * UNITS + UNITS:(i + 1) * 2 * UNITS]
            units = (gate / (1.0 + jnp.exp(-gate)) * up).astype(BF)
            hid[h, pl.ds(c, 1), pl.ds(x, 1), :, i * UNITS:(i + 1) * UNITS] = units[None, None]
        for k in near:
            start(hid.at[h, c, x], hid.at[h, c, x], "dp", at_x(k) * NC + c, hx_send.at[h], hx_recv.at[h])
    for h in range(2):
        drain(hid.at[h, 0, pl.ds(0, NX - 1)], hx_recv.at[h])
        start(hid.at[h, c], hid.at[h, c], "dp", sibling, hc_send.at[h], hc_recv.at[h])
    drain(wda.at[0], recv_sem.at[25])
    for h in range(2):
        drain(hid.at[h, 0], hc_recv.at[h])
    hidden = [hid[h].reshape(NZ * LINE, NY * UNITS // 2) for h in range(2)]
    down = wda[...].reshape(2, NY * UNITS // 2, KE)
    for h in range(2):
        for i in range(tile // 256):
            at = h * tile + i * 256
            dn[h, :, :, i * 256:(i + 1) * 256] = (dot(hidden[0], down[0, :, at:at + 256]) + dot(hidden[1], down[1, :, at:at + 256])).astype(BF).reshape(NZ, LINE, 256)
        for k in near:
            start(dn.at[h, at_z(k)], dr.at[h, k - 1], "tensor", at_z(k) * NY + y, dn_send.at[h], dn_recv.at[h])
    chunk_sum(0)
    drain(wqg.at[:, pl.ds(0, ZC)], recv_sem.at[8])
    chunk_product(1)
    chunk_pair(1)
    drain(wqg.at[:, pl.ds(0, ZC)], recv_sem.at[6])
    chunk_product(3)
    def mix_half(h):
        drain(dr.at[h], dn_recv.at[h])
        branch = dn[h, pl.ds(z, 1)][0].astype(F32)
        for i in range(NZ - 1):
            branch += dr[h, i].astype(F32)
        cols = slice(h * tile, (h + 1) * tile)
        mixed = (raw[:, cols].astype(F32) + line_weight * branch).astype(BF)
        ms[h] = mixed.reshape(DP, BAL, tile)
        spread("dp", DP, d, lambda peer: ms.at[h, peer], mb.at[h, d], ms_send.at[h], ms_recv.at[h])
        mb[h, pl.ds(d, 1)] = ms[h, pl.ds(d, 1)]
        gain = gnx_ref[:, pl.ds(pl.multiple_of(d * KE + h * tile, tile), tile)]
        return (mixed.astype(F32) * gain).astype(BF)

    def return_half(h):
        drain(mb.at[h, pl.ds(0, DP - 1)], ms_recv.at[h])
        for i in range(per):
            stacked = jnp.concatenate([mb[h, q * per + i] for q in range(QN)], axis=0)
            rts[h, :, i * tile:(i + 1) * tile] = dot(back[...], stacked).astype(BF)
        spread("tensor", T, t, lambda peer: rts.at[h, aligned(peer, 16), :], rtr.at[h, aligned(t, 16), :], rt_send.at[h], rt_recv.at[h])
        rtr[h, aligned(t, 16), :] = rts[h, aligned(t, 16), :]

    upper_rows = mix_half(0)
    chunk_pair(3)
    chunk_pass(1)
    drain(wqg.at[:, pl.ds(0, 3 * HEAD)], recv_sem.at[11])
    chunk_product(2)
    return_half(0)
    chunk_pass(3)
    rows = jnp.concatenate([upper_rows, mix_half(1)], axis=1)
    for i in range(T // 2):
        cols = slice(i * 2 * HEAD, (i + 1) * 2 * HEAD)
        product = dot(rows, wqg[:, cols]).astype(BF)
        for e in range(DP):
            rp[e % NC, e // NC, :, cols] = product[e * BAL:(e + 1) * BAL]
    start(rp.at[1 - c], rpc, "dp", sibling, send_sem.at[20], recv_sem.at[20])
    chunk_pair(2)
    drain(rpc, recv_sem.at[20])
    for i in range(NX):
        rps[i] = (rp[c, i].astype(F32) + rpc[i].astype(F32)).astype(BF)
    for k in near:
        start(rps.at[at_x(k)], rpr.at[k - 1], "dp", at_x(k) * NC + c, send_sem.at[6], recv_sem.at[24])
    chunk_sum(1)
    chunk_sum(3)
    return_half(1)
    square = jnp.zeros((BAL, 1), F32)
    for h in range(2):
        for e in range(DP):
            wide = mb[h, e].astype(F32)
            square += jnp.sum(wide * wide, axis=1, keepdims=True)
    scale = lax.rsqrt(square / D + EPS)
    chunk_pass(2)
    drain(rpr, recv_sem.at[24])
    total = rps[pl.ds(x, 1)][0].astype(F32)
    for i in range(NX - 1):
        total += rpr[i].astype(F32)
    total = (total * scale).astype(BF)
    for h in range(T):
        rqs[h] = total[:, h * HEAD:(h + 1) * HEAD]
    spread("tensor", T, t, lambda peer: rqs.at[peer], rq.at[t], send_sem.at[22], recv_sem.at[22])
    rq[pl.ds(t, 1)] = rqs[pl.ds(t, 1)]
    chunk_sum(2)
    outs = []

    def place_chunk(k):
        routed = rq[...].reshape(ROUTED, HEAD)
        if k > 0:
            drain(q0r.at[pl.ds(0, NY)], q0_recv.at[k])
        else:
            drain(q0r.at[pl.ds(0, NY - 1)], q0_recv.at[k])
        from_z = at_z((NZ - k) % NZ)
        for i in range(NY):
            o = from_z * NY + i
            moved = dot(spots[pl.ds(o, 1)][0], routed)
            plain = q0r[pl.ds(o, 1)][0].astype(F32)
            qo[aligned(o, ROWS), :] = (moved + plain).astype(BF)
        rows = aligned(from_z, NY * ROWS)
        copy = pltpu.make_async_copy(qo.at[rows, :], query_hbm.at[rows, :], out_sem.at[k])
        copy.start()
        outs.append(copy)

    def place_half(h):
        drain(rtr.at[h, pl.ds(0, (T - 1) * 16), :], rt_recv.at[h])
        for q in range(QN):
            for i in range(per):
                at = q * CW + i * KE + h * tile
                moved = dot(spot_m[q], rtr[h, :, i * tile:(i + 1) * tile]).astype(BF)
                mix[:, at:at + tile] = jnp.where(g_col >= 0, moved, tok[:, at:at + tile])
                cols = pl.ds(at, tile)
                copy = pltpu.make_async_copy(mix.at[:, cols], mixed_hbm.at[:, cols], out_sem.at[NZ + h * QN * per + q * per + i])
                copy.start()
                outs.append(copy)

    place_half(0)
    place_half(1)
    drain(tabs.at[pl.ds(0, T - 1)], send_sem.at[0])
    drain(wqg.at[:, pl.ds(0, HEAD)], send_sem.at[1])
    drain(wqg.at[:, pl.ds(0, 2 * HEAD)], send_sem.at[2])
    drain(n0.at[pl.ds(0, DP - 1)], send_sem.at[3])
    drain(a2s.at[pl.ds(0, (T - 1) * 16), :], send_sem.at[4])
    drain(wga.at[pl.ds(0, 2)], send_sem.at[5])
    drain(wqg.at[:, pl.ds(0, HEAD)], send_sem.at[7])
    drain(wqg.at[:, pl.ds(0, 2 * ZC)], send_sem.at[8])
    drain(wga.at[0], send_sem.at[23])
    drain(gx.at[pl.ds(0, 2)], send_sem.at[9])
    drain(gx.at[0], send_sem.at[14])
    drain(wda.at[pl.ds(0, 2)], send_sem.at[10])
    drain(wda.at[0], send_sem.at[25])
    drain(wqg.at[:, pl.ds(0, 3 * HEAD)], send_sem.at[11])
    drain(rws.at[pl.ds(0, DP - 1)], send_sem.at[12])
    for h in range(2):
        drain(gc.at[h], gc_send.at[h])
        drain(gr.at[h], gs_send.at[h])
        drain(hid.at[h, 0, pl.ds(0, NX - 1)], hx_send.at[h])
        drain(hid.at[h, 0], hc_send.at[h])
    for h in range(2):
        drain(dr.at[h], dn_send.at[h])
        drain(ms.at[h, pl.ds(0, DP - 1)], ms_send.at[h])
    drain(rpc, send_sem.at[20])
    for k in range(NZ):
        drain(pc.at[k], pc_send.at[k])
        drain(fr.at[k], fr_send.at[k])
        drain(qr.at[k], qr_send.at[k])
    drain(rq.at[pl.ds(0, T - 1)], recv_sem.at[22])
    place_chunk(0)
    place_chunk(1)
    place_chunk(3)
    place_chunk(2)
    drain(rqs.at[pl.ds(0, T - 1)], send_sem.at[22])
    drain(q0r.at[pl.ds(0, T - 1)], send_sem.at[13])
    drain(rpr, send_sem.at[6])
    for h in range(2):
        drain(rts.at[h, pl.ds(0, (T - 1) * 16), :], rt_send.at[h])
    for copy in outs:
        copy.wait()


def hand_over(mixed, query, mixed_out, query_out, held_mixed, held_query, in_sem, out_sem):
    loads, stores = [], []
    for i in range(PARTS):
        for j, (source, held, target) in enumerate(((mixed, held_mixed, mixed_out), (query, held_query, query_out))):
            n = source.shape[0] // PARTS
            rows = pl.ds(i * n, n)
            loads.append(pltpu.make_async_copy(source.at[rows, :], held.at[rows, :], in_sem.at[2 * i + j]))
            stores.append(pltpu.make_async_copy(held.at[rows, :], target.at[rows, :], out_sem.at[2 * i + j]))
            loads[-1].start()
    for load, store in zip(loads, stores):
        load.wait()
        store.start()
    for store in stores:
        store.wait()


def on_device(tokens, route_order, route_counts, w_router, gain_in, w_gate_up, w_down, gain_next, w_query):
    hbm = pl.BlockSpec(memory_space=pltpu.HBM)
    anywhere = pl.BlockSpec(memory_space=pl.ANY)
    mixed, query = pl.pallas_call(
        kernel,
        out_shape=(
            jax.ShapeDtypeStruct((ROWS, D), BF),
            jax.ShapeDtypeStruct((T * ROWS, HEAD), BF),
        ),
        in_specs=[hbm, pl.BlockSpec(memory_space=pltpu.SMEM)] + [hbm] * 7,
        out_specs=(anywhere, anywhere),
        scratch_shapes=[
            pltpu.VMEM((1, ROWS), I32),
            pltpu.VMEM((D // 128, 128), BF),
            pltpu.VMEM((1, D), F32),
            pltpu.VMEM((1, D), F32),
            pltpu.VMEM((ROWS, D), BF),
            pltpu.VMEM((T, 8, ROWS), I32),
            pltpu.VMEM((ROWS, ROWS), I32),
            pltpu.VMEM((DP, ROWS, KE), BF),
            pltpu.VMEM((NC, NX, ROWS, KE), BF),
            pltpu.VMEM((NY, KE, 2 * UNITS), BF),
            pltpu.VMEM((NY, UNITS, KE), BF),
            pltpu.VMEM((KE, T * HEAD), BF),
            pltpu.VMEM((ROUTED, CW), BF),
            pltpu.VMEM((ROUTED, CW), BF),
            pltpu.VMEM((QN * BAL, CW), F32),
            pltpu.VMEM((NZ, DP, BAL, KE), BF),
            pltpu.VMEM((DP, BAL, KE + 128), BF),
            pltpu.VMEM((DP, BAL, KE + 128), BF),
            pltpu.VMEM((2, NC, NX, BLK, NY * UNITS), F32),
            pltpu.VMEM((2, NX, BLK, NY * UNITS), F32),
            pltpu.VMEM((2, NX, BLK, NY * UNITS), BF),
            pltpu.VMEM((2, NX - 1, BLK, NY * UNITS), BF),
            pltpu.VMEM((2, NC, NX, BLK, NY * UNITS // 2), BF),
            pltpu.VMEM((2, NZ, LINE, KE // 2), BF),
            pltpu.VMEM((2, NZ - 1, LINE, KE // 2), BF),
            pltpu.VMEM((NZ, NC, NX, ROWS, ZC), BF),
            pltpu.VMEM((NZ, NX, ROWS, ZC), BF),
            pltpu.VMEM((NZ, NX, ROWS, ZC), BF),
            pltpu.VMEM((NZ, 2, ROWS // 2, ZC), BF),
            pltpu.VMEM((NZ, 2, ROWS, ZC), BF),
            pltpu.VMEM((NZ, NY, ROWS, HEAD), BF),
            pltpu.VMEM((T, ROWS, HEAD), BF),
            pltpu.VMEM((2, DP, BAL, KE // 2), BF),
            pltpu.VMEM((2, DP, BAL, KE // 2), BF),
            pltpu.VMEM((NC, NX, BAL, T * HEAD), BF),
            pltpu.VMEM((NX, BAL, T * HEAD), BF),
            pltpu.VMEM((NX, BAL, T * HEAD), BF),
            pltpu.VMEM((NX - 1, BAL, T * HEAD), BF),
            pltpu.VMEM((T, BAL, HEAD), BF),
            pltpu.VMEM((T, BAL, HEAD), BF),
            pltpu.VMEM((2, ROUTED, CW // 2), BF),
            pltpu.VMEM((2, ROUTED, CW // 2), BF),
            pltpu.VMEM((ROWS, D), BF),
            pltpu.VMEM((T * ROWS, HEAD), BF),
            pltpu.VMEM((T, ROWS, ROUTED), BF),
            pltpu.VMEM((QN, ROWS, ROUTED), BF),
            pltpu.VMEM((ROUTED, QN * BAL), BF),
            pltpu.SemaphoreType.DMA((9,)),
            pltpu.SemaphoreType.DMA((26,)),
            pltpu.SemaphoreType.DMA((26,)),
            pltpu.SemaphoreType.DMA((NZ,)),
            pltpu.SemaphoreType.DMA((NZ,)),
            pltpu.SemaphoreType.DMA((NZ,)),
            pltpu.SemaphoreType.DMA((NZ,)),
            pltpu.SemaphoreType.DMA((NZ,)),
            pltpu.SemaphoreType.DMA((NZ,)),
            pltpu.SemaphoreType.DMA((NZ,)),
            pltpu.SemaphoreType.DMA((NZ + 2 * QN * (CW // KE),)),
            pltpu.SemaphoreType.DMA((2,)),
            pltpu.SemaphoreType.DMA((2,)),
            pltpu.SemaphoreType.DMA((2,)),
            pltpu.SemaphoreType.DMA((2,)),
            pltpu.SemaphoreType.DMA((2,)),
            pltpu.SemaphoreType.DMA((2,)),
            pltpu.SemaphoreType.DMA((2,)),
            pltpu.SemaphoreType.DMA((2,)),
            pltpu.SemaphoreType.DMA((2,)),
            pltpu.SemaphoreType.DMA((2,)),
            pltpu.SemaphoreType.DMA((2,)),
            pltpu.SemaphoreType.DMA((2,)),
            pltpu.SemaphoreType.DMA((2,)),
            pltpu.SemaphoreType.DMA((2,)),
        ],
        compiler_params=pltpu.CompilerParams(
            collective_id=0, has_side_effects=True, vmem_limit_bytes=LIMIT * 1024 * 1024
        ),
    )(
        route_order, route_counts, w_router.reshape(D // 128, 128), gain_in.reshape(1, D), gain_next.reshape(1, D),
        tokens, w_gate_up, w_down, w_query,
    )
    return pl.pallas_call(
        hand_over,
        out_shape=(
            jax.ShapeDtypeStruct((ROWS, D), BF),
            jax.ShapeDtypeStruct((T * ROWS, HEAD), BF),
        ),
        in_specs=[anywhere] * 2,
        out_specs=(anywhere, anywhere),
        scratch_shapes=[
            pltpu.VMEM((ROWS, D), BF),
            pltpu.VMEM((T * ROWS, HEAD), BF),
            pltpu.SemaphoreType.DMA((2 * PARTS,)),
            pltpu.SemaphoreType.DMA((2 * PARTS,)),
        ],
    )(mixed, query)


def solution(mesh):
    in_specs = (
        P(("dp", "tensor"), None),
        P(("dp", "tensor"), None),
        P(("dp", "tensor")),
        P(),
        P(),
        P(None, "tensor"),
        P("tensor", None),
        P(),
        P(None, "tensor"),
    )
    out_specs = (P(("dp", "tensor"), None), P("dp", "tensor"))
    return jax.shard_map(
        on_device, mesh=mesh, in_specs=in_specs, out_specs=out_specs, check_vma=False
    )
```

```python
import jax
import jax.numpy as jnp
from jax import lax
from jax.experimental import pallas as pl
from jax.experimental.pallas import tpu as pltpu
from jax.sharding import PartitionSpec as P

T = 16
DP = 8
D = 8192
ROWS = 128
HEAD = 128
UNITS = 128
QN = 4
CW = D // QN
KE = D // DP
ROUTED = 256
BAL = ROUTED // T
NZ = 4
NY = 4
NX = 4
NC = 2
LINE = DP * BAL
ZC = NY * HEAD
BLK = NZ * LINE // DP
LIMIT = 60
PARTS = 4
EPS = 1e-05
MESH = pl.DeviceIdType.MESH
BF = jnp.bfloat16
F32 = jnp.float32
I32 = jnp.int32


def start(source, target, axis, peer, send_sem, recv_sem):
    pltpu.make_async_remote_copy(
        src_ref=source,
        dst_ref=target,
        send_sem=send_sem,
        recv_sem=recv_sem,
        device_id={axis: peer},
        device_id_type=MESH,
    ).start()


def spread(axis, size, me, source, target, send_sem, recv_sem):
    def body(k, carry):
        peer = lax.rem(me + k, size)
        start(source(peer), target, axis, peer, send_sem, recv_sem)
        return carry

    lax.fori_loop(1, size, body, 0)


def drain(view, sem):
    pltpu.make_async_copy(view, view, sem).wait()


def iota(shape, dim):
    return lax.broadcasted_iota(I32, shape, dim)


def dot(a, b):
    return jnp.dot(a, b, preferred_element_type=F32)


def one_hot(mask):
    return jnp.where(mask, 1.0, 0.0).astype(BF)


def aligned(at, size):
    return pl.ds(pl.multiple_of(at * size, size), size)


def column_of(row):
    eye = iota((ROWS, ROWS), 0) == iota((ROWS, ROWS), 1)
    return jnp.sum(jnp.where(eye, row.astype(F32), 0.0), axis=1, keepdims=True).astype(I32)


def kernel(
    order_hbm, count_ref, wr_hbm, gin_hbm, gnx_hbm, tok_hbm, wgu_hbm, wd_hbm, wq_hbm,
    mixed_hbm, query_hbm,
    order_ref, wr_ref, gin_ref, gnx_ref, tok, tabs, offs, n0, xr, wga, wda, wqg, a2s, a2r, xb, gx, rws, rwr,
    gp, gc, gs, gr, hid, dn, dr, pq, pc, ps, fr, qr, q0s, q0r, ms, mb, rp, rpc, rps, rpr, rqs, rq,
    rts, rtr, mix, qo, spots, spot_m, back,
    local_sem, send_sem, recv_sem, pc_send, pc_recv, fr_send, fr_recv, qr_send, qr_recv, q0_recv, out_sem,
    gc_send, gc_recv, gs_send, gs_recv, hx_send, hx_recv, hc_send, hc_recv,
    dn_send, dn_recv, ms_send, ms_recv, rt_send, rt_recv,
):
    t = lax.axis_index("tensor")
    d = lax.axis_index("dp")
    z, y = lax.div(t, NY), lax.rem(t, NY)
    x, c = lax.div(d, NC), lax.rem(d, NC)
    sibling = x * NC + 1 - c
    near = (2, 1, 3)
    tile = 512
    per = CW // KE

    def at_y(k):
        return lax.rem(y + k, NY)

    def at_z(k):
        return lax.rem(z + k, NZ)

    def at_x(k):
        return lax.rem(x + k, NX)

    def pass_on(part, sem):
        for half, k in ((0, 1), (1, 3)):
            piece = part(at_y(4 - k), half)
            start(piece, piece, "tensor", z * NY + at_y(k), send_sem.at[sem], recv_sem.at[sem])

    my_k = aligned(d, KE)
    wq_own = wq_hbm.at[my_k, :]
    load_order = pltpu.make_async_copy(order_hbm, order_ref, local_sem.at[5])
    load_order.start()
    load_tok = pltpu.make_async_copy(tok_hbm, tok, local_sem.at[0])
    load_tok.start()
    load_gnx = pltpu.make_async_copy(gnx_hbm, gnx_ref, local_sem.at[6])
    load_gnx.start()
    load_gin = pltpu.make_async_copy(gin_hbm, gin_ref, local_sem.at[7])
    load_gin.start()
    load_wr = pltpu.make_async_copy(wr_hbm, wr_ref, local_sem.at[8])
    load_wr.start()
    own_wg = pltpu.make_async_copy(wgu_hbm.at[my_k, :], wga.at[y], local_sem.at[1])
    own_wg.start()
    own_wd = pltpu.make_async_copy(wd_hbm.at[:, my_k], wda.at[y], local_sem.at[2])
    own_wd.start()
    own_wq = pltpu.make_async_copy(wq_own, wqg.at[:, aligned(t, HEAD)], local_sem.at[3])
    own_wq.start()

    barrier = pltpu.get_barrier_semaphore()

    def greet_t(k, carry):
        pl.semaphore_signal(barrier, inc=1, device_id={"tensor": lax.rem(t + k, T)}, device_id_type=MESH)
        return carry

    def greet_d(k, carry):
        pl.semaphore_signal(barrier, inc=1, device_id={"dp": lax.rem(d + k, DP)}, device_id_type=MESH)
        return carry

    lax.fori_loop(1, T, greet_t, 0)
    lax.fori_loop(1, DP, greet_d, 0)

    count = count_ref[0]
    slot = iota((8, ROWS), 1)
    values = jnp.where(slot < count, slot + 1, 0).astype(F32).astype(BF)
    load_order.wait()
    pairs = one_hot(iota((ROWS, ROWS), 0) == order_ref[...])
    own = lax.dot_general(values, pairs, (((1,), (1,)), ((), ())), preferred_element_type=F32)
    tabs[pl.ds(t, 1)] = (own.astype(I32) - 1)[None]

    load_tok.wait()
    load_gnx.wait()
    square = jnp.zeros((ROWS, 1), F32)
    for e in range(DP):
        wide = tok[:, e * KE:(e + 1) * KE].astype(F32)
        square += jnp.sum(wide * wide, axis=1, keepdims=True)
    scale = lax.rsqrt(square / D + EPS)
    for e in range(DP):
        cols = slice(e * KE, (e + 1) * KE)
        n0[e] = (tok[:, cols].astype(F32) * scale * gnx_ref[:, cols]).astype(BF)
    pl.semaphore_wait(barrier, T - 1 + DP - 1)
    spread("tensor", T, t, lambda peer: tabs.at[t], tabs.at[t], send_sem.at[0], recv_sem.at[0])

    start(wq_own, wqg.at[:, aligned(t, HEAD)], "tensor", at_z(2) * NY + y, send_sem.at[1], recv_sem.at[1])
    for k in (1, 3):
        start(wq_own, wqg.at[:, aligned(t, HEAD)], "tensor", z * NY + at_y(k), send_sem.at[2], recv_sem.at[2])

    my_n0 = xr.at[c, x]
    for k in (1, 3):
        for i in range(NC):
            peer = at_x(k) * NC + i
            start(n0.at[peer], my_n0, "dp", peer, send_sem.at[3], recv_sem.at[3])
    start(n0.at[sibling], my_n0, "dp", sibling, send_sem.at[3], recv_sem.at[3])

    def far_n0(i):
        peer = at_x(2) * NC + i
        start(n0.at[peer], my_n0, "dp", peer, send_sem.at[3], recv_sem.at[3])

    own_n0 = pltpu.make_async_copy(n0.at[d], my_n0, local_sem.at[4])
    own_n0.start()
    far_n0(c)
    drain(tabs.at[pl.ds(0, T - 1)], recv_sem.at[0])
    marks = one_hot(tabs[...].reshape(T * 8, ROWS) >= 0)
    counts = dot(marks, jnp.ones((ROWS, ROWS), BF))
    sub, lane = iota((ROWS, ROWS), 0), iota((ROWS, ROWS), 1)
    before = one_hot(((lane // 8) < (sub // 8)) & (lane % 8 == 0))
    firsts = dot(before, counts.astype(BF))
    firsts_i, counts_i = firsts.astype(I32), counts.astype(I32)
    offs[...] = firsts_i

    my_first = offs[aligned(t, 8), :][:1]
    my_slots = tabs[pl.ds(t, 1)][0, :1]
    g_row = jnp.where(my_slots >= 0, my_slots + my_first, -1)
    j = iota((ROUTED, ROWS), 0)
    hit = ((j // 16) == (g_row % 16)) & ((j % 4) == ((g_row // 16) % 4)) & (g_row >= 0)
    pick = jnp.concatenate([one_hot(hit & (((j // 4) % 4) == q)) for q in range(QN)], axis=1)
    for i in range(CW // tile):
        stacked = jnp.concatenate([tok[:, q * CW + i * tile:q * CW + (i + 1) * tile] for q in range(QN)], axis=0)
        a2s[:, i * tile:(i + 1) * tile] = dot(pick, stacked).astype(BF)
    spread("tensor", T, t, lambda peer: a2s.at[aligned(peer, 16), :], a2r.at[aligned(t, 16), :], send_sem.at[4], recv_sem.at[4])
    a2r[aligned(t, 16), :] = a2s[aligned(t, 16), :]

    drain(wqg.at[:, pl.ds(0, 2 * HEAD)], recv_sem.at[2])
    pass_on(lambda at, half: wqg.at[half * (KE // 2):(half + 1) * (KE // 2), aligned(z * NY + at, HEAD)], 7)

    own_wg.wait()
    for k in (1, 3):
        start(wga.at[y], wga.at[y], "tensor", z * NY + at_y(k), send_sem.at[5], recv_sem.at[5])

    first_l, last_l = [], []
    for half in range(2):
        group = iota((8, ROWS), 1) // 16
        lo, hi = jnp.zeros((8, ROWS), I32), jnp.zeros((8, ROWS), I32)
        for i in range(8):
            o = half * 8 + i
            f = firsts_i[o * 8:(o + 1) * 8]
            n = counts_i[o * 8:(o + 1) * 8]
            lo = jnp.where(group == i, f, lo)
            hi = jnp.where(group == i, f + n, hi)
        first_l.append(lo)
        last_l.append(hi)
    first_l = jnp.concatenate(first_l, axis=1)[:1]
    last_l = jnp.concatenate(last_l, axis=1)[:1]
    bi, bj = iota((QN * BAL, ROUTED), 0), iota((QN * BAL, ROUTED), 1)
    g_bal = (bi % BAL) * T + t
    compact = one_hot(
        ((bi // BAL) == ((bj // 4) % 4)) & ((bj % 4) == (bi % 4)) & (first_l <= g_bal) & (g_bal < last_l)
    )
    ri, rj = iota((16, QN * BAL), 0), iota((16, QN * BAL), 1)
    g_bal = (rj % BAL) * T + t
    fits = ((rj // BAL) == (ri // 4)) & ((rj % 4) == (ri % 4))
    for o in range(T):
        lo = jnp.concatenate([firsts_i[o * 8:(o + 1) * 8, :QN * BAL]] * 2, axis=0)
        n = jnp.concatenate([counts_i[o * 8:(o + 1) * 8, :QN * BAL]] * 2, axis=0)
        back[o * 16:(o + 1) * 16, :] = one_hot(fits & (lo <= g_bal) & (g_bal < lo + n))
    g_col = column_of(g_row)
    jl = iota((ROWS, ROUTED), 1)
    hit = ((jl // 16) == (g_col % 16)) & ((jl % 4) == ((g_col // 16) % 4)) & (g_col >= 0)
    for q in range(QN):
        spot_m[q] = one_hot(hit & (((jl // 4) % 4) == q))
    g_lane = (jl % 16) * T + jl // 16

    def find_owner(o, carry):
        slots = tabs[pl.ds(o, 1)][0, :1]
        lo = offs[aligned(o, 8), :][:1]
        col = column_of(jnp.where(slots >= 0, slots + lo, -1))
        spots[pl.ds(o, 1)] = one_hot(col == g_lane)[None]
        return carry

    lax.fori_loop(0, T, find_owner, 0)

    load_gin.wait()
    load_wr.wait()
    drain(a2r.at[pl.ds(0, (T - 1) * 16), :], recv_sem.at[4])
    xb[...] = dot(compact, a2r[...])
    square, logit = jnp.zeros((BAL, 128), F32), jnp.zeros((BAL, 128), F32)
    for q in range(QN):
        rows = xb[q * BAL:(q + 1) * BAL]
        for h in range(per):
            rws[q * per + h, :, :KE] = rows[:, h * KE:(h + 1) * KE].astype(BF)
        for i in range(CW // 128):
            part = rows[:, i * 128:(i + 1) * 128]
            at = q * (CW // 128) + i
            square += part * part
            logit += part * wr_ref[at:at + 1, :].astype(F32)
    scale = lax.rsqrt(jnp.sum(square, axis=1, keepdims=True) / D + EPS)
    weight = 1.0 / (1.0 + jnp.exp(-jnp.sum(logit, axis=1, keepdims=True)))
    terms = []
    for value in (scale, weight):
        for i in range(3):
            terms.append(value.astype(BF).astype(F32))
            value = value - terms[-1]
    at = iota((BAL, 128), 1)
    tail = jnp.zeros((BAL, 128), F32)
    for i in range(6):
        tail = jnp.where(at == i, terms[i], tail)
    for e in range(DP):
        rws[e, :, KE:] = tail.astype(BF)
    spread("dp", DP, d, lambda peer: rws.at[peer], rwr.at[d], send_sem.at[12], recv_sem.at[12])
    rwr[pl.ds(d, 1)] = rws[pl.ds(d, 1)]

    own_wq.wait()
    drain(wqg.at[:, pl.ds(0, HEAD)], recv_sem.at[7])

    def send_piece(i):
        piece = wqg.at[i * (KE // 8):(i + 1) * (KE // 8), aligned(z, ZC)]
        for k in (1, 3):
            start(piece, piece, "tensor", at_z(k) * NY + y, send_sem.at[8], recv_sem.at[8 if k == 3 else 6])

    send_piece(0)

    drain(rwr.at[pl.ds(0, DP - 1)], recv_sem.at[12])
    far_n0(1 - c)
    raw = rwr[...].reshape(LINE, KE + 128)
    both = raw[:, KE:].astype(F32)
    scale = both[:, :1] + both[:, 1:2] + both[:, 2:3]
    line_weight = both[:, 3:4] + both[:, 4:5] + both[:, 5:6]
    normed = (raw[:, :KE].astype(F32) * scale * gin_ref[:, my_k]).astype(BF)
    gx[pl.ds(z, 1)] = normed.reshape(1, DP, BAL, KE)
    for k in (1, 3):
        start(gx.at[z], gx.at[z], "tensor", at_z(k) * NY + y, send_sem.at[9], recv_sem.at[9])
    send_piece(1)

    def pass_gx():
        drain(gx.at[pl.ds(0, 2)], recv_sem.at[9])
        for half, k in ((0, 1), (1, 3)):
            piece = gx.at[at_z(4 - k), half * (DP // 2):(half + 1) * (DP // 2)]
            start(piece, piece, "tensor", at_z(k) * NY + y, send_sem.at[14], recv_sem.at[14])

    def chunk_product(k):
        rows = xr[...].reshape(DP * ROWS, KE)
        for i in range(2):
            cols = pl.ds(pl.multiple_of(at_z(k) * ZC + i * (ZC // 2), ZC // 2), ZC // 2)
            product = dot(rows, wqg[:, cols]).astype(BF)
            pq[k, :, :, :, i * (ZC // 2):(i + 1) * (ZC // 2)] = product.reshape(NC, NX, ROWS, ZC // 2)
        start(pq.at[k, 1 - c], pc.at[k], "dp", sibling, pc_send.at[k], pc_recv.at[k])

    def chunk_pair(k):
        drain(pc.at[k], pc_recv.at[k])
        for i in range(NX):
            ps[k, i] = (pq[k, c, i].astype(F32) + pc[k, i].astype(F32)).astype(BF)
        for half, i in ((0, 1), (1, 3)):
            part = ps.at[k, at_x(2), half * (ROWS // 2):(half + 1) * (ROWS // 2)]
            start(part, fr.at[k, half], "dp", at_x(i) * NC + c, fr_send.at[k], fr_recv.at[k])

    def chunk_pass(k):
        drain(fr.at[k], fr_recv.at[k])
        for half, i in ((0, 1), (1, 3)):
            rows = slice(half * (ROWS // 2), (half + 1) * (ROWS // 2))
            total = ps[k, pl.ds(at_x(i), 1), rows].astype(F32) + fr[k, half].astype(F32)[None]
            ps[k, pl.ds(at_x(i), 1), rows] = total.astype(BF)
        for half, i in ((0, 1), (1, 3)):
            start(ps.at[k, at_x(i)], qr.at[k, half], "dp", at_x(i) * NC + c, qr_send.at[k], qr_recv.at[k])

    def chunk_sum(k):
        drain(qr.at[k], qr_recv.at[k])
        total = ps[k, pl.ds(x, 1)][0].astype(F32)
        for i in range(2):
            total += qr[k, i].astype(F32)
        total = jnp.where(g_col >= 0, 0.0, total).astype(BF)
        for i in range(NY):
            q0s[k, i] = total[:, i * HEAD:(i + 1) * HEAD]
        for i in range(NY):
            if k > 0 or i > 0:
                start(q0s.at[k, at_y(i)], q0r.at[t], "tensor", at_z(k) * NY + at_y(i), send_sem.at[13], q0_recv.at[k])
        if k == 0:
            q0r[pl.ds(t, 1)] = q0s[0, pl.ds(y, 1)]

    drain(wga.at[pl.ds(0, 2)], recv_sem.at[5])
    pass_on(lambda at, half: wga.at[at, half * (KE // 2):(half + 1) * (KE // 2)], 23)
    pass_gx()
    send_piece(2)
    send_piece(3)
    send_piece(4)
    send_piece(5)
    send_piece(6)
    send_piece(7)
    own_wd.wait()
    for k in (1, 3):
        start(wda.at[y], wda.at[y], "tensor", z * NY + at_y(k), send_sem.at[10], recv_sem.at[10])
    drain(wqg.at[:, pl.ds(0, HEAD)], recv_sem.at[1])

    def send_far():
        far_head = wqg.at[:, aligned(at_z(2) * NY + y, HEAD)]
        for k in near:
            start(far_head, far_head, "tensor", z * NY + at_y(k), send_sem.at[11], recv_sem.at[11])

    def pass_wda():
        drain(wda.at[pl.ds(0, 2)], recv_sem.at[10])
        pass_on(lambda at, half: wda.at[at, half * (UNITS // 2):(half + 1) * (UNITS // 2)], 25)


    own_n0.wait()
    drain(n0.at[pl.ds(0, DP - 1)], recv_sem.at[3])
    chunk_product(0)
    chunk_pair(0)

    drain(wga.at[0], recv_sem.at[23])
    chunk_pass(0)
    drain(gx.at[0], recv_sem.at[14])
    rows = gx[...].reshape(NZ * LINE, KE)
    for i in range(NY):
        gp[i // 2, :, :, :, i % 2 * 2 * UNITS:(i % 2 + 1) * 2 * UNITS] = dot(rows, wga[i]).astype(BF).reshape(NC, NX, BLK, 2 * UNITS)
        if i % 2 == 1:
            start(gp.at[i // 2, 1 - c], gc.at[i // 2], "dp", sibling, gc_send.at[i // 2], gc_recv.at[i // 2])
    for h in range(2):
        drain(gc.at[h], gc_recv.at[h])
        for i in range(NX):
            gs[h, i] = (gp[h, c, i].astype(F32) + gc[h, i].astype(F32)).astype(BF)
        for k in near:
            start(gs.at[h, at_x(k)], gr.at[h, k - 1], "dp", at_x(k) * NC + c, gs_send.at[h], gs_recv.at[h])
    pass_wda()
    send_far()
    for h in range(2):
        drain(gr.at[h], gs_recv.at[h])
        total = gp[h, pl.ds(c, 1), pl.ds(x, 1)][0, 0].astype(F32) + gc[h, pl.ds(x, 1)][0].astype(F32)
        for i in range(NX - 1):
            total += gr[h, i].astype(F32)
        for i in range(NY // 2):
            gate = total[:, i * 2 * UNITS:i * 2 * UNITS + UNITS]
            up = total[:, i * 2 * UNITS + UNITS:(i + 1) * 2 * UNITS]
            units = (gate / (1.0 + jnp.exp(-gate)) * up).astype(BF)
            hid[h, pl.ds(c, 1), pl.ds(x, 1), :, i * UNITS:(i + 1) * UNITS] = units[None, None]
        for k in near:
            start(hid.at[h, c, x], hid.at[h, c, x], "dp", at_x(k) * NC + c, hx_send.at[h], hx_recv.at[h])
    for h in range(2):
        drain(hid.at[h, 0, pl.ds(0, NX - 1)], hx_recv.at[h])
        start(hid.at[h, c], hid.at[h, c], "dp", sibling, hc_send.at[h], hc_recv.at[h])
    drain(wda.at[0], recv_sem.at[25])
    for h in range(2):
        drain(hid.at[h, 0], hc_recv.at[h])
    hidden = [hid[h].reshape(NZ * LINE, NY * UNITS // 2) for h in range(2)]
    down = wda[...].reshape(2, NY * UNITS // 2, KE)
    for h in range(2):
        for i in range(tile // 256):
            at = h * tile + i * 256
            dn[h, :, :, i * 256:(i + 1) * 256] = (dot(hidden[0], down[0, :, at:at + 256]) + dot(hidden[1], down[1, :, at:at + 256])).astype(BF).reshape(NZ, LINE, 256)
        for k in near:
            start(dn.at[h, at_z(k)], dr.at[h, k - 1], "tensor", at_z(k) * NY + y, dn_send.at[h], dn_recv.at[h])
    chunk_sum(0)
    drain(wqg.at[:, pl.ds(0, ZC)], recv_sem.at[8])
    chunk_product(1)
    chunk_pair(1)
    drain(wqg.at[:, pl.ds(0, ZC)], recv_sem.at[6])
    chunk_product(3)
    def mix_half(h):
        drain(dr.at[h], dn_recv.at[h])
        branch = dn[h, pl.ds(z, 1)][0].astype(F32)
        for i in range(NZ - 1):
            branch += dr[h, i].astype(F32)
        cols = slice(h * tile, (h + 1) * tile)
        mixed = (raw[:, cols].astype(F32) + line_weight * branch).astype(BF)
        ms[h] = mixed.reshape(DP, BAL, tile)
        spread("dp", DP, d, lambda peer: ms.at[h, peer], mb.at[h, d], ms_send.at[h], ms_recv.at[h])
        mb[h, pl.ds(d, 1)] = ms[h, pl.ds(d, 1)]
        gain = gnx_ref[:, pl.ds(pl.multiple_of(d * KE + h * tile, tile), tile)]
        return (mixed.astype(F32) * gain).astype(BF)

    def return_half(h):
        drain(mb.at[h, pl.ds(0, DP - 1)], ms_recv.at[h])
        for i in range(per):
            stacked = jnp.concatenate([mb[h, q * per + i] for q in range(QN)], axis=0)
            rts[h, :, i * tile:(i + 1) * tile] = dot(back[...], stacked).astype(BF)
        spread("tensor", T, t, lambda peer: rts.at[h, aligned(peer, 16), :], rtr.at[h, aligned(t, 16), :], rt_send.at[h], rt_recv.at[h])
        rtr[h, aligned(t, 16), :] = rts[h, aligned(t, 16), :]

    upper_rows = mix_half(0)
    chunk_pair(3)
    chunk_pass(1)
    drain(wqg.at[:, pl.ds(0, 3 * HEAD)], recv_sem.at[11])
    chunk_product(2)
    return_half(0)
    chunk_pass(3)
    rows = jnp.concatenate([upper_rows, mix_half(1)], axis=1)
    for i in range(T // 2):
        cols = slice(i * 2 * HEAD, (i + 1) * 2 * HEAD)
        product = dot(rows, wqg[:, cols]).astype(BF)
        for e in range(DP):
            rp[e % NC, e // NC, :, cols] = product[e * BAL:(e + 1) * BAL]
    start(rp.at[1 - c], rpc, "dp", sibling, send_sem.at[20], recv_sem.at[20])
    chunk_pair(2)
    drain(rpc, recv_sem.at[20])
    for i in range(NX):
        rps[i] = (rp[c, i].astype(F32) + rpc[i].astype(F32)).astype(BF)
    for k in near:
        start(rps.at[at_x(k)], rpr.at[k - 1], "dp", at_x(k) * NC + c, send_sem.at[6], recv_sem.at[24])
    chunk_sum(1)
    chunk_sum(3)
    return_half(1)
    square = jnp.zeros((BAL, 1), F32)
    for h in range(2):
        for e in range(DP):
            wide = mb[h, e].astype(F32)
            square += jnp.sum(wide * wide, axis=1, keepdims=True)
    scale = lax.rsqrt(square / D + EPS)
    chunk_pass(2)
    drain(rpr, recv_sem.at[24])
    total = rps[pl.ds(x, 1)][0].astype(F32)
    for i in range(NX - 1):
        total += rpr[i].astype(F32)
    total = (total * scale).astype(BF)
    for h in range(T):
        rqs[h] = total[:, h * HEAD:(h + 1) * HEAD]
    spread("tensor", T, t, lambda peer: rqs.at[peer], rq.at[t], send_sem.at[22], recv_sem.at[22])
    rq[pl.ds(t, 1)] = rqs[pl.ds(t, 1)]
    chunk_sum(2)
    outs = []

    def place_chunk(k):
        routed = rq[...].reshape(ROUTED, HEAD)
        if k > 0:
            drain(q0r.at[pl.ds(0, NY)], q0_recv.at[k])
        else:
            drain(q0r.at[pl.ds(0, NY - 1)], q0_recv.at[k])
        from_z = at_z((NZ - k) % NZ)
        for i in range(NY):
            o = from_z * NY + i
            moved = dot(spots[pl.ds(o, 1)][0], routed)
            plain = q0r[pl.ds(o, 1)][0].astype(F32)
            qo[aligned(o, ROWS), :] = (moved + plain).astype(BF)
        rows = aligned(from_z, NY * ROWS)
        copy = pltpu.make_async_copy(qo.at[rows, :], query_hbm.at[rows, :], out_sem.at[k])
        copy.start()
        outs.append(copy)

    def place_half(h):
        drain(rtr.at[h, pl.ds(0, (T - 1) * 16), :], rt_recv.at[h])
        for q in range(QN):
            for i in range(per):
                at = q * CW + i * KE + h * tile
                moved = dot(spot_m[q], rtr[h, :, i * tile:(i + 1) * tile]).astype(BF)
                mix[:, at:at + tile] = jnp.where(g_col >= 0, moved, tok[:, at:at + tile])
                cols = pl.ds(at, tile)
                copy = pltpu.make_async_copy(mix.at[:, cols], mixed_hbm.at[:, cols], out_sem.at[NZ + h * QN * per + q * per + i])
                copy.start()
                outs.append(copy)

    place_half(0)
    place_half(1)
    drain(tabs.at[pl.ds(0, T - 1)], send_sem.at[0])
    drain(wqg.at[:, pl.ds(0, HEAD)], send_sem.at[1])
    drain(wqg.at[:, pl.ds(0, 2 * HEAD)], send_sem.at[2])
    drain(n0.at[pl.ds(0, DP - 1)], send_sem.at[3])
    drain(a2s.at[pl.ds(0, (T - 1) * 16), :], send_sem.at[4])
    drain(wga.at[pl.ds(0, 2)], send_sem.at[5])
    drain(wqg.at[:, pl.ds(0, HEAD)], send_sem.at[7])
    drain(wqg.at[:, pl.ds(0, 2 * ZC)], send_sem.at[8])
    drain(wga.at[0], send_sem.at[23])
    drain(gx.at[pl.ds(0, 2)], send_sem.at[9])
    drain(gx.at[0], send_sem.at[14])
    drain(wda.at[pl.ds(0, 2)], send_sem.at[10])
    drain(wda.at[0], send_sem.at[25])
    drain(wqg.at[:, pl.ds(0, 3 * HEAD)], send_sem.at[11])
    drain(rws.at[pl.ds(0, DP - 1)], send_sem.at[12])
    for h in range(2):
        drain(gc.at[h], gc_send.at[h])
        drain(gr.at[h], gs_send.at[h])
        drain(hid.at[h, 0, pl.ds(0, NX - 1)], hx_send.at[h])
        drain(hid.at[h, 0], hc_send.at[h])
    for h in range(2):
        drain(dr.at[h], dn_send.at[h])
        drain(ms.at[h, pl.ds(0, DP - 1)], ms_send.at[h])
    drain(rpc, send_sem.at[20])
    for k in range(NZ):
        drain(pc.at[k], pc_send.at[k])
        drain(fr.at[k], fr_send.at[k])
        drain(qr.at[k], qr_send.at[k])
    drain(rq.at[pl.ds(0, T - 1)], recv_sem.at[22])
    place_chunk(0)
    place_chunk(1)
    place_chunk(3)
    place_chunk(2)
    drain(rqs.at[pl.ds(0, T - 1)], send_sem.at[22])
    drain(q0r.at[pl.ds(0, T - 1)], send_sem.at[13])
    drain(rpr, send_sem.at[6])
    for h in range(2):
        drain(rts.at[h, pl.ds(0, (T - 1) * 16), :], rt_send.at[h])
    for copy in outs:
        copy.wait()


def hand_over(mixed, query, mixed_out, query_out, held_mixed, held_query, in_sem, out_sem):
    loads, stores = [], []
    for i in range(PARTS):
        for j, (source, held, target) in enumerate(((mixed, held_mixed, mixed_out), (query, held_query, query_out))):
            n = source.shape[0] // PARTS
            rows = pl.ds(i * n, n)
            loads.append(pltpu.make_async_copy(source.at[rows, :], held.at[rows, :], in_sem.at[2 * i + j]))
            stores.append(pltpu.make_async_copy(held.at[rows, :], target.at[rows, :], out_sem.at[2 * i + j]))
            loads[-1].start()
    for load, store in zip(loads, stores):
        load.wait()
        store.start()
    for store in stores:
        store.wait()


def on_device(tokens, route_order, route_counts, w_router, gain_in, w_gate_up, w_down, gain_next, w_query):
    hbm = pl.BlockSpec(memory_space=pltpu.HBM)
    anywhere = pl.BlockSpec(memory_space=pl.ANY)
    mixed, query = pl.pallas_call(
        kernel,
        out_shape=(
            jax.ShapeDtypeStruct((ROWS, D), BF),
            jax.ShapeDtypeStruct((T * ROWS, HEAD), BF),
        ),
        in_specs=[hbm, pl.BlockSpec(memory_space=pltpu.SMEM)] + [hbm] * 7,
        out_specs=(anywhere, anywhere),
        scratch_shapes=[
            pltpu.VMEM((1, ROWS), I32),
            pltpu.VMEM((D // 128, 128), BF),
            pltpu.VMEM((1, D), F32),
            pltpu.VMEM((1, D), F32),
            pltpu.VMEM((ROWS, D), BF),
            pltpu.VMEM((T, 8, ROWS), I32),
            pltpu.VMEM((ROWS, ROWS), I32),
            pltpu.VMEM((DP, ROWS, KE), BF),
            pltpu.VMEM((NC, NX, ROWS, KE), BF),
            pltpu.VMEM((NY, KE, 2 * UNITS), BF),
            pltpu.VMEM((NY, UNITS, KE), BF),
            pltpu.VMEM((KE, T * HEAD), BF),
            pltpu.VMEM((ROUTED, CW), BF),
            pltpu.VMEM((ROUTED, CW), BF),
            pltpu.VMEM((QN * BAL, CW), F32),
            pltpu.VMEM((NZ, DP, BAL, KE), BF),
            pltpu.VMEM((DP, BAL, KE + 128), BF),
            pltpu.VMEM((DP, BAL, KE + 128), BF),
            pltpu.VMEM((2, NC, NX, BLK, NY * UNITS), BF),
            pltpu.VMEM((2, NX, BLK, NY * UNITS), BF),
            pltpu.VMEM((2, NX, BLK, NY * UNITS), BF),
            pltpu.VMEM((2, NX - 1, BLK, NY * UNITS), BF),
            pltpu.VMEM((2, NC, NX, BLK, NY * UNITS // 2), BF),
            pltpu.VMEM((2, NZ, LINE, KE // 2), BF),
            pltpu.VMEM((2, NZ - 1, LINE, KE // 2), BF),
            pltpu.VMEM((NZ, NC, NX, ROWS, ZC), BF),
            pltpu.VMEM((NZ, NX, ROWS, ZC), BF),
            pltpu.VMEM((NZ, NX, ROWS, ZC), BF),
            pltpu.VMEM((NZ, 2, ROWS // 2, ZC), BF),
            pltpu.VMEM((NZ, 2, ROWS, ZC), BF),
            pltpu.VMEM((NZ, NY, ROWS, HEAD), BF),
            pltpu.VMEM((T, ROWS, HEAD), BF),
            pltpu.VMEM((2, DP, BAL, KE // 2), BF),
            pltpu.VMEM((2, DP, BAL, KE // 2), BF),
            pltpu.VMEM((NC, NX, BAL, T * HEAD), BF),
            pltpu.VMEM((NX, BAL, T * HEAD), BF),
            pltpu.VMEM((NX, BAL, T * HEAD), BF),
            pltpu.VMEM((NX - 1, BAL, T * HEAD), BF),
            pltpu.VMEM((T, BAL, HEAD), BF),
            pltpu.VMEM((T, BAL, HEAD), BF),
            pltpu.VMEM((2, ROUTED, CW // 2), BF),
            pltpu.VMEM((2, ROUTED, CW // 2), BF),
            pltpu.VMEM((ROWS, D), BF),
            pltpu.VMEM((T * ROWS, HEAD), BF),
            pltpu.VMEM((T, ROWS, ROUTED), BF),
            pltpu.VMEM((QN, ROWS, ROUTED), BF),
            pltpu.VMEM((ROUTED, QN * BAL), BF),
            pltpu.SemaphoreType.DMA((9,)),
            pltpu.SemaphoreType.DMA((26,)),
            pltpu.SemaphoreType.DMA((26,)),
            pltpu.SemaphoreType.DMA((NZ,)),
            pltpu.SemaphoreType.DMA((NZ,)),
            pltpu.SemaphoreType.DMA((NZ,)),
            pltpu.SemaphoreType.DMA((NZ,)),
            pltpu.SemaphoreType.DMA((NZ,)),
            pltpu.SemaphoreType.DMA((NZ,)),
            pltpu.SemaphoreType.DMA((NZ,)),
            pltpu.SemaphoreType.DMA((NZ + 2 * QN * (CW // KE),)),
            pltpu.SemaphoreType.DMA((2,)),
            pltpu.SemaphoreType.DMA((2,)),
            pltpu.SemaphoreType.DMA((2,)),
            pltpu.SemaphoreType.DMA((2,)),
            pltpu.SemaphoreType.DMA((2,)),
            pltpu.SemaphoreType.DMA((2,)),
            pltpu.SemaphoreType.DMA((2,)),
            pltpu.SemaphoreType.DMA((2,)),
            pltpu.SemaphoreType.DMA((2,)),
            pltpu.SemaphoreType.DMA((2,)),
            pltpu.SemaphoreType.DMA((2,)),
            pltpu.SemaphoreType.DMA((2,)),
            pltpu.SemaphoreType.DMA((2,)),
            pltpu.SemaphoreType.DMA((2,)),
        ],
        compiler_params=pltpu.CompilerParams(
            collective_id=0, has_side_effects=True, vmem_limit_bytes=LIMIT * 1024 * 1024
        ),
    )(
        route_order, route_counts, w_router.reshape(D // 128, 128), gain_in.reshape(1, D), gain_next.reshape(1, D),
        tokens, w_gate_up, w_down, w_query,
    )
    return pl.pallas_call(
        hand_over,
        out_shape=(
            jax.ShapeDtypeStruct((ROWS, D), BF),
            jax.ShapeDtypeStruct((T * ROWS, HEAD), BF),
        ),
        in_specs=[anywhere] * 2,
        out_specs=(anywhere, anywhere),
        scratch_shapes=[
            pltpu.VMEM((ROWS, D), BF),
            pltpu.VMEM((T * ROWS, HEAD), BF),
            pltpu.SemaphoreType.DMA((2 * PARTS,)),
            pltpu.SemaphoreType.DMA((2 * PARTS,)),
        ],
    )(mixed, query)


def solution(mesh):
    in_specs = (
        P(("dp", "tensor"), None),
        P(("dp", "tensor"), None),
        P(("dp", "tensor")),
        P(),
        P(),
        P(None, "tensor"),
        P("tensor", None),
        P(),
        P(None, "tensor"),
    )
    out_specs = (P(("dp", "tensor"), None), P("dp", "tensor"))
    return jax.shard_map(
        on_device, mesh=mesh, in_specs=in_specs, out_specs=out_specs, check_vma=False
    )
```
